128 devices in a mesh: fsdp: 8 (over x_lo, z), ctx: 16 (over y, x_hi, core).
Axes of the slice: x: 4 (x_hi: 2, x_lo: 2; x = x_hi * 2 + x_lo), y: 4, z: 4, core: 2. Of those that a mesh axis runs over, the one named last changes fastest.
Arguments:
- query_in: bfloat16 [16384, 1024], P('ctx', 'fsdp'), may hold values from -6 to 6
- key_in: bfloat16 [16384, 1024], P('ctx', 'fsdp'), may hold values from -6 to 6
- value_in: bfloat16 [16384, 1024], P('ctx', 'fsdp'), may hold values from -6 to 6
- filt: bfloat16 [16384, 1024], P('ctx', 'fsdp'), may hold values from -1 to 1
- w_out: bfloat16 [1024, 8192], P(None, 'fsdp'), may hold values from -0.1875 to 0.1875
- d_out: bfloat16 [16384, 8192], P('ctx', 'fsdp'), may hold values from -6 to 6
Outputs:
- layer_out: bfloat16 [16384, 8192], P('ctx', 'fsdp')
- grad_query: bfloat16 [16384, 1024], P('ctx', 'fsdp')
- grad_key: bfloat16 [16384, 1024], P('ctx', 'fsdp')
- grad_value: bfloat16 [16384, 1024], P('ctx', 'fsdp')
- grad_weight: float32 [1024, 8192], P('ctx', 'fsdp')
The draws below stay inside these ranges and needn't reach their ends.
All inputs are finite; a program needn't handle non-finite values.
Results may differ from the reference program's by a relative error of at most 0.025.
Values may be sent and summed in bfloat16 or wider, within the bound.
No kernel may reach another device: no remote copies, remote signals or barrier semaphores. Data moves between devices by JAX's collectives and lax.ppermute only.
A program may use at most 128 MiB of HBM per device.

```python
import math
import jax
import jax.numpy as jnp
from jax import lax

D = 8192
FAC = 1024
CH = 1024
SEQ = 16384
NT = 32768
QF = 32


def draw_filt(key, part):
    key = jax.random.fold_in(key, 7)
    key_rate, key_noise = jax.random.split(key)
    low = math.log(32.0)
    high = math.log(4.0 * SEQ)
    spans = jnp.exp(jax.random.uniform(key_rate, (CH,), jnp.float32, low, high))
    noise = jnp.clip(jax.random.normal(key_noise, (SEQ, CH), jnp.float32), -4.0, 4.0)
    lags = jnp.arange(SEQ, dtype=jnp.float32)[:, None]
    amplitude = 1.0 / jnp.sqrt(jnp.minimum(spans, SEQ * 1.0))
    return (noise * amplitude[None, :] * jnp.exp(-lags / spans[None, :])).astype(jnp.bfloat16)


def block_scale(rng, extent, shards, least, high):
    level, own = 1.0, jax.random.fold_in(rng, 6)
    for dim, parts in shards:
        steps = jnp.exp(jax.random.uniform(jax.random.fold_in(own, dim), (parts,), jnp.float32, least / len(shards), high / len(shards)))
        level = level * jnp.repeat(steps, extent[dim] // parts).reshape([-1 if axis == dim else 1 for axis in range(len(extent))])
    return level


def bell_draw(own_key, dims, deviation, bound, pieces=(), kind=jnp.bfloat16):
    factor_of = block_scale(own_key, dims, pieces, -0.22, 0.18) if pieces else 1.0
    drawn = jax.random.normal(own_key, dims, jnp.float32) * deviation * factor_of
    return jnp.minimum(jnp.maximum(drawn, -bound), bound).astype(kind)


def setup_inputs(seed: int = 0) -> dict:
    key_list = jax.random.split(jax.random.key(seed), 7)
    return {
        "query_in": bell_draw(key_list[0], (SEQ, CH), 1.0, 6.0, ((0, 16), (1, 8))),
        "key_in": bell_draw(key_list[1], (SEQ, CH), 1.0, 6.0, ((0, 16), (1, 8))),
        "value_in": bell_draw(key_list[2], (SEQ, CH), 1.0, 6.0, ((0, 16), (1, 8))),
        "filt": draw_filt(jax.random.fold_in(key_list[6], 71), 0),
        "w_out": bell_draw(key_list[4], (CH, D), CH ** -0.5, 0.1875, ((1, 8),)),
        "d_out": bell_draw(key_list[5], (SEQ, D), 1.0, 6.0, ((0, 16), (1, 8))),
    }


HIGH = lax.Precision.HIGHEST

def angle_table(rows, cols, modulus):
    product = rows[:, None] * cols[None, :] % modulus
    return product.astype(jnp.float32) * (2.0 * math.pi / modulus)

def square_tables(order):
    index = jnp.arange(order, dtype=jnp.int32)
    angles = angle_table(index, index, order)
    return (jnp.cos(angles).astype(jnp.bfloat16), jnp.sin(angles).astype(jnp.bfloat16))

def first_table(length):
    angles = angle_table(jnp.arange(length, dtype=jnp.int32), jnp.arange(length // 2, dtype=jnp.int32), length)
    return jnp.concatenate([jnp.cos(angles), -jnp.sin(angles)], axis=0).astype(jnp.bfloat16)

def last_table(length):
    angles = angle_table(jnp.arange(length // 2, dtype=jnp.int32), jnp.arange(length, dtype=jnp.int32), length)
    return (jnp.concatenate([jnp.cos(angles), -jnp.sin(angles)], axis=1) / length).astype(jnp.bfloat16)

def apply_square(square, block):
    return jnp.einsum('kt,qtc->qkc', square.astype(jnp.float32), block.astype(jnp.float32), precision=HIGH)

def twiddles():
    angles = angle_table(jnp.arange(QF, dtype=jnp.int32), jnp.arange(FAC, dtype=jnp.int32), NT)
    return (jnp.cos(angles)[:, :, None], jnp.sin(angles)[:, :, None])

def to_spectrum(signal):
    width = signal.shape[1]
    cosine, sine = square_tables(FAC)
    first = first_table(QF)
    blocks = signal.reshape(QF // 2, FAC, width).astype(jnp.float32)
    section = jnp.einsum('kt,tjc->kjc', first.astype(jnp.float32), blocks, precision=HIGH)
    real_part, imag_part = (section[:QF], section[QF:])
    tw_cos, tw_sin = twiddles()
    turned_re = (real_part * tw_cos + imag_part * tw_sin).astype(jnp.bfloat16)
    turned_im = (imag_part * tw_cos - real_part * tw_sin).astype(jnp.bfloat16)
    spec_re = apply_square(cosine, turned_re) + apply_square(sine, turned_im)
    spec_im = apply_square(cosine, turned_im) - apply_square(sine, turned_re)
    return (spec_re.astype(jnp.bfloat16), spec_im.astype(jnp.bfloat16))

def to_signal(spec_re, spec_im):
    width = spec_re.shape[2]
    cosine, sine = square_tables(FAC)
    last = last_table(QF)
    back_re = (apply_square(cosine, spec_re) - apply_square(sine, spec_im)) / FAC
    back_im = (apply_square(cosine, spec_im) + apply_square(sine, spec_re)) / FAC
    tw_cos, tw_sin = twiddles()
    turned_re = (back_re * tw_cos - back_im * tw_sin).astype(jnp.bfloat16)
    turned_im = (back_im * tw_cos + back_re * tw_sin).astype(jnp.bfloat16)
    stacked = jnp.concatenate([turned_re, turned_im], axis=0).astype(jnp.float32)
    section = jnp.einsum('tk,kjc->tjc', last.astype(jnp.float32), stacked, precision=HIGH)
    return section.astype(jnp.bfloat16).reshape(SEQ, width)

def spectral_product(a_re, a_im, b_re, b_im):
    a_re, a_im = (a_re.astype(jnp.float32), a_im.astype(jnp.float32))
    b_re, b_im = (b_re.astype(jnp.float32), b_im.astype(jnp.float32))
    return ((a_re * b_re - a_im * b_im).astype(jnp.bfloat16), (a_re * b_im + a_im * b_re).astype(jnp.bfloat16))

def reference(query_in, key_in, value_in, filt, w_out, d_out):
    mixed = (key_in.astype(jnp.float32) * value_in.astype(jnp.float32)).astype(jnp.bfloat16)
    grad_y = jnp.dot(d_out, w_out.T, preferred_element_type=jnp.float32)
    grad_z = (grad_y * query_in.astype(jnp.float32)).astype(jnp.bfloat16)
    mix_re, mix_im = to_spectrum(mixed)
    fil_re, fil_im = to_spectrum(filt)
    grz_re, grz_im = to_spectrum(grad_z)
    conv_re, conv_im = spectral_product(mix_re, mix_im, fil_re, fil_im)
    adj_re, adj_im = spectral_product(fil_re, -fil_im, grz_re, grz_im)
    conv = to_signal(conv_re, conv_im)
    grad_u = to_signal(adj_re, adj_im)
    gated = (query_in.astype(jnp.float32) * conv.astype(jnp.float32)).astype(jnp.bfloat16)
    layer_out = jnp.dot(gated, w_out, preferred_element_type=jnp.float32).astype(jnp.bfloat16)
    scale = 1.0 / math.sqrt(SEQ)
    grad_weight = jnp.dot(gated.T, d_out, preferred_element_type=jnp.float32) * scale
    grad_query = (grad_y * conv.astype(jnp.float32)).astype(jnp.bfloat16)
    grad_key = (grad_u.astype(jnp.float32) * value_in.astype(jnp.float32)).astype(jnp.bfloat16)
    grad_value = (grad_u.astype(jnp.float32) * key_in.astype(jnp.float32)).astype(jnp.bfloat16)
    return (layer_out, grad_query, grad_key, grad_value, grad_weight)
```

```python
import functools
import math

import jax
import jax.numpy as jnp
import numpy as np
from jax import lax
from jax.experimental import pallas as pl
from jax.experimental.pallas import tpu as pltpu
from jax.sharding import PartitionSpec as P

FAC = 1024
QF = 32
HALF = QF // 2 + 1
BF = jnp.bfloat16
F32 = jnp.float32
MIB = 1 << 20


def angles(rows, cols, modulus):
    product = (rows[:, None].astype(np.int64) * cols[None, :]) % modulus
    return (product.astype(np.float32) * np.float32(2.0 * math.pi / modulus)).astype(np.float64)


def host_tables(ways, group, sigs):
    k2, t2, t1 = np.arange(HALF), np.arange(ways), np.arange(FAC)
    eye = np.eye(group)
    a = angles(k2, t2, QF)
    steps = np.stack([np.cos(a), -np.sin(a)])
    first = np.einsum("rkt,sp,cd->srkctpd", steps, np.eye(sigs), eye)
    first = first.reshape(sigs * 2 * HALF * group, ways * sigs * group)
    weight = np.where((k2 == 0) | (k2 == QF // 2), 1.0, 2.0)
    b = angles(t2, k2, QF)
    back = np.stack([np.cos(b), -np.sin(b)], axis=1) * weight / (QF * FAC)
    last = np.einsum("trk,cd->tcrkd", back, eye).reshape(ways * group, 2 * HALF * group)
    s = angles(t1, t1, FAC)
    square = np.concatenate([np.cos(s), np.sin(s)])
    w = angles(k2, t1, QF * FAC)
    tc, ts = (np.repeat(f(w), group, axis=0).astype(np.float32) for f in (np.cos, np.sin))
    as_bf = lambda v: np.asarray(v, np.float32).astype(BF)
    return as_bf(first), as_bf(last), as_bf(square), tc, ts


def params(mib):
    return pltpu.CompilerParams(vmem_limit_bytes=mib * MIB)


VMEM = pl.BlockSpec(memory_space=pltpu.VMEM)
SMEM = pl.BlockSpec(memory_space=pltpu.SMEM)


def prep_kernel(k_ref, v_ref, f_ref, q_ref, send_ref, qt_ref):
    ways = send_ref.shape[0]
    mixed = k_ref[...].astype(F32) * v_ref[...].astype(F32)
    mixed_t = mixed.T.reshape(ways, 1, -1, FAC)
    filt_t = f_ref[...].astype(F32).T.reshape(ways, 1, -1, FAC)
    both = jnp.concatenate([mixed_t, filt_t], axis=1)
    send_ref[...] = both.reshape(send_ref.shape).astype(BF)
    qt_ref[...] = q_ref[...].astype(F32).T.astype(BF)


def turn(section, tc, ts):
    n = section.shape[0] // 2
    re, im = section[:n], section[n:]
    b_re, b_im = re * tc + im * ts, im * tc - re * ts
    return (
        jnp.concatenate([b_re, b_im], axis=0).astype(BF),
        jnp.concatenate([b_im, -b_re], axis=0).astype(BF),
    )


def cols_of(j, width):
    return pl.ds(pl.multiple_of(j * width, width), width)


def inverse(y_ref, square_ref, last_ref, tc_ref, ts_ref, out_ref, width):
    n = y_ref.shape[0] // 2

    def back(j, carry):
        cols = cols_of(j, width)
        c = jnp.dot(y_ref[...], square_ref[:, cols], preferred_element_type=F32)
        re, im = c[:n], c[n:]
        tc, ts = tc_ref[:, cols], ts_ref[:, cols]
        e = jnp.concatenate([re * tc - im * ts, im * tc + re * ts], axis=0).astype(BF)
        out_ref[:, cols] = jnp.dot(last_ref[...], e, preferred_element_type=F32).astype(BF)
        return carry

    lax.fori_loop(0, FAC // width, back, 0)


def put_spectrum(y_ref, cols, lower, re, im):
    y_ref[:, cols] = jnp.concatenate([re, im], axis=0).astype(BF)
    y_ref[:, lower] = jnp.concatenate([-im, re], axis=0).astype(BF)


def conv_kernel(width, r_ref, first_ref, last_ref, square_ref, tc_ref, ts_ref, z_ref, h_ref, x_ref, y_ref):
    n = tc_ref.shape[0]
    tc, ts = tc_ref[...], ts_ref[...]
    for s in range(2):
        rows = pl.ds(2 * n * s, 2 * n)
        section = jnp.dot(first_ref[rows, :], r_ref[...], preferred_element_type=F32)
        left, right = turn(section, tc, ts)
        x_ref[rows, pl.ds(0, FAC)] = left
        x_ref[rows, pl.ds(FAC, FAC)] = right

    def forth(j, carry):
        cols = cols_of(j, width)
        lower = pl.ds(pl.multiple_of(FAC + j * width, width), width)
        f = jnp.dot(x_ref[...], square_ref[:, cols], preferred_element_type=F32)
        u_re, u_im, h_re, h_im = f[:n], f[n : 2 * n], f[2 * n : 3 * n], f[3 * n :]
        h_ref[:, cols] = f[2 * n :].astype(BF)
        put_spectrum(y_ref, cols, lower, u_re * h_re - u_im * h_im, u_re * h_im + u_im * h_re)
        return carry

    lax.fori_loop(0, FAC // width, forth, 0)
    inverse(y_ref, square_ref, last_ref, tc_ref, ts_ref, z_ref, width)


def adjoint_kernel(width, r_ref, h_ref, first_ref, last_ref, square_ref, tc_ref, ts_ref, du_ref, x_ref, y_ref):
    n = tc_ref.shape[0]
    section = jnp.dot(first_ref[...], r_ref[...], preferred_element_type=F32)
    left, right = turn(section, tc_ref[...], ts_ref[...])
    x_ref[:, pl.ds(0, FAC)] = left
    x_ref[:, pl.ds(FAC, FAC)] = right

    def forth(j, carry):
        cols = cols_of(j, width)
        lower = pl.ds(pl.multiple_of(FAC + j * width, width), width)
        g = jnp.dot(x_ref[...], square_ref[:, cols], preferred_element_type=F32)
        g_re, g_im = g[:n], g[n:]
        h = h_ref[:, cols].astype(F32)
        h_re, h_im = h[:n], h[n:]
        put_spectrum(y_ref, cols, lower, h_re * g_re + h_im * g_im, h_re * g_im - h_im * g_re)
        return carry

    lax.fori_loop(0, FAC // width, forth, 0)
    inverse(y_ref, square_ref, last_ref, tc_ref, ts_ref, du_ref, width)


def weight_kernel(scale, at_ref, *refs):
    blocks, (d_ref, all_ref, away_ref, keep_ref, left_ref) = refs[:8], refs[8:]
    rows = blocks[0].shape[0]
    for i, block in enumerate(blocks):
        all_ref[pl.ds(pl.multiple_of(at_ref[i] * rows, rows), rows), :] = block[...]
    core = at_ref[8]
    half = rows // 2
    for out_ref, mine in ((away_ref, 1 - core), (keep_ref, core)):
        for g in range(8):
            start = pl.multiple_of(g * rows + mine * half, half)
            left_ref[pl.ds(g * half, half), :] = all_ref[pl.ds(start, half), :]

        def step(j, carry, out_ref=out_ref):
            cols = cols_of(j, 256)
            p = jnp.dot(left_ref[...], d_ref[:, cols], preferred_element_type=F32)
            out_ref[:, cols] = (p * scale).astype(BF)
            return carry

        lax.fori_loop(0, d_ref.shape[1] // 256, step, 0)


def finish_kernel(dy_ref, z_ref, du_ref, k_ref, v_ref, gq_ref, gk_ref, gv_ref):
    gq = dy_ref[...].astype(F32) * z_ref[...].astype(F32)
    gq_ref[...] = gq.T.astype(BF)
    du = du_ref[...].astype(F32).T
    gk_ref[...] = (du * v_ref[...].astype(F32)).astype(BF)
    gv_ref[...] = (du * k_ref[...].astype(F32)).astype(BF)


def call(kernel, outs, ins, scratch=(), mib=40, specs=None, flops=0):
    total = sum(math.prod(o.shape) * o.dtype.itemsize for o in (*outs, *ins))
    return pl.pallas_call(
        kernel,
        out_shape=outs,
        in_specs=specs or [VMEM] * len(ins),
        out_specs=[VMEM] * len(outs),
        scratch_shapes=scratch,
        compiler_params=params(mib),
        cost_estimate=pl.CostEstimate(flops=flops, bytes_accessed=total, transcendentals=0),
    )(*ins)


def shape(*dims, dtype=BF):
    return jax.ShapeDtypeStruct(dims, dtype)


def spread(values):
    return lax.all_to_all(values, "ctx", 0, 0, tiled=True)


def ring(gated):
    pair = [(i, i ^ 4) for i in range(8)]
    up = [(i, (i & 4) | ((i + 1) & 3)) for i in range(8)]
    down = [(i, (i & 4) | ((i - 1) & 3)) for i in range(8)]
    move = lambda v, p: lax.ppermute(v, "fsdp", p)
    other = move(gated, pair)
    own_up, own_down = move(gated, up), move(gated, down)
    other_up, other_down = move(other, up), move(other, down)
    own_far, other_far = move(own_up, up), move(other_down, down)
    me = lax.axis_index("fsdp")
    at = lambda flip, step: (me ^ 4 if flip else me) & 4 | ((me + step) & 3)
    blocks = (gated, other, own_up, own_down, other_up, other_down, own_far, other_far)
    places = (at(0, 0), at(1, 0), at(0, -1), at(0, 1), at(1, -1), at(1, 1), at(0, 2), at(1, 2))
    return blocks, places


def on_device(query_in, key_in, value_in, filt, w_out, d_out):
    seq_rows, width = query_in.shape
    ways = lax.axis_size("ctx")
    group = width // ways
    n = HALF * group
    first2, last, square, tc, ts = map(jnp.asarray, host_tables(ways, group, 2))
    first1 = jnp.asarray(host_tables(ways, group, 1)[0])

    send, query_t = call(
        prep_kernel,
        [shape(ways, 2 * group, seq_rows), shape(width, seq_rows)],
        [key_in, value_in, filt, query_in],
    )
    arrived = spread(send.reshape(ways * 2 * group, seq_rows))
    partial_y = lax.dot_general(w_out, d_out, (((1,), (1,)), ((), ())), preferred_element_type=F32)
    grad_y = lax.psum_scatter(partial_y.astype(BF), "fsdp", scatter_dimension=0, tiled=True)

    product = 2 * 2 * n * 2 * FAC * FAC
    conv, spectrum = call(
        functools.partial(conv_kernel, 256),
        [shape(ways * group, FAC), shape(2 * n, FAC)],
        [arrived, first2, last, square, tc, ts],
        [pltpu.VMEM((4 * n, 2 * FAC), BF), pltpu.VMEM((2 * n, 2 * FAC), BF)],
        flops=3 * product,
    )
    z = spread(conv)
    gated = (query_t.astype(F32) * z.astype(F32)).astype(BF)

    blocks, places = ring(gated)
    core = lax.axis_index("ctx") & 1
    at = jnp.stack([*places, core]).astype(jnp.int32)
    scale = 1.0 / math.sqrt(seq_rows * ways)
    channels, columns = w_out.shape
    gated_all, away, keep = call(
        functools.partial(weight_kernel, scale),
        [shape(channels, seq_rows), shape(channels // 2, columns), shape(channels // 2, columns)],
        [at, *blocks, d_out],
        [pltpu.VMEM((channels // 2, seq_rows), BF)],
        specs=[SMEM] + [VMEM] * 9,
        flops=2 * channels * seq_rows * columns,
    )
    swapped = lax.ppermute(away, "ctx", [(i, i ^ 1) for i in range(ways)])
    summed = (keep.astype(F32) + swapped.astype(F32)).astype(BF)
    groups = [list(range(c, ways, 2)) for c in range(2)]
    parts = lax.all_to_all(summed, "ctx", 0, 0, tiled=True, axis_index_groups=groups)
    grad_weight = jnp.sum(parts.reshape(ways // 2, channels // ways, columns).astype(F32), axis=0)
    layer_out = lax.dot_general(
        gated_all, w_out, (((0,), (0,)), ((), ())), preferred_element_type=F32
    ).astype(BF)

    grad_z = (grad_y.astype(F32) * query_t.astype(F32)).astype(BF)
    (adjoint,) = call(
        functools.partial(adjoint_kernel, 256),
        [shape(ways * group, FAC)],
        [spread(grad_z), spectrum, first1, last, square, tc, ts],
        [pltpu.VMEM((2 * n, 2 * FAC), BF), pltpu.VMEM((2 * n, 2 * FAC), BF)],
        flops=2 * product,
    )
    grad_u = spread(adjoint)
    like = shape(seq_rows, width)
    grad_query, grad_key, grad_value = call(
        finish_kernel, [like, like, like], [grad_y, z, grad_u, key_in, value_in]
    )
    return (layer_out, grad_query, grad_key, grad_value, grad_weight)


def solution(mesh):
    both = P("ctx", "fsdp")
    return jax.shard_map(
        on_device,
        mesh=mesh,
        in_specs=(both, both, both, both, P(None, "fsdp"), both),
        out_specs=(both, both, both, both, both),
        check_vma=False,
    )
```

```python
import functools
import math

import jax
import jax.numpy as jnp
import numpy as np
from jax import lax
from jax.experimental import pallas as pl
from jax.experimental.pallas import tpu as pltpu
from jax.sharding import PartitionSpec as P

FAC = 1024
QF = 32
HALF = QF // 2 + 1
BF = jnp.bfloat16
F32 = jnp.float32
MIB = 1 << 20


def angles(rows, cols, modulus):
    product = (rows[:, None].astype(np.int64) * cols[None, :]) % modulus
    return (product.astype(np.float32) * np.float32(2.0 * math.pi / modulus)).astype(np.float64)


def channel_order(ways, group):
    half = group // 2
    ctx, h, r = np.meshgrid(np.arange(ways), np.arange(2), np.arange(half), indexing="ij")
    return (h * ways * half + ctx * half + r).reshape(-1)


def host_tables(ways, group, sigs):
    k2, t2, t1 = np.arange(HALF), np.arange(ways), np.arange(FAC)
    eye = np.eye(group)
    a = angles(k2, t2, QF)
    steps = np.stack([np.cos(a), -np.sin(a)])
    first = np.einsum("rkt,sp,cd->srkctpd", steps, np.eye(sigs), eye)
    first = first.reshape(sigs * 2 * HALF * group, ways * sigs * group)
    weight = np.where((k2 == 0) | (k2 == QF // 2), 1.0, 2.0)
    b = angles(t2, k2, QF)
    back = np.stack([np.cos(b), -np.sin(b)], axis=1) * weight / (QF * FAC)
    last = np.einsum("trk,cd->tcrkd", back, eye).reshape(ways * group, 2 * HALF * group)
    s = angles(t1, t1, FAC)
    square = np.concatenate([np.cos(s), np.sin(s)])
    w = angles(k2, t1, QF * FAC)
    tc, ts = (np.repeat(f(w), group, axis=0).astype(np.float32) for f in (np.cos, np.sin))
    as_bf = lambda v: np.asarray(v, np.float32).astype(BF)
    return as_bf(first), as_bf(last), as_bf(square), tc, ts


def params(mib):
    return pltpu.CompilerParams(vmem_limit_bytes=mib * MIB)


VMEM = pl.BlockSpec(memory_space=pltpu.VMEM)
SMEM = pl.BlockSpec(memory_space=pltpu.SMEM)


def product_t(order, values):
    return lax.dot_general(order, values, (((1,), (1,)), ((), ())), preferred_element_type=F32)


def dy_kernel(w_ref, d_ref, out_ref):
    out_ref[...] = product_t(w_ref[...], d_ref[...]).astype(BF)


def prep_kernel(k_ref, v_ref, f_ref, order_ref, send_ref):
    ways = send_ref.shape[0]
    mixed = (k_ref[...].astype(F32) * v_ref[...].astype(F32)).astype(BF)
    parts = [product_t(order_ref[...], x).reshape(ways, 1, -1, FAC) for x in (mixed, f_ref[...])]
    send_ref[...] = jnp.concatenate(parts, axis=1).reshape(send_ref.shape).astype(BF)


def turn_query_kernel(core_ref, q_ref, qt_ref, mine_ref, away_ref):
    qt_ref[...] = q_ref[...].astype(F32).T.astype(BF)
    rows = mine_ref.shape[0]
    for out_ref, half in ((mine_ref, core_ref[0]), (away_ref, 1 - core_ref[0])):
        out_ref[...] = qt_ref[pl.ds(pl.multiple_of(half * rows, rows), rows), :]


def gate_kernel(core_ref, z_ref, order_ref, q_mine_ref, q_theirs_ref, gated_ref, z_mine_ref, z_away_ref):
    z = jnp.dot(order_ref[core_ref[0]], z_ref[...], preferred_element_type=F32)
    n = z.shape[0] // 2
    z_mine_ref[...] = z[:n].astype(BF)
    z_away_ref[...] = z[n:].astype(BF)
    gated_ref[pl.ds(0, n), :] = (z[:n] * q_mine_ref[...].astype(F32)).astype(BF)
    gated_ref[pl.ds(n, n), :] = (z[n:] * q_theirs_ref[...].astype(F32)).astype(BF)


def dz_kernel(dy_ref, qt_ref, order_ref, send_ref):
    dz = (dy_ref[...].astype(F32) * qt_ref[...].astype(F32)).astype(BF)
    send_ref[...] = jnp.dot(order_ref[...], dz, preferred_element_type=F32).astype(BF)


def turn(section, tc, ts):
    n = section.shape[0] // 2
    re, im = section[:n], section[n:]
    b_re, b_im = re * tc + im * ts, im * tc - re * ts
    return (
        jnp.concatenate([b_re, b_im], axis=0).astype(BF),
        jnp.concatenate([b_im, -b_re], axis=0).astype(BF),
    )


def cols_of(j, width):
    return pl.ds(pl.multiple_of(j * width, width), width)


def inverse(y_ref, square_ref, last_ref, tc_ref, ts_ref, out_ref, width):
    n = y_ref.shape[0] // 2

    def back(j, carry):
        cols = cols_of(j, width)
        c = jnp.dot(y_ref[...], square_ref[:, cols], preferred_element_type=F32)
        re, im = c[:n], c[n:]
        tc, ts = tc_ref[:, cols], ts_ref[:, cols]
        e = jnp.concatenate([re * tc - im * ts, im * tc + re * ts], axis=0).astype(BF)
        out_ref[:, cols] = jnp.dot(last_ref[...], e, preferred_element_type=F32).astype(BF)
        return carry

    lax.fori_loop(0, FAC // width, back, 0)


def put_spectrum(y_ref, cols, lower, re, im):
    y_ref[:, cols] = jnp.concatenate([re, im], axis=0).astype(BF)
    y_ref[:, lower] = jnp.concatenate([-im, re], axis=0).astype(BF)


def conv_kernel(width, r_ref, first_ref, last_ref, square_ref, tc_ref, ts_ref, z_ref, h_ref, x_ref, y_ref):
    n = tc_ref.shape[0]
    tc, ts = tc_ref[...], ts_ref[...]
    for s in range(2):
        rows = pl.ds(2 * n * s, 2 * n)
        section = jnp.dot(first_ref[rows, :], r_ref[...], preferred_element_type=F32)
        left, right = turn(section, tc, ts)
        x_ref[rows, pl.ds(0, FAC)] = left
        x_ref[rows, pl.ds(FAC, FAC)] = right

    def forth(j, carry):
        cols = cols_of(j, width)
        lower = pl.ds(pl.multiple_of(FAC + j * width, width), width)
        f = jnp.dot(x_ref[...], square_ref[:, cols], preferred_element_type=F32)
        u_re, u_im, h_re, h_im = f[:n], f[n : 2 * n], f[2 * n : 3 * n], f[3 * n :]
        h_ref[:, cols] = f[2 * n :].astype(BF)
        put_spectrum(y_ref, cols, lower, u_re * h_re - u_im * h_im, u_re * h_im + u_im * h_re)
        return carry

    lax.fori_loop(0, FAC // width, forth, 0)
    inverse(y_ref, square_ref, last_ref, tc_ref, ts_ref, z_ref, width)


def adjoint_kernel(width, r_ref, h_ref, first_ref, last_ref, square_ref, tc_ref, ts_ref, du_ref, x_ref, y_ref):
    n = tc_ref.shape[0]
    section = jnp.dot(first_ref[...], r_ref[...], preferred_element_type=F32)
    left, right = turn(section, tc_ref[...], ts_ref[...])
    x_ref[:, pl.ds(0, FAC)] = left
    x_ref[:, pl.ds(FAC, FAC)] = right

    def forth(j, carry):
        cols = cols_of(j, width)
        lower = pl.ds(pl.multiple_of(FAC + j * width, width), width)
        g = jnp.dot(x_ref[...], square_ref[:, cols], preferred_element_type=F32)
        g_re, g_im = g[:n], g[n:]
        h = h_ref[:, cols].astype(F32)
        h_re, h_im = h[:n], h[n:]
        put_spectrum(y_ref, cols, lower, h_re * g_re + h_im * g_im, h_re * g_im - h_im * g_re)
        return carry

    lax.fori_loop(0, FAC // width, forth, 0)
    inverse(y_ref, square_ref, last_ref, tc_ref, ts_ref, du_ref, width)


def weight_kernel(scale, width, at_ref, *refs):
    blocks, (d_ref, d_other_ref, part_ref, mine_ref, away_ref) = refs[:8], refs[8:]
    n = blocks[0].shape[0] // 2
    for i, block in enumerate(blocks):
        rows = pl.ds(pl.multiple_of(at_ref[i] * n, n), n)
        mine_ref[rows, :] = block[pl.ds(0, n), :]
        away_ref[rows, :] = block[pl.ds(n, n), :]

    def step(j, carry):
        cols = cols_of(j, width)
        p = jnp.dot(mine_ref[...], d_ref[:, cols], preferred_element_type=F32)
        p += jnp.dot(away_ref[...], d_other_ref[:, cols], preferred_element_type=F32)
        part_ref[:, cols] = (p * scale).astype(BF)
        return carry

    lax.fori_loop(0, d_ref.shape[1] // width, step, 0)


def finish_kernel(core_ref, dy_ref, z_mine_ref, z_theirs_ref, du_ref, order_ref, k_ref, v_ref, gq_ref, gk_ref, gv_ref, gq_t_ref):
    n = z_mine_ref.shape[0]
    for z_ref, half in ((z_mine_ref, core_ref[0]), (z_theirs_ref, 1 - core_ref[0])):
        rows = pl.ds(pl.multiple_of(half * n, n), n)
        gq_t_ref[rows, :] = dy_ref[rows, :].astype(F32) * z_ref[...].astype(F32)
    gq_ref[...] = gq_t_ref[...].T.astype(BF)
    du = jnp.dot(du_ref[...].astype(F32).T.astype(BF), order_ref[...], preferred_element_type=F32)
    gk_ref[...] = (du * v_ref[...].astype(F32)).astype(BF)
    gv_ref[...] = (du * k_ref[...].astype(F32)).astype(BF)


def call(kernel, outs, ins, scratch=(), mib=16, flops=0, scalars=0):
    total = sum(math.prod(o.shape) * o.dtype.itemsize for o in (*outs, *ins))
    return pl.pallas_call(
        kernel,
        out_shape=outs,
        in_specs=[SMEM] * scalars + [VMEM] * (len(ins) - scalars),
        out_specs=[VMEM] * len(outs),
        scratch_shapes=scratch,
        compiler_params=params(mib),
        cost_estimate=pl.CostEstimate(flops=flops, bytes_accessed=total, transcendentals=0),
    )(*ins)


def shape(*dims, dtype=BF):
    return jax.ShapeDtypeStruct(dims, dtype)


def spread(values):
    return lax.all_to_all(values, "ctx", 0, 0, tiled=True)


def ring(gated):
    pair = [(i, i ^ 4) for i in range(8)]
    up = [(i, (i & 4) | ((i + 1) & 3)) for i in range(8)]
    down = [(i, (i & 4) | ((i - 1) & 3)) for i in range(8)]
    move = lambda v, p: lax.ppermute(v, "fsdp", p)
    other = move(gated, pair)
    own_up, own_down = move(gated, up), move(gated, down)
    other_up, other_down = move(other, up), move(other, down)
    own_far, other_far = move(own_up, up), move(other_down, down)
    me = lax.axis_index("fsdp")
    at = lambda flip, step: (me ^ 4 if flip else me) & 4 | ((me + step) & 3)
    blocks = (gated, other, own_up, own_down, other_up, other_down, own_far, other_far)
    places = (at(0, 0), at(1, 0), at(0, -1), at(0, 1), at(1, -1), at(1, 1), at(0, 2), at(1, 2))
    return blocks, places


def dy_product(w_out, d_out, tile=256):
    channels, depth = w_out.shape
    rows = d_out.shape[0]
    return pl.pallas_call(
        dy_kernel,
        out_shape=shape(channels, rows),
        grid=(rows // tile,),
        in_specs=[
            pl.BlockSpec((channels, depth), lambda i: (0, 0)),
            pl.BlockSpec((tile, depth), lambda i: (i, 0)),
        ],
        out_specs=pl.BlockSpec((channels, tile), lambda i: (0, i)),
        compiler_params=params(20),
        cost_estimate=pl.CostEstimate(
            flops=2 * channels * depth * rows, bytes_accessed=6 * channels * rows, transcendentals=0
        ),
    )(w_out, d_out)


def on_device(query_in, key_in, value_in, filt, w_out, d_out):
    seq_rows, width = query_in.shape
    channels, columns = w_out.shape
    ways = lax.axis_size("ctx")
    group, half = width // ways, width // 2
    n = HALF * group
    first2, last, square, tc, ts = host_tables(ways, group, 2)
    first1 = host_tables(ways, group, 1)[0]
    pick = np.arange(ways * group).reshape(ways // 2, 2, 2, group // 2).transpose(0, 2, 1, 3).reshape(-1)
    last_z = last[pick]
    order = channel_order(ways, group)
    order_in = np.eye(width)[order].astype(BF)
    slots = np.arange(width).reshape(ways, 2, group // 2).transpose(1, 0, 2)
    order_z = np.stack([np.eye(width)[slots[list(s)].reshape(-1)] for s in ((0, 1), (1, 0))]).astype(BF)

    ctx = lax.axis_index("ctx")
    core = (ctx & 1).astype(jnp.int32)
    core_at = core.reshape(1)
    swap = lambda v: lax.ppermute(v, "ctx", [(i, i ^ 1) for i in range(ways)])

    partial_y = dy_product(w_out, d_out)
    grad_y = lax.psum_scatter(partial_y, "fsdp", scatter_dimension=0, tiled=True)
    (send,) = call(prep_kernel, [shape(ways, 2 * group, seq_rows)], [key_in, value_in, filt, order_in])
    arrived = spread(send.reshape(ways * 2 * group, seq_rows))
    d_other = swap(d_out)
    query_t, q_mine, q_away = call(
        turn_query_kernel,
        [shape(width, seq_rows), shape(half, seq_rows), shape(half, seq_rows)],
        [core_at, query_in],
        scalars=1,
    )
    q_theirs = swap(q_away)

    product = 2 * 2 * n * 2 * FAC * FAC
    conv, spectrum = call(
        functools.partial(conv_kernel, 256),
        [shape(ways * group, FAC), shape(2 * n, FAC)],
        [arrived, first2, last_z, square, tc, ts],
        [pltpu.VMEM((4 * n, 2 * FAC), BF), pltpu.VMEM((2 * n, 2 * FAC), BF)],
        mib=24,
        flops=3 * product,
    )
    gated, z_mine, z_away = call(
        gate_kernel,
        [shape(width, seq_rows), shape(half, seq_rows), shape(half, seq_rows)],
        [core_at, spread(conv), order_z, q_mine, q_theirs],
        scalars=1,
    )
    z_theirs = swap(z_away)

    blocks, places = ring(gated)
    at = jnp.stack(places).astype(jnp.int32)
    scale = 1.0 / math.sqrt(seq_rows * ways)
    part, mine, away = call(
        functools.partial(weight_kernel, scale, 256),
        [shape(channels // 2, columns), shape(channels // 2, seq_rows), shape(channels // 2, seq_rows)],
        [at, *blocks, d_out, d_other],
        scalars=1,
        mib=20,
        flops=2 * channels * seq_rows * columns,
    )
    groups = [list(range(c, ways, 2)) for c in range(2)]
    parts = lax.all_to_all(part, "ctx", 0, 0, tiled=True, axis_index_groups=groups)
    grad_weight = jnp.sum(parts.reshape(ways // 2, channels // ways, columns).astype(F32), axis=0)

    theirs = swap(away)
    split = lambda v: v.reshape(-1, 1, half, seq_rows)
    low, high = jnp.where(core == 0, mine, theirs), jnp.where(core == 0, theirs, mine)
    gated_all = jnp.concatenate([split(low), split(high)], axis=1).reshape(channels, seq_rows)
    layer_out = lax.dot_general(
        gated_all, w_out, (((0,), (0,)), ((), ())), preferred_element_type=F32
    ).astype(BF)

    (grad_z,) = call(dz_kernel, [shape(width, seq_rows)], [grad_y, query_t, order_in])
    (adjoint,) = call(
        functools.partial(adjoint_kernel, 256),
        [shape(ways * group, FAC)],
        [spread(grad_z), spectrum, first1, last, square, tc, ts],
        [pltpu.VMEM((2 * n, 2 * FAC), BF), pltpu.VMEM((2 * n, 2 * FAC), BF)],
        mib=20,
        flops=2 * product,
    )
    like = shape(seq_rows, width)
    grad_query, grad_key, grad_value = call(
        finish_kernel,
        [like, like, like],
        [core_at, grad_y, z_mine, z_theirs, spread(adjoint), order_in, key_in, value_in],
        [pltpu.VMEM((width, seq_rows), F32)],
        scalars=1,
    )
    return (layer_out, grad_query, grad_key, grad_value, grad_weight)


def solution(mesh):
    both = P("ctx", "fsdp")
    return jax.shard_map(
        on_device,
        mesh=mesh,
        in_specs=(both, both, both, both, P(None, "fsdp"), both),
        out_specs=(both, both, both, both, both),
        check_vma=False,
    )
```

```python
import functools
import math

import jax
import jax.numpy as jnp
import numpy as np
from jax import lax
from jax.experimental import pallas as pl
from jax.experimental.pallas import tpu as pltpu
from jax.sharding import PartitionSpec as P

ROW = 1024
FAC = 256
QF = 128
HALF = QF // 2 + 1
LANE_TILES = ROW // FAC
BF = jnp.bfloat16
F32 = jnp.float32
MIB = 1 << 20


def angles(rows, cols, modulus):
    product = (rows[:, None].astype(np.int64) * cols[None, :]) % modulus
    return (product.astype(np.float32) * np.float32(2.0 * math.pi / modulus)).astype(np.float64)


def channel_order(ways, group):
    half = group // 2
    ctx, h, r = np.meshgrid(np.arange(ways), np.arange(2), np.arange(half), indexing="ij")
    return (h * ways * half + ctx * half + r).reshape(-1)


def host_tables(ways, group):
    k2, t1 = np.arange(HALF), np.arange(FAC)
    t2 = (np.arange(LANE_TILES)[:, None] + LANE_TILES * np.arange(ways)[None, :]).reshape(-1)
    eye = np.eye(group)
    a = angles(k2, t2, QF)
    steps = np.stack([np.cos(a), -np.sin(a)])
    first = np.einsum("rkt,cd->rkctd", steps, eye).reshape(2 * HALF * group, t2.size * group)
    weight = np.where((k2 == 0) | (k2 == QF // 2), 1.0, 2.0) / (QF * FAC)
    b = angles(t2, k2, QF)
    back = np.concatenate([np.cos(b) * weight, (-np.sin(b) * weight)[:, 1:-1]], axis=1)
    last = np.einsum("tk,cd->tckd", back, eye).reshape(t2.size * group, -1)
    s = angles(t1, t1, FAC)
    square = np.concatenate([np.cos(s), np.sin(s)])
    w = angles(k2, t1, QF * FAC)
    tc, ts = (np.repeat(f(w), group, axis=0).astype(np.float32) for f in (np.cos, np.sin))
    as_bf = lambda v: np.asarray(v, np.float32).astype(BF)
    return as_bf(first), as_bf(last), as_bf(square), tc, ts


def params(mib):
    return pltpu.CompilerParams(vmem_limit_bytes=mib * MIB)


VMEM = pl.BlockSpec(memory_space=pltpu.VMEM)
ANY = pl.BlockSpec(memory_space=pl.ANY)
MOVES = ((0, 1), (0, -1), (1, 0), (0, 2), (1, 1), (1, -1), (1, 2))


def place(index, move):
    flip, step = move
    return ((index ^ 4) if flip else index) & 4 | ((index + step) & 3)


def dot(a, b):
    return jnp.dot(a, b, preferred_element_type=F32)


def my_core():
    return lax.axis_index("ctx") & 1


def rows_at(i, n):
    return pl.ds(pl.multiple_of(i * n, n), n)


def product_t(order, values):
    return lax.dot_general(order, values, (((1,), (1,)), ((), ())), preferred_element_type=F32)


def dy_kernel(step, w_hbm, d_hbm, *refs):
    outs, (w_ref, d_ref, w_sem, d_sem) = refs[:-4], refs[-4:]
    me = lax.axis_index("fsdp")
    n = outs[0].shape[0]
    copies = [
        pltpu.make_async_copy(w_hbm.at[rows_at(place(me, move), n), :], w_ref.at[pl.ds(i * n, n), :], w_sem.at[i])
        for i, move in enumerate(((0, 0), *MOVES))
    ]
    pieces = range(d_ref.shape[0] // step)
    parts = [
        pltpu.make_async_copy(d_hbm.at[pl.ds(i * step, step), :], d_ref.at[pl.ds(i * step, step), :], d_sem.at[i])
        for i in pieces
    ]
    for copy in (*copies, *parts):
        copy.start()
    for copy in copies:
        copy.wait()
    for i in pieces:
        parts[i].wait()
        rows = pl.ds(i * step, step)
        p = product_t(w_ref[...], d_ref[rows, :]).astype(BF)
        for j, out_ref in enumerate(outs):
            out_ref[:, rows] = p[j * n : (j + 1) * n]


def prep_kernel(k_ref, v_ref, f_ref, order_ref, send_ref):
    ways = send_ref.shape[0]
    mixed = (k_ref[...].astype(F32) * v_ref[...].astype(F32)).astype(BF)
    parts = [product_t(order_ref[...], x).reshape(ways, 1, -1, ROW) for x in (mixed, f_ref[...])]
    send_ref[...] = jnp.concatenate(parts, axis=1).reshape(send_ref.shape).astype(BF)


def turn_query_kernel(q_ref, qt_ref, mine_ref, away_ref):
    qt_ref[...] = q_ref[...].astype(F32).T.astype(BF)
    core, n = my_core(), mine_ref.shape[0]
    mine_ref[...] = qt_ref[rows_at(core, n), :]
    away_ref[...] = qt_ref[rows_at(1 - core, n), :]


def gate_kernel(z_ref, order_ref, q_mine_ref, q_theirs_ref, gated_ref, z_mine_ref, z_away_ref):
    z = dot(order_ref[my_core()], z_ref[...])
    n = z.shape[0] // 2
    z_mine_ref[...] = z[:n].astype(BF)
    z_away_ref[...] = z[n:].astype(BF)
    gated_ref[pl.ds(0, n), :] = (z[:n] * q_mine_ref[...].astype(F32)).astype(BF)
    gated_ref[pl.ds(n, n), :] = (z[n:] * q_theirs_ref[...].astype(F32)).astype(BF)


def dz_kernel(*refs):
    parts, (qt_ref, order_ref, send_ref, dy_ref) = refs[:8], refs[8:]
    dy = parts[0][...].astype(F32)
    for part in parts[1:]:
        dy += part[...].astype(F32)
    dy_ref[...] = dy
    dz = (dy * qt_ref[...].astype(F32)).astype(BF)
    send_ref[...] = dot(order_ref[...], dz).astype(BF)


def transform(x, first_ref, square_ref, tc_ref, ts_ref):
    x = jnp.concatenate([x[:, u * FAC : (u + 1) * FAC] for u in range(LANE_TILES)], axis=0)
    section = dot(first_ref[...], x)
    n = section.shape[0] // 2
    re, im, tc, ts = section[:n], section[n:], tc_ref[...], ts_ref[...]
    b_re, b_im = re * tc + im * ts, im * tc - re * ts
    left = jnp.concatenate([b_re, b_im], axis=0).astype(BF)
    right = jnp.concatenate([b_im, -b_re], axis=0).astype(BF)
    f = dot(left, square_ref[:FAC]) + dot(right, square_ref[FAC:])
    return f[:n], f[n:]


def put_signal(p_re, p_im, last_ref, square_ref, tc_ref, ts_ref, out_ref):
    n, group = p_re.shape[0], p_re.shape[0] // HALF
    left = jnp.concatenate([p_re, p_im], axis=0).astype(BF)
    right = jnp.concatenate([-p_im, p_re], axis=0).astype(BF)
    c = dot(left, square_ref[:FAC]) + dot(right, square_ref[FAC:])
    re, im, tc, ts = c[:n], c[n:], tc_ref[...], ts_ref[...]
    e_re, e_im = re * tc - im * ts, im * tc + re * ts
    e = jnp.concatenate([e_re, e_im[group : n - group]], axis=0).astype(BF)
    x = dot(last_ref[...], e).astype(BF)
    rows = out_ref.shape[0]
    for u in range(LANE_TILES):
        out_ref[:, pl.ds(u * FAC, FAC)] = x[u * rows : (u + 1) * rows]


def conv_kernel(r_ref, first_ref, last_ref, square_ref, tc_ref, ts_ref, z_ref, h_ref):
    rows = z_ref.shape[0]
    group = h_ref.shape[0] // (2 * HALF)
    r = r_ref[...].astype(F32).reshape(-1, 2, group, ROW)
    u, h = (
        transform(r[:, s].reshape(rows, ROW).astype(BF), first_ref, square_ref, tc_ref, ts_ref)
        for s in range(2)
    )
    h_ref[...] = jnp.concatenate(h, axis=0).astype(BF)
    p_re, p_im = u[0] * h[0] - u[1] * h[1], u[0] * h[1] + u[1] * h[0]
    put_signal(p_re, p_im, last_ref, square_ref, tc_ref, ts_ref, z_ref)


def adjoint_kernel(r_ref, h_ref, first_ref, last_ref, square_ref, tc_ref, ts_ref, du_ref):
    g_re, g_im = transform(r_ref[...], first_ref, square_ref, tc_ref, ts_ref)
    h = h_ref[...].astype(F32)
    n = h.shape[0] // 2
    h_re, h_im = h[:n], h[n:]
    q_re, q_im = h_re * g_re + h_im * g_im, h_re * g_im - h_im * g_re
    put_signal(q_re, q_im, last_ref, square_ref, tc_ref, ts_ref, du_ref)


def weight_kernel(scale, width, *refs):
    blocks, (d_ref, d_other_ref, part_ref, mine_ref, away_ref, sem) = refs[:8], refs[8:]
    me = lax.axis_index("fsdp")
    n = blocks[0].shape[0] // 2
    copies = []
    for i, (block, move) in enumerate(zip(blocks, RING_FROM)):
        rows = rows_at(place(me, move), n)
        for j, to_ref in enumerate((mine_ref, away_ref)):
            copies.append(pltpu.make_async_copy(block.at[pl.ds(j * n, n), :], to_ref.at[rows, :], sem.at[2 * i + j]))
    for copy in copies:
        copy.start()
    for copy in copies:
        copy.wait()

    for j in range(d_ref.shape[1] // width):
        cols = pl.ds(j * width, width)
        p = dot(mine_ref[...], d_ref[:, cols]) + dot(away_ref[...], d_other_ref[:, cols])
        part_ref[:, cols] = (p * scale).astype(BF)


def finish_kernel(dy_ref, z_mine_ref, z_theirs_ref, du_ref, order_ref, k_ref, v_ref, gq_ref, gk_ref, gv_ref, gq_t_ref):
    core, n = my_core(), z_mine_ref.shape[0]
    for z_ref, half in ((z_mine_ref, core), (z_theirs_ref, 1 - core)):
        rows = rows_at(half, n)
        gq_t_ref[rows, :] = dy_ref[rows, :] * z_ref[...].astype(F32)
    gq_ref[...] = gq_t_ref[...].T.astype(BF)
    du = dot(du_ref[...].astype(F32).T.astype(BF), order_ref[...])
    gk_ref[...] = (du * v_ref[...].astype(F32)).astype(BF)
    gv_ref[...] = (du * k_ref[...].astype(F32)).astype(BF)


def call(kernel, outs, ins, scratch=(), mib=16, flops=0, specs=None):
    total = sum(math.prod(o.shape) * o.dtype.itemsize for o in (*outs, *ins))
    return pl.pallas_call(
        kernel,
        out_shape=outs,
        in_specs=specs or [VMEM] * len(ins),
        out_specs=[VMEM] * len(outs),
        scratch_shapes=scratch,
        compiler_params=params(mib),
        cost_estimate=pl.CostEstimate(flops=flops, bytes_accessed=total, transcendentals=0),
    )(*ins)


def shape(*dims, dtype=BF):
    return jax.ShapeDtypeStruct(dims, dtype)


def spread(values):
    return lax.all_to_all(values, "ctx", 0, 0, tiled=True)


def move_over(values, move):
    return lax.ppermute(values, "fsdp", [(i, place(i, move)) for i in range(8)])


RING_FROM = ((0, 0), (1, 0), (0, -1), (0, 1), (1, -1), (1, 1), (0, 2), (1, 2))


def ring(gated):
    up, down = (0, 1), (0, -1)
    other = move_over(gated, (1, 0))
    own_up, own_down = move_over(gated, up), move_over(gated, down)
    other_up, other_down = move_over(other, up), move_over(other, down)
    own_far, other_far = move_over(own_up, up), move_over(other_down, down)
    return gated, other, own_up, own_down, other_up, other_down, own_far, other_far


def dy_product(w_out, d_out):
    channels, depth = w_out.shape
    rows = d_out.shape[0]
    n, step = channels // 8, 512
    return call(
        functools.partial(dy_kernel, step),
        [shape(n, rows)] * 8,
        [w_out, d_out],
        [
            pltpu.VMEM((channels, depth), BF),
            pltpu.VMEM((rows, depth), BF),
            pltpu.SemaphoreType.DMA((8,)),
            pltpu.SemaphoreType.DMA((rows // step,)),
        ],
        mib=20,
        flops=2 * channels * depth * rows,
        specs=[ANY, ANY],
    )


def on_device(query_in, key_in, value_in, filt, w_out, d_out):
    seq_rows, width = query_in.shape
    channels, columns = w_out.shape
    ways = lax.axis_size("ctx")
    group, half = width // ways, width // 2
    n = HALF * group
    first, last, square, tc, ts = host_tables(ways, group)
    pick = np.arange(ways * group).reshape(ways // 2, 2, 2, group // 2).transpose(0, 2, 1, 3).reshape(-1)
    last_z = last.reshape(LANE_TILES, ways * group, -1)[:, pick].reshape(last.shape)
    order = channel_order(ways, group)
    order_in = np.eye(width)[order].astype(BF)
    slots = np.arange(width).reshape(ways, 2, group // 2).transpose(1, 0, 2)
    order_z = np.stack([np.eye(width)[slots[list(s)].reshape(-1)] for s in ((0, 1), (1, 0))]).astype(BF)

    core = my_core()
    swap = lambda v: lax.ppermute(v, "ctx", [(i, i ^ 1) for i in range(ways)])
    rows_like, half_like = shape(width, seq_rows), shape(half, seq_rows)

    (send,) = call(prep_kernel, [shape(ways, 2 * group, seq_rows)], [key_in, value_in, filt, order_in])
    arrived = spread(send.reshape(ways * 2 * group, seq_rows))
    own_y, *sent_y = dy_product(w_out, d_out)
    parts_y = [own_y, *(move_over(v, move) for v, move in zip(sent_y, MOVES))]

    query_t, q_mine, q_away = call(turn_query_kernel, [rows_like, half_like, half_like], [query_in])
    q_theirs, d_other = swap(q_away), swap(d_out)

    forward = 2 * 2 * n * (first.shape[1] + 2 * FAC) * FAC
    tables = (square, tc, ts)
    conv, spectrum = call(
        conv_kernel,
        [rows_like, shape(2 * n, FAC)],
        [arrived, first, last_z, *tables],
        mib=32,
        flops=3 * forward,
    )
    gated, z_mine, z_away = call(
        gate_kernel, [rows_like, half_like, half_like], [spread(conv), order_z, q_mine, q_theirs]
    )
    z_theirs = swap(z_away)

    blocks = ring(gated)
    scale = 1.0 / math.sqrt(seq_rows * ways)
    part, mine, away = call(
        functools.partial(weight_kernel, scale, 512),
        [shape(channels // 2, columns), shape(channels // 2, seq_rows), shape(channels // 2, seq_rows)],
        [*blocks, d_out, d_other],
        [pltpu.SemaphoreType.DMA((16,))],
        mib=20,
        flops=2 * channels * seq_rows * columns,
        specs=[ANY] * 8 + [VMEM] * 2,
    )

    send_z, grad_y = call(
        dz_kernel, [rows_like, shape(width, seq_rows, dtype=F32)], [*parts_y, query_t, order_in]
    )
    (adjoint,) = call(
        adjoint_kernel,
        [rows_like],
        [spread(send_z), spectrum, first, last, *tables],
        mib=32,
        flops=2 * forward,
    )
    grad_u = spread(adjoint)

    part, grad_u = lax.optimization_barrier((part, grad_u))
    groups = [list(range(c, ways, 2)) for c in range(2)]
    parts = lax.all_to_all(part, "ctx", 0, 0, tiled=True, axis_index_groups=groups)
    grad_weight = jnp.sum(parts.reshape(ways // 2, channels // ways, columns).astype(F32), axis=0)

    theirs = swap(away)
    split = lambda v: v.reshape(-1, 1, half, seq_rows)
    low, high = jnp.where(core == 0, mine, theirs), jnp.where(core == 0, theirs, mine)
    gated_all = jnp.concatenate([split(low), split(high)], axis=1).reshape(channels, seq_rows)
    layer_out = lax.dot_general(
        gated_all, w_out, (((0,), (0,)), ((), ())), preferred_element_type=F32
    ).astype(BF)

    like = shape(seq_rows, width)
    grad_query, grad_key, grad_value = call(
        finish_kernel,
        [like, like, like],
        [grad_y, z_mine, z_theirs, grad_u, order_in, key_in, value_in],
        [pltpu.VMEM((width, seq_rows), F32)],
    )
    return (layer_out, grad_query, grad_key, grad_value, grad_weight)


def solution(mesh):
    both = P("ctx", "fsdp")
    return jax.shard_map(
        on_device,
        mesh=mesh,
        in_specs=(both, both, both, both, P(None, "fsdp"), both),
        out_specs=(both, both, both, both, both),
        check_vma=False,
    )
```

```python
import functools
import math

import jax
import jax.numpy as jnp
import numpy as np
from jax import lax
from jax.experimental import pallas as pl
from jax.experimental.pallas import tpu as pltpu
from jax.sharding import PartitionSpec as P

ROW = 1024
FAC = 256
QF = 128
HALF = QF // 2 + 1
LANE_TILES = ROW // FAC
BF = jnp.bfloat16
F32 = jnp.float32
MIB = 1 << 20


def angles(rows, cols, modulus):
    product = (rows[:, None].astype(np.int64) * cols[None, :]) % modulus
    return (product.astype(np.float32) * np.float32(2.0 * math.pi / modulus)).astype(np.float64)


def host_tables(ways, group):
    k2, t1 = np.arange(HALF), np.arange(FAC)
    t2 = (np.arange(LANE_TILES)[:, None] + LANE_TILES * np.arange(ways)[None, :]).reshape(-1)
    eye = np.eye(group)
    a = angles(k2, t2, QF)
    steps = np.stack([np.cos(a), -np.sin(a)])
    first = np.einsum("rkt,cd->rkctd", steps, eye).reshape(2 * HALF * group, t2.size * group)
    weight = np.where((k2 == 0) | (k2 == QF // 2), 1.0, 2.0) / (QF * FAC)
    b = angles(t2, k2, QF)
    back = np.concatenate([np.cos(b) * weight, (-np.sin(b) * weight)[:, 1:-1]], axis=1)
    last = np.einsum("tk,cd->tckd", back, eye).reshape(t2.size * group, -1)
    s = angles(t1, t1, FAC)
    square = np.concatenate([np.cos(s), np.sin(s)])
    w = angles(k2, t1, QF * FAC)
    tc, ts = (np.repeat(f(w), group, axis=0).astype(np.float32) for f in (np.cos, np.sin))
    as_bf = lambda v: np.asarray(v, np.float32).astype(BF)
    return as_bf(first), as_bf(last), as_bf(square), tc, ts


def params(mib):
    return pltpu.CompilerParams(vmem_limit_bytes=mib * MIB)


VMEM = pl.BlockSpec(memory_space=pltpu.VMEM)
ANY = pl.BlockSpec(memory_space=pl.ANY)
ALONG_Z = (0, 1, -1, 2)


def place(index, move):
    flip, step = move
    return ((index ^ 4) if flip else index) & 4 | ((index + step) & 3)


def dot(a, b):
    return jnp.dot(a, b, preferred_element_type=F32)


def my_core():
    return lax.axis_index("ctx") & 1


def rows_at(i, n):
    return pl.ds(pl.multiple_of(i * n, n), n)


def product_t(order, values):
    return lax.dot_general(order, values, (((1,), (1,)), ((), ())), preferred_element_type=F32)


def copy_all(copies):
    for copy in copies:
        copy.start()
    for copy in copies:
        copy.wait()


def iota(axis, n):
    return lax.broadcasted_iota(jnp.int32, (n, n), axis)


def order_in(ways, width):
    row, group = iota(0, width), width // ways
    r = group // 2
    channel = (row // r % 2) * (width // 2) + (row // group) * r + row % r
    return (channel == iota(1, width)).astype(F32).astype(BF)


def order_z(ways, width):
    row, r = iota(0, width), width // ways // 2
    core = (row // (width // 2)) ^ my_core()
    slot = (row % (width // 2) // r) * 2 * r + core * r + row % r
    return (slot == iota(1, width)).astype(F32).astype(BF)


def dy_kernel(step, w_hbm, d_hbm, *refs):
    outs, (w_ref, d_ref, p_ref, w_sem, d_sem, o_sem) = refs[:4], refs[4:]
    me = lax.axis_index("fsdp")
    n = outs[0].shape[0] // 2
    gather = [
        pltpu.make_async_copy(
            w_hbm.at[rows_at(place(me, (flip, z)), n), :],
            w_ref.at[pl.ds((2 * i + flip) * n, n), :],
            w_sem.at[2 * i + flip],
        )
        for i, z in enumerate(ALONG_Z)
        for flip in range(2)
    ]
    pieces = [pl.ds(i * step, step) for i in range(d_ref.shape[0] // step)]
    loads = [
        pltpu.make_async_copy(d_hbm.at[rows, :], d_ref.at[rows, :], d_sem.at[i]) for i, rows in enumerate(pieces)
    ]
    for copy in (*gather, *loads):
        copy.start()
    for copy in gather:
        copy.wait()
    stores = []
    for i, rows in enumerate(pieces):
        loads[i].wait()
        p_ref[:, rows] = product_t(w_ref[...], d_ref[rows, :]).astype(BF)
        for j, out in enumerate(outs):
            store = pltpu.make_async_copy(
                p_ref.at[pl.ds(2 * n * j, 2 * n), rows], out.at[:, rows], o_sem.at[i * len(outs) + j]
            )
            store.start()
            stores.append(store)
    for store in stores:
        store.wait()


def prep_kernel(k_ref, v_ref, f_ref, send_ref):
    width = k_ref.shape[1]
    ways = send_ref.shape[0] // (2 * 8)
    order = order_in(ways, width)
    mixed = (k_ref[...].astype(F32) * v_ref[...].astype(F32)).astype(BF)
    parts = [product_t(order, x).reshape(ways, 1, -1, ROW) for x in (mixed, f_ref[...])]
    send_ref[...] = jnp.concatenate(parts, axis=1).reshape(send_ref.shape).astype(BF)


def turn_query_kernel(q_ref, qt_ref, mine_ref, away_ref):
    qt_ref[...] = q_ref[...].astype(F32).T.astype(BF)
    core, n = my_core(), mine_ref.shape[0]
    mine_ref[...] = qt_ref[rows_at(core, n), :]
    away_ref[...] = qt_ref[rows_at(1 - core, n), :]


def gate_kernel(ways, z_ref, q_mine_ref, q_theirs_ref, gated_ref, z_mine_ref, z_away_ref):
    z = dot(order_z(ways, z_ref.shape[0]), z_ref[...])
    n = z.shape[0] // 2
    z_mine_ref[...] = z[:n].astype(BF)
    z_away_ref[...] = z[n:].astype(BF)
    gated_ref[pl.ds(0, n), :] = (z[:n] * q_mine_ref[...].astype(F32)).astype(BF)
    gated_ref[pl.ds(n, n), :] = (z[n:] * q_theirs_ref[...].astype(F32)).astype(BF)


def sum_kernel(a_ref, b_ref, c_ref, d_ref, keep_ref, send_ref):
    n = keep_ref.shape[0]
    for out_ref, rows in ((keep_ref, pl.ds(0, n)), (send_ref, pl.ds(n, n))):
        total = a_ref[rows, :].astype(F32) + b_ref[rows, :].astype(F32)
        total += c_ref[rows, :].astype(F32) + d_ref[rows, :].astype(F32)
        out_ref[...] = total.astype(out_ref.dtype)


def dz_kernel(ways, keep_ref, other_ref, qt_ref, send_ref, dy_ref):
    dy = keep_ref[...] + other_ref[...].astype(F32)
    dy_ref[...] = dy
    dz = (dy * qt_ref[...].astype(F32)).astype(BF)
    send_ref[...] = dot(order_in(ways, dz.shape[0]), dz).astype(BF)


def transform(x, first_ref, square_ref, tc_ref, ts_ref):
    x = jnp.concatenate([x[:, u * FAC : (u + 1) * FAC] for u in range(LANE_TILES)], axis=0)
    section = dot(first_ref[...], x)
    n = section.shape[0] // 2
    re, im, tc, ts = section[:n], section[n:], tc_ref[...], ts_ref[...]
    b_re, b_im = re * tc + im * ts, im * tc - re * ts
    left = jnp.concatenate([b_re, b_im], axis=0).astype(BF)
    right = jnp.concatenate([b_im, -b_re], axis=0).astype(BF)
    f = dot(left, square_ref[:FAC]) + dot(right, square_ref[FAC:])
    return f[:n], f[n:]


def signal(p_re, p_im, last_ref, square_ref, tc_ref, ts_ref):
    n, group = p_re.shape[0], p_re.shape[0] // HALF
    left = jnp.concatenate([p_re, p_im], axis=0).astype(BF)
    right = jnp.concatenate([-p_im, p_re], axis=0).astype(BF)
    c = dot(left, square_ref[:FAC]) + dot(right, square_ref[FAC:])
    re, im, tc, ts = c[:n], c[n:], tc_ref[...], ts_ref[...]
    e_re, e_im = re * tc - im * ts, im * tc + re * ts
    e = jnp.concatenate([e_re, e_im[group : n - group]], axis=0).astype(BF)
    x = dot(last_ref[...], e)
    rows = x.shape[0] // LANE_TILES
    return jnp.concatenate([x[u * rows : (u + 1) * rows] for u in range(LANE_TILES)], axis=1)


def conv_kernel(r_ref, first_ref, last_ref, square_ref, tc_ref, ts_ref, z_ref, h_ref):
    rows = z_ref.shape[0]
    group = h_ref.shape[0] // (2 * HALF)
    r = r_ref[...].astype(F32).reshape(-1, 2, group, ROW)
    u, h = (
        transform(r[:, s].reshape(rows, ROW).astype(BF), first_ref, square_ref, tc_ref, ts_ref)
        for s in range(2)
    )
    h_ref[...] = jnp.concatenate(h, axis=0).astype(BF)
    p_re, p_im = u[0] * h[0] - u[1] * h[1], u[0] * h[1] + u[1] * h[0]
    z_ref[...] = signal(p_re, p_im, last_ref, square_ref, tc_ref, ts_ref).astype(BF)


def adjoint_kernel(r_ref, h_ref, first_ref, last_ref, square_ref, tc_ref, ts_ref, keep_ref, away_ref):
    g_re, g_im = transform(r_ref[...], first_ref, square_ref, tc_ref, ts_ref)
    h = h_ref[...].astype(F32)
    n = h.shape[0] // 2
    h_re, h_im = h[:n], h[n:]
    q_re, q_im = h_re * g_re + h_im * g_im, h_re * g_im - h_im * g_re
    du = signal(q_re, q_im, last_ref, square_ref, tc_ref, ts_ref)
    half = du.shape[0] // 2
    low, high, first_core = du[:half], du[half:], my_core() == 0
    keep_ref[...] = jnp.where(first_core, low, high).astype(BF)
    away_ref[...] = jnp.where(first_core, high, low).astype(BF)


def weight_kernel(scale, width, *refs):
    blocks, (d_hbm, d_other_hbm, pack_hbm, mine_hbm, away_hbm) = refs[:8], refs[8:13]
    mine_ref, away_ref, d_ref, d_other_ref, part_ref, sem, d_sem, o_sem = refs[13:]
    me = lax.axis_index("fsdp")
    n = blocks[0].shape[0] // 2
    copies = []
    for i, (block, move) in enumerate(zip(blocks, RING_FROM)):
        rows = rows_at(place(me, move), n)
        for j, to_ref in enumerate((mine_ref, away_ref)):
            copies.append(pltpu.make_async_copy(block.at[pl.ds(j * n, n), :], to_ref.at[rows, :], sem.at[2 * i + j]))
    pieces = [pl.ds(j * width, width) for j in range(d_ref.shape[1] // width)]
    loads = [
        pltpu.make_async_copy(from_ref.at[:, cols], to_ref.at[:, cols], d_sem.at[2 * j + i])
        for j, cols in enumerate(pieces)
        for i, (from_ref, to_ref) in enumerate(((d_hbm, d_ref), (d_other_hbm, d_other_ref)))
    ]
    for copy in (*copies, *loads):
        copy.start()
    for copy in copies:
        copy.wait()
    stores = [
        pltpu.make_async_copy(mine_ref, mine_hbm, o_sem.at[0]),
        pltpu.make_async_copy(away_ref, away_hbm, o_sem.at[1]),
    ]
    for store in stores:
        store.start()
    for j, cols in enumerate(pieces):
        loads[2 * j].wait()
        loads[2 * j + 1].wait()
        p = dot(mine_ref[...], d_ref[:, cols]) + dot(away_ref[...], d_other_ref[:, cols])
        part_ref[:, cols] = (p * scale).astype(BF)
        for g in range(8):
            store = pltpu.make_async_copy(
                part_ref.at[pl.ds(g * n, n), cols], pack_hbm.at[g, pl.ds(0, n), cols], o_sem.at[2 + 8 * j + g]
            )
            store.start()
            stores.append(store)
    for store in stores:
        store.wait()


def pack_kernel(pack_in, keep_ref, got_ref, pack_hbm, both_ref, sem):
    del pack_in
    groups, rows, _ = both_ref.shape
    pieces = [ref[...].astype(F32).reshape(groups, rows // 2, ROW) for ref in (keep_ref, got_ref)]
    both_ref[...] = jnp.concatenate(pieces, axis=1).astype(BF)
    behind = pl.ds(pack_hbm.shape[1] - rows, rows)
    copy_all([pltpu.make_async_copy(both_ref, pack_hbm.at[:, behind, :], sem.at[0])])


def final_kernel(parts_ref, dy_ref, z_mine_ref, z_theirs_ref, k_ref, v_ref, gw_ref, gq_ref, gk_ref, gv_ref, gq_t_ref):
    core, n = my_core(), z_mine_ref.shape[0]
    groups, rows, _ = parts_ref.shape
    total = parts_ref[0, pl.ds(0, n), :].astype(F32)
    for g in range(1, groups):
        total += parts_ref[g, pl.ds(0, n), :].astype(F32)
    gw_ref[...] = total
    for z_ref, half in ((z_mine_ref, core), (z_theirs_ref, 1 - core)):
        own = rows_at(half, n)
        gq_t_ref[own, :] = dy_ref[own, :] * z_ref[...].astype(F32)
    gq_ref[...] = gq_t_ref[...].T.astype(BF)
    c = (rows - n) // 2
    du = parts_ref[:, pl.ds(n, 2 * c), :].astype(F32)
    keep, got = du[:, :c], du[:, c:]
    low, high = jnp.where(core == 0, keep, got), jnp.where(core == 0, got, keep)
    width = 2 * groups * c
    du = jnp.concatenate([low, high], axis=1).reshape(width, -1)
    du = dot(du.T.astype(BF), order_in(2 * groups, width))
    gk_ref[...] = (du * v_ref[...].astype(F32)).astype(BF)
    gv_ref[...] = (du * k_ref[...].astype(F32)).astype(BF)


def staged(kernel, n_in, n_out, n_after, staged_in, staged_out):
    def run(*refs):
        ins, refs = list(refs[:n_in]), refs[n_in + n_after :]
        outs, refs = list(refs[:n_out]), refs[n_out:]
        extra = len(staged_in) + len(staged_out) + 2
        own, extra = refs[: len(refs) - extra], refs[len(refs) - extra :]
        buffers, (in_sem, out_sem) = extra[:-2], extra[-2:]
        loads, stores = [], []
        for j, i in enumerate(staged_in):
            loads.append(pltpu.make_async_copy(ins[i], buffers[j], in_sem.at[j]))
            ins[i] = buffers[j]
        for j, i in enumerate(staged_out):
            buffer = buffers[len(staged_in) + j]
            stores.append(pltpu.make_async_copy(buffer, outs[i], out_sem.at[j]))
            outs[i] = buffer
        copy_all(loads)
        kernel(*ins, *outs, *own)
        copy_all(stores)

    return run


def call(kernel, outs, ins, scratch=(), mib=16, flops=0, specs=None, after=(), staged_in=(), staged_out=(), aliases=None):
    total = sum(math.prod(o.shape) * o.dtype.itemsize for o in (*outs, *ins))
    if after or staged_in or staged_out:
        kernel = staged(kernel, len(ins), len(outs), len(after), staged_in, staged_out)
        buffers = [pltpu.VMEM(ins[i].shape, ins[i].dtype) for i in staged_in]
        buffers += [pltpu.VMEM(outs[i].shape, outs[i].dtype) for i in staged_out]
        sems = [pltpu.SemaphoreType.DMA((max(len(x), 1),)) for x in (staged_in, staged_out)]
        scratch = [*scratch, *buffers, *sems]
    in_specs, out_specs = specs or ([VMEM] * len(ins), [VMEM] * len(outs))
    in_specs = [ANY if i in staged_in else s for i, s in enumerate(in_specs)]
    out_specs = [ANY if i in staged_out else s for i, s in enumerate(out_specs)]
    return pl.pallas_call(
        kernel,
        out_shape=outs,
        in_specs=[*in_specs, *([ANY] * len(after))],
        out_specs=out_specs,
        scratch_shapes=scratch,
        input_output_aliases=aliases or {},
        compiler_params=params(mib),
        cost_estimate=pl.CostEstimate(flops=flops, bytes_accessed=total, transcendentals=0),
    )(*ins, *after)


def shape(*dims, dtype=BF):
    return jax.ShapeDtypeStruct(dims, dtype)


def spread(values):
    return lax.all_to_all(values, "ctx", 0, 0, tiled=True)


def move_over(values, move):
    return lax.ppermute(values, "fsdp", [(i, place(i, move)) for i in range(8)])


RING_FROM = ((0, 0), (1, 0), (0, -1), (0, 1), (1, -1), (1, 1), (0, 2), (1, 2))


def ring(gated):
    up, down = (0, 1), (0, -1)
    other = move_over(gated, (1, 0))
    own_up, own_down = move_over(gated, up), move_over(gated, down)
    other_up, other_down = move_over(other, up), move_over(other, down)
    own_far, other_far = move_over(own_up, up), move_over(other_down, down)
    return gated, other, own_up, own_down, other_up, other_down, own_far, other_far


def dy_product(w_out, d_out, after):
    channels, depth = w_out.shape
    rows = d_out.shape[0]
    step = 512
    pieces = rows // step
    return call(
        functools.partial(dy_kernel, step),
        [shape(channels // 4, rows)] * 4,
        [w_out, d_out],
        [
            pltpu.VMEM((channels, depth), BF),
            pltpu.VMEM((rows, depth), BF),
            pltpu.VMEM((channels, rows), BF),
            pltpu.SemaphoreType.DMA((8,)),
            pltpu.SemaphoreType.DMA((pieces,)),
            pltpu.SemaphoreType.DMA((4 * pieces,)),
        ],
        mib=24,
        flops=2 * channels * depth * rows,
        specs=([ANY] * 2, [ANY] * 4),
        after=after,
    )


def weight_product(blocks, d_out, d_other, scale, pack_rows):
    rows, columns = d_out.shape
    half = blocks[0].shape[0] * 4
    width = 512
    pieces = columns // width
    return call(
        functools.partial(weight_kernel, scale, width),
        [shape(8, pack_rows, columns), shape(half, rows), shape(half, rows)],
        [*blocks, d_out, d_other],
        [
            pltpu.VMEM((half, rows), BF),
            pltpu.VMEM((half, rows), BF),
            pltpu.VMEM((rows, columns), BF),
            pltpu.VMEM((rows, columns), BF),
            pltpu.VMEM((half, columns), BF),
            pltpu.SemaphoreType.DMA((16,)),
            pltpu.SemaphoreType.DMA((2 * pieces,)),
            pltpu.SemaphoreType.DMA((2 + 8 * pieces,)),
        ],
        mib=24,
        flops=4 * half * rows * columns,
        specs=([ANY] * 10, [ANY] * 3),
    )


def on_device(query_in, key_in, value_in, filt, w_out, d_out):
    seq_rows, width = query_in.shape
    channels, columns = w_out.shape
    ways = lax.axis_size("ctx")
    group, half = width // ways, width // 2
    n = HALF * group
    first, last, square, tc, ts = host_tables(ways, group)
    slots = np.arange(ways * group).reshape(ways // 2, 2, 2, group // 2)
    pick = lambda rows: last.reshape(LANE_TILES, ways * group, -1)[:, rows.reshape(-1)].reshape(last.shape)
    last_z = pick(slots.transpose(0, 2, 1, 3))
    last_du = pick(slots.reshape(ways // 2, 2, group).transpose(1, 0, 2))

    swap = lambda v: lax.ppermute(v, "ctx", [(i, i ^ 1) for i in range(ways)])
    rows_like, half_like = shape(width, seq_rows), shape(half, seq_rows)

    (send,) = call(
        prep_kernel,
        [shape(ways * 2 * group, seq_rows)],
        [key_in, value_in, filt],
        staged_in=(0, 1, 2),
        staged_out=(0,),
    )
    arrived = spread(send)
    own_y, *sent_y = dy_product(w_out, d_out, [send])
    came_y = [move_over(v, (0, z)) for v, z in zip(sent_y, ALONG_Z[1:])]

    forward = 2 * 2 * n * (first.shape[1] + 2 * FAC) * FAC
    tables = (square, tc, ts)
    conv, spectrum = call(
        conv_kernel,
        [rows_like, shape(2 * n, FAC)],
        [arrived, first, last_z, *tables],
        mib=32,
        flops=3 * forward,
        staged_out=(0,),
    )
    query_t, q_mine, q_away = call(
        turn_query_kernel,
        [rows_like, half_like, half_like],
        [query_in],
        after=[conv],
        staged_in=(0,),
        staged_out=(0, 1, 2),
    )
    conv, d_late = lax.optimization_barrier((conv, d_out))
    q_theirs, d_other = swap(q_away), swap(d_late)
    gated, z_mine, z_away = call(
        functools.partial(gate_kernel, ways),
        [rows_like, half_like, half_like],
        [spread(conv), q_mine, q_theirs],
        after=[d_other],
        staged_in=(0, 1, 2),
        staged_out=(0, 1, 2),
    )
    z_theirs = swap(z_away)
    blocks = ring(gated)

    keep_y, away_y = call(
        sum_kernel,
        [shape(width, seq_rows, dtype=F32), rows_like],
        [own_y, *came_y],
        after=[gated],
        staged_in=(0, 1, 2, 3),
        staged_out=(0, 1),
    )
    send_z, grad_y = call(
        functools.partial(dz_kernel, ways),
        [rows_like, shape(width, seq_rows, dtype=F32)],
        [keep_y, move_over(away_y, (1, 0)), query_t],
        staged_in=(0, 1, 2),
        staged_out=(0, 1),
    )
    du_keep, du_away = call(
        adjoint_kernel,
        [half_like, half_like],
        [spread(send_z), spectrum, first, last_du, *tables],
        mib=32,
        flops=2 * forward,
        staged_out=(1,),
    )
    du_got = swap(du_away)

    scale = 1.0 / math.sqrt(seq_rows * ways)
    pack, mine, away = weight_product(blocks, d_out, d_other, scale, half + 2 * group)
    (pack,) = call(
        pack_kernel,
        [shape(*pack.shape)],
        [pack, du_keep, du_got],
        [pltpu.VMEM((ways // 2, 2 * group, columns), BF), pltpu.SemaphoreType.DMA((1,))],
        specs=([ANY, VMEM, VMEM], [ANY]),
        aliases={0: 0},
    )
    groups = [list(range(c, ways, 2)) for c in range(2)]
    parts = lax.all_to_all(pack, "ctx", 0, 0, tiled=True, axis_index_groups=groups)

    theirs = swap(away)
    core = my_core()
    split = lambda v: v.reshape(-1, 1, half, seq_rows)
    low, high = jnp.where(core == 0, mine, theirs), jnp.where(core == 0, theirs, mine)
    gated_all = jnp.concatenate([split(low), split(high)], axis=1).reshape(channels, seq_rows)
    layer_out = lax.dot_general(
        gated_all, w_out, (((0,), (0,)), ((), ())), preferred_element_type=F32
    ).astype(BF)

    like = shape(seq_rows, width)
    grad_weight, grad_query, grad_key, grad_value = call(
        final_kernel,
        [shape(channels // ways, columns, dtype=F32), like, like, like],
        [parts, grad_y, z_mine, z_theirs, key_in, value_in],
        [pltpu.VMEM((width, seq_rows), F32)],
        after=[layer_out],
    )
    return (layer_out, grad_query, grad_key, grad_value, grad_weight)


def solution(mesh):
    both = P("ctx", "fsdp")
    return jax.shard_map(
        on_device,
        mesh=mesh,
        in_specs=(both, both, both, both, P(None, "fsdp"), both),
        out_specs=(both, both, both, both, both),
        check_vma=False,
    )
```

```python
import functools
import math

import jax
import jax.numpy as jnp
import numpy as np
from jax import lax
from jax.experimental import pallas as pl
from jax.experimental.pallas import tpu as pltpu
from jax.sharding import PartitionSpec as P

ROW = 1024
FAC = 256
QF = 128
HALF = QF // 2 + 1
LANE_TILES = ROW // FAC
BF = jnp.bfloat16
F32 = jnp.float32
MIB = 1 << 20
MOST = 56


def angles(rows, cols, modulus):
    product = (rows[:, None].astype(np.int64) * cols[None, :]) % modulus
    return (product.astype(np.float32) * np.float32(2.0 * math.pi / modulus)).astype(np.float64)


def host_tables(ways, group):
    k2, t1 = np.arange(HALF), np.arange(FAC)
    t2 = (np.arange(LANE_TILES)[:, None] + LANE_TILES * np.arange(ways)[None, :]).reshape(-1)
    eye = np.eye(group)
    a = angles(k2, t2, QF)
    steps = np.stack([np.cos(a), -np.sin(a)])
    first = np.einsum("rkt,cd->rkctd", steps, eye).reshape(2 * HALF * group, t2.size * group)
    weight = np.where((k2 == 0) | (k2 == QF // 2), 1.0, 2.0) / (QF * FAC)
    b = angles(t2, k2, QF)
    back = np.concatenate([np.cos(b) * weight, (-np.sin(b) * weight)[:, 1:-1]], axis=1)
    last = np.einsum("tk,cd->tckd", back, eye).reshape(t2.size * group, -1)
    s = angles(t1, t1, FAC)
    square = np.concatenate([np.cos(s), np.sin(s)])
    w = angles(k2, t1, QF * FAC)
    twiddle = np.concatenate([np.repeat(f(w), group, axis=0) for f in (np.cos, np.sin)]).astype(np.float32)
    as_bf = lambda v: np.asarray(v, np.float32).astype(BF)
    return as_bf(first), as_bf(square), twiddle, as_bf(last)


def params(mib):
    return pltpu.CompilerParams(vmem_limit_bytes=mib * MIB)


VMEM = pl.BlockSpec(memory_space=pltpu.VMEM)
ANY = pl.BlockSpec(memory_space=pl.ANY)
DY_MOVES = ((0, 0), (0, 2), (1, 0), (1, 2), (0, 1), (1, 1), (0, -1), (1, -1))


def place(index, move):
    flip, step = move
    return ((index ^ 4) if flip else index) & 4 | ((index + step) & 3)


def dot(a, b):
    return jnp.dot(a, b, preferred_element_type=F32)


def my_core():
    return lax.axis_index("ctx") & 1


def rows_at(i, n):
    return pl.ds(pl.multiple_of(i * n, n), n)


def product_t(order, values):
    return lax.dot_general(order, values, (((1,), (1,)), ((), ())), preferred_element_type=F32)


def copy_all(copies):
    copies = list(copies)
    for copy in copies:
        copy.start()
    for copy in copies:
        copy.wait()


def iota(axis, n):
    return lax.broadcasted_iota(jnp.int32, (n, n), axis)


def order_in(ways, width):
    row, group = iota(0, width), width // ways
    r = group // 2
    channel = (row // r % 2) * (width // 2) + (row // group) * r + row % r
    return (channel == iota(1, width)).astype(F32).astype(BF)


def order_z(ways, width):
    row, r = iota(0, width), width // ways // 2
    core = (row // (width // 2)) ^ my_core()
    slot = (row % (width // 2) // r) * 2 * r + core * r + row % r
    return (slot == iota(1, width)).astype(F32).astype(BF)


def dy_kernel(step, w_hbm, d_hbm, *refs):
    outs, (w_ref, d_ref, p_ref, w_sem, d_sem, o_sem) = refs[:4], refs[4:]
    me = lax.axis_index("fsdp")
    n = outs[0].shape[0] // 2
    gather = [
        pltpu.make_async_copy(w_hbm.at[rows_at(place(me, move), n), :], w_ref.at[pl.ds(i * n, n), :], w_sem.at[i])
        for i, move in enumerate(DY_MOVES)
    ]
    pieces = [pl.ds(i * step, step) for i in range(d_ref.shape[0] // step)]
    loads = [
        pltpu.make_async_copy(d_hbm.at[rows, :], d_ref.at[rows, :], d_sem.at[i]) for i, rows in enumerate(pieces)
    ]
    for copy in (*gather, *loads):
        copy.start()
    for copy in gather:
        copy.wait()
    stores = []
    for i, rows in enumerate(pieces):
        loads[i].wait()
        p_ref[:, rows] = product_t(w_ref[...], d_ref[rows, :]).astype(BF)
        for j, out in enumerate(outs):
            store = pltpu.make_async_copy(
                p_ref.at[pl.ds(2 * n * j, 2 * n), rows], out.at[:, rows], o_sem.at[i * len(outs) + j]
            )
            store.start()
            stores.append(store)
    for store in stores:
        store.wait()


def prep_kernel(k_ref, v_ref, f_ref, send_ref):
    width = k_ref.shape[1]
    ways = send_ref.shape[0] // (2 * 8)
    order = order_in(ways, width)
    mixed = (k_ref[...].astype(F32) * v_ref[...].astype(F32)).astype(BF)
    parts = [product_t(order, x).reshape(ways, 1, -1, ROW) for x in (mixed, f_ref[...])]
    send_ref[...] = jnp.concatenate(parts, axis=1).reshape(send_ref.shape).astype(BF)


def turn_query_kernel(q_ref, qt_ref, mine_ref, away_ref):
    qt_ref[...] = q_ref[...].astype(F32).T.astype(BF)
    core, n = my_core(), mine_ref.shape[0]
    mine_ref[...] = qt_ref[rows_at(core, n), :]
    away_ref[...] = qt_ref[rows_at(1 - core, n), :]


def gate_kernel(ways, z_ref, q_mine_ref, q_theirs_ref, gated_ref, z_mine_ref, z_away_ref):
    z = dot(order_z(ways, z_ref.shape[0]), z_ref[...])
    n = z.shape[0] // 2
    z_mine_ref[...] = z[:n].astype(BF)
    z_away_ref[...] = z[n:].astype(BF)
    gated_ref[pl.ds(0, n), :] = (z[:n] * q_mine_ref[...].astype(F32)).astype(BF)
    gated_ref[pl.ds(n, n), :] = (z[n:] * q_theirs_ref[...].astype(F32)).astype(BF)


def sum_kernel(own_ref, x_ref, up_ref, down_ref, keep_ref, far_ref, side_ref):
    n = keep_ref.shape[0]
    near, second = pl.ds(0, n), pl.ds(n, n)
    own = own_ref[near, :].astype(F32) + x_ref[near, :].astype(F32)
    keep_ref[...] = own + (up_ref[near, :].astype(F32) + down_ref[near, :].astype(F32))
    far_ref[...] = (own_ref[second, :].astype(F32) + x_ref[second, :].astype(F32)).astype(BF)
    side_ref[...] = (up_ref[second, :].astype(F32) + down_ref[second, :].astype(F32)).astype(BF)


def dz_kernel(ways, keep_ref, far_ref, side_ref, qt_ref, send_ref):
    dy = keep_ref[...] + (far_ref[...].astype(F32) + side_ref[...].astype(F32))
    dz = (dy * qt_ref[...].astype(F32)).astype(BF)
    send_ref[...] = dot(order_in(ways, dz.shape[0]), dz).astype(BF)


def query_kernel(keep_ref, far_ref, side_ref, z_mine_ref, z_theirs_ref, gq_ref, gq_t_ref):
    gq_t_ref[...] = keep_ref[...] + (far_ref[...].astype(F32) + side_ref[...].astype(F32))
    core, n = my_core(), z_mine_ref.shape[0]
    for z_ref, half in ((z_mine_ref, core), (z_theirs_ref, 1 - core)):
        own = rows_at(half, n)
        gq_t_ref[own, :] *= z_ref[...].astype(F32)
    gq_ref[...] = gq_t_ref[...].T.astype(BF)


class Tables:
    def __init__(self, hbm, vmem, sem):
        self.refs = dict(zip(("first", "square", "twiddle", "last"), vmem))
        self.loads = {
            name: pltpu.make_async_copy(x, to, sem.at[i]) for i, (name, x, to) in enumerate(zip(self.refs, hbm, vmem))
        }

    def start(self):
        for load in self.loads.values():
            load.start()

    def __getitem__(self, name):
        if name in self.loads:
            self.loads.pop(name).wait()
        return self.refs[name]


def times_square(left, right, tables):
    square = tables["square"]
    return dot(left, square[:FAC]) + dot(right, square[FAC:])


def transform(x, tables):
    x = jnp.concatenate([x[:, u * FAC : (u + 1) * FAC] for u in range(LANE_TILES)], axis=0)
    section = dot(tables["first"][...], x)
    n = section.shape[0] // 2
    twiddle = tables["twiddle"]
    re, im, tc, ts = section[:n], section[n:], twiddle[:n], twiddle[n:]
    b_re, b_im = re * tc + im * ts, im * tc - re * ts
    left = jnp.concatenate([b_re, b_im], axis=0).astype(BF)
    right = jnp.concatenate([b_im, -b_re], axis=0).astype(BF)
    f = times_square(left, right, tables)
    return f[:n], f[n:]


def signal(p_re, p_im, tables):
    n, group = p_re.shape[0], p_re.shape[0] // HALF
    left = jnp.concatenate([p_re, p_im], axis=0).astype(BF)
    right = jnp.concatenate([-p_im, p_re], axis=0).astype(BF)
    c = times_square(left, right, tables)
    twiddle = tables["twiddle"]
    re, im, tc, ts = c[:n], c[n:], twiddle[:n], twiddle[n:]
    e_re, e_im = re * tc - im * ts, im * tc + re * ts
    e = jnp.concatenate([e_re, e_im[group : n - group]], axis=0).astype(BF)
    x = dot(tables["last"][...], e)
    rows = x.shape[0] // LANE_TILES
    return jnp.concatenate([x[u * rows : (u + 1) * rows] for u in range(LANE_TILES)], axis=1)


def conv_kernel(*refs):
    (r_hbm, *tables_hbm), (z_hbm, h_hbm) = refs[:5], refs[7:9]
    r_ref, z_ref, h_ref, *tables, table_sem, sem = refs[9:]
    tables = Tables(tables_hbm, tables, table_sem)
    load = pltpu.make_async_copy(r_hbm, r_ref, sem.at[0])
    load.start()
    tables.start()
    rows = z_ref.shape[0]
    group = h_ref.shape[0] // (2 * HALF)
    load.wait()
    r = r_ref[...].astype(F32).reshape(-1, 2, group, ROW)
    u, h = (transform(r[:, s].reshape(rows, ROW).astype(BF), tables) for s in range(2))
    h_ref[...] = jnp.concatenate(h, axis=0).astype(BF)
    h_store = pltpu.make_async_copy(h_ref, h_hbm, sem.at[1])
    h_store.start()
    p_re, p_im = u[0] * h[0] - u[1] * h[1], u[0] * h[1] + u[1] * h[0]
    z_ref[...] = signal(p_re, p_im, tables).astype(BF)
    z_store = pltpu.make_async_copy(z_ref, z_hbm, sem.at[2])
    z_store.start()
    h_store.wait()
    z_store.wait()


def adjoint_kernel(*refs):
    (r_hbm, h_hbm, *tables_hbm), outs = refs[:6], refs[7:9]
    r_ref, h_ref, keep_ref, away_ref, *tables, table_sem, sem = refs[9:]
    tables = Tables(tables_hbm, tables, table_sem)
    load = pltpu.make_async_copy(r_hbm, r_ref, sem.at[0])
    h_load = pltpu.make_async_copy(h_hbm, h_ref, sem.at[1])
    load.start()
    tables.start()
    h_load.start()
    load.wait()
    g_re, g_im = transform(r_ref[...], tables)
    h_load.wait()
    h = h_ref[...].astype(F32)
    n = h.shape[0] // 2
    h_re, h_im = h[:n], h[n:]
    q_re, q_im = h_re * g_re + h_im * g_im, h_re * g_im - h_im * g_re
    du = signal(q_re, q_im, tables)
    half = du.shape[0] // 2
    low, high, first_core = du[:half], du[half:], my_core() == 0
    keep_ref[...] = jnp.where(first_core, low, high).astype(BF)
    away_ref[...] = jnp.where(first_core, high, low).astype(BF)
    copy_all([pltpu.make_async_copy(x, to, sem.at[2 + i]) for i, (x, to) in enumerate(zip((away_ref, keep_ref), outs))])


def weight_kernel(scale, width, moves, *refs):
    count = len(moves)
    blocks, (d_ref, d_other_ref), refs = refs[:count], refs[count : count + 2], refs[-7:]
    pack_hbm, away_hbm, mine_ref, away_ref, part_ref, sem, o_sem = refs
    me = lax.axis_index("fsdp")
    n = blocks[0].shape[0] // 2
    places = [place(me, move) for move in moves]
    copy_all(
        pltpu.make_async_copy(block.at[pl.ds(j * n, n), :], to_ref.at[pl.ds(i * n, n), :], sem.at[2 * i + j])
        for i, block in enumerate(blocks)
        for j, to_ref in enumerate((mine_ref, away_ref))
    )
    stores = [pltpu.make_async_copy(away_ref, away_hbm, o_sem.at[0])]
    stores[0].start()
    for j in range(d_ref.shape[1] // width):
        cols = pl.ds(j * width, width)
        p = dot(mine_ref[...], d_ref[:, cols]) + dot(away_ref[...], d_other_ref[:, cols])
        part_ref[:, cols] = (p * scale).astype(BF)
        for i in range(count):
            store = pltpu.make_async_copy(
                part_ref.at[pl.ds(i * n, n), cols],
                pack_hbm.at[places[i], pl.ds(0, n), cols],
                o_sem.at[1 + j * count + i],
            )
            store.start()
            stores.append(store)
    for store in stores:
        store.wait()


def assemble_kernel(*refs):
    blocks, theirs, (all_hbm, sem) = refs[:8], refs[8:10], refs[10:]
    me, core = lax.axis_index("fsdp"), my_core()
    n = blocks[0].shape[0] // 2
    copies = []
    for i, (block, move) in enumerate(zip(blocks, RING_FROM)):
        start = 2 * place(me, move)
        other = theirs[i // 4].at[pl.ds(i % 4 * n, n), :]
        for j, (x, half) in enumerate(((block.at[pl.ds(0, n), :], core), (other, 1 - core))):
            copies.append(pltpu.make_async_copy(x, all_hbm.at[rows_at(start + half, n), :], sem.at[2 * i + j]))
    copy_all(copies)


def pack_kernel(pack_in, keep_ref, got_ref, pack_hbm, both_ref, sem):
    del pack_in
    groups, rows, _ = both_ref.shape
    pieces = [ref[...].astype(F32).reshape(groups, rows // 2, ROW) for ref in (keep_ref, got_ref)]
    both_ref[...] = jnp.concatenate(pieces, axis=1).astype(BF)
    behind = pl.ds(pack_hbm.shape[1] - rows, rows)
    copy_all([pltpu.make_async_copy(both_ref, pack_hbm.at[:, behind, :], sem.at[0])])


def final_kernel(parts_ref, k_ref, v_ref, gw_ref, gk_ref, gv_ref):
    n = gw_ref.shape[0]
    groups, rows, _ = parts_ref.shape
    total = parts_ref[0, pl.ds(0, n), :].astype(F32)
    for g in range(1, groups):
        total += parts_ref[g, pl.ds(0, n), :].astype(F32)
    gw_ref[...] = total
    c = (rows - n) // 2
    du = parts_ref[:, pl.ds(n, 2 * c), :].astype(F32)
    keep, got = du[:, :c], du[:, c:]
    first_core = my_core() == 0
    low, high = jnp.where(first_core, keep, got), jnp.where(first_core, got, keep)
    width = 2 * groups * c
    du = jnp.concatenate([low, high], axis=1).reshape(width, -1)
    du = dot(du.T.astype(BF), order_in(2 * groups, width))
    gk_ref[...] = (du * v_ref[...].astype(F32)).astype(BF)
    gv_ref[...] = (du * k_ref[...].astype(F32)).astype(BF)


def staged(kernel, n_in, n_out, n_after, staged_in, staged_out):
    def run(*refs):
        ins, refs = list(refs[:n_in]), refs[n_in + n_after :]
        outs, refs = list(refs[:n_out]), refs[n_out:]
        extra = len(staged_in) + len(staged_out) + 2
        own, extra = refs[: len(refs) - extra], refs[len(refs) - extra :]
        buffers, (in_sem, out_sem) = extra[:-2], extra[-2:]
        loads, stores = [], []
        for j, i in enumerate(staged_in):
            loads.append(pltpu.make_async_copy(ins[i], buffers[j], in_sem.at[j]))
            ins[i] = buffers[j]
        for j, i in enumerate(staged_out):
            buffer = buffers[len(staged_in) + j]
            stores.append(pltpu.make_async_copy(buffer, outs[i], out_sem.at[j]))
            outs[i] = buffer
        copy_all(loads)
        kernel(*ins, *outs, *own)
        copy_all(stores)

    return run


def call(kernel, outs, ins, scratch=(), mib=16, flops=0, specs=None, after=(), staged_in=(), staged_out=(), aliases=None):
    total = sum(math.prod(o.shape) * o.dtype.itemsize for o in (*outs, *ins))
    if after or staged_in or staged_out:
        kernel = staged(kernel, len(ins), len(outs), len(after), staged_in, staged_out)
        buffers = [pltpu.VMEM(ins[i].shape, ins[i].dtype) for i in staged_in]
        buffers += [pltpu.VMEM(outs[i].shape, outs[i].dtype) for i in staged_out]
        sems = [pltpu.SemaphoreType.DMA((max(len(x), 1),)) for x in (staged_in, staged_out)]
        scratch = [*scratch, *buffers, *sems]
    in_specs, out_specs = specs or ([VMEM] * len(ins), [VMEM] * len(outs))
    in_specs = [ANY if i in staged_in else s for i, s in enumerate(in_specs)]
    out_specs = [ANY if i in staged_out else s for i, s in enumerate(out_specs)]
    return pl.pallas_call(
        kernel,
        out_shape=outs,
        in_specs=[*in_specs, *([ANY] * len(after))],
        out_specs=out_specs,
        scratch_shapes=scratch,
        input_output_aliases=aliases or {},
        compiler_params=params(mib),
        cost_estimate=pl.CostEstimate(flops=0, bytes_accessed=0, transcendentals=0),
    )(*ins, *after)


def shape(*dims, dtype=BF):
    return jax.ShapeDtypeStruct(dims, dtype)


def spread(values):
    return lax.all_to_all(values, "ctx", 0, 0, tiled=True)


def move_over(values, move):
    return lax.ppermute(values, "fsdp", [(i, place(i, move)) for i in range(8)])


RING_FROM = ((0, 0), (1, 0), (0, -1), (0, 1), (1, -1), (1, 1), (0, 2), (1, 2))


def ring_near(gated):
    up, down = (0, 1), (0, -1)
    other = move_over(gated, (1, 0))
    own_up, own_down = move_over(gated, up), move_over(gated, down)
    return gated, other, own_up, own_down, move_over(other, up), move_over(other, down)


def ring_far(own_up, other_down):
    return move_over(own_up, (0, 1)), move_over(other_down, (0, -1))


def dy_product(w_out, d_out, after):
    channels, depth = w_out.shape
    rows = d_out.shape[0]
    step = 512
    pieces = rows // step
    return call(
        functools.partial(dy_kernel, step),
        [shape(channels // 4, rows)] * 4,
        [w_out, d_out],
        [
            pltpu.VMEM((channels, depth), BF),
            pltpu.VMEM((rows, depth), BF),
            pltpu.VMEM((channels, rows), BF),
            pltpu.SemaphoreType.DMA((8,)),
            pltpu.SemaphoreType.DMA((pieces,)),
            pltpu.SemaphoreType.DMA((4 * pieces,)),
        ],
        flops=2 * channels * depth * rows,
        mib=MOST,
        specs=([ANY] * 2, [ANY] * 4),
        after=after,
    )


def weight_product(blocks, moves, d_out, d_other, scale, pack_rows, so_far=(), after=()):
    rows, columns = d_out.shape
    n = blocks[0].shape[0] // 2
    count, width = len(moves), 512
    ins = [*blocks, d_out, d_other]
    return call(
        functools.partial(weight_kernel, scale, width, moves),
        [shape(8, pack_rows, columns), shape(count * n, rows)],
        [*ins, *so_far],
        [
            pltpu.VMEM((count * n, rows), BF),
            pltpu.VMEM((count * n, rows), BF),
            pltpu.VMEM((count * n, columns), BF),
            pltpu.SemaphoreType.DMA((2 * count,)),
            pltpu.SemaphoreType.DMA((1 + columns // width * count,)),
        ],
        flops=4 * count * n * rows * columns,
        specs=([ANY] * count + [VMEM] * 2 + [ANY] * len(so_far), [ANY] * 2),
        after=after,
        aliases={len(ins) + i: i for i in range(len(so_far))},
    )


def on_device(query_in, key_in, value_in, filt, w_out, d_out):
    seq_rows, width = query_in.shape
    channels, columns = w_out.shape
    ways = lax.axis_size("ctx")
    group, half = width // ways, width // 2
    n = HALF * group
    *tables, last = host_tables(ways, group)
    slots = np.arange(ways * group).reshape(ways // 2, 2, 2, group // 2)
    pick = lambda rows: last.reshape(LANE_TILES, ways * group, -1)[:, rows.reshape(-1)].reshape(last.shape)
    last_z = pick(slots.transpose(0, 2, 1, 3))
    last_du = pick(slots.reshape(ways // 2, 2, group).transpose(1, 0, 2))

    swap = lambda v: lax.ppermute(v, "ctx", [(i, i ^ 1) for i in range(ways)])
    rows_like, half_like = shape(width, seq_rows), shape(half, seq_rows)

    (send,) = call(
        prep_kernel,
        [shape(ways * 2 * group, seq_rows)],
        [key_in, value_in, filt],
        mib=MOST,
        staged_in=(0, 1, 2),
        staged_out=(0,),
    )
    arrived = spread(send)
    own_y, x_y, up_y, down_y = dy_product(w_out, d_out, [send])
    keep_y, far_y, side_y = call(
        sum_kernel,
        [shape(width, seq_rows, dtype=F32), rows_like, rows_like],
        [own_y, move_over(x_y, (1, 0)), move_over(up_y, (0, 1)), move_over(down_y, (0, -1))],
    )

    query_t, q_mine, q_away = call(
        turn_query_kernel, [rows_like, half_like, half_like], [query_in], after=[own_y], mib=MOST, staged_in=(0,), staged_out=(0, 1, 2)
    )
    q_theirs = swap(q_away)

    flops = 2 * 2 * n * (tables[0].shape[1] + 2 * FAC) * FAC
    table_buffers = [pltpu.VMEM(x.shape, x.dtype) for x in (*tables, last)] + [pltpu.SemaphoreType.DMA((4,))]
    spectrum_like = shape(2 * n, FAC)
    conv, spectrum = call(
        conv_kernel,
        [rows_like, spectrum_like],
        [arrived, *tables, last_z, q_theirs, far_y],
        [pltpu.VMEM(x.shape, x.dtype) for x in (arrived, rows_like, spectrum_like)]
        + [*table_buffers, pltpu.SemaphoreType.DMA((3,))],
        mib=MOST,
        flops=3 * flops,
        specs=([ANY] * 7, [ANY] * 2),
    )
    conv, d_late = lax.optimization_barrier((conv, d_out))
    d_other = swap(d_late)
    dy = (keep_y, move_over(far_y, (0, 2)), move_over(side_y, (1, 0)))
    (send_z,) = call(
        functools.partial(dz_kernel, ways), [rows_like], [*dy, query_t], staged_out=(0,)
    )
    gated, z_mine, z_away = call(
        functools.partial(gate_kernel, ways),
        [rows_like, half_like, half_like],
        [spread(conv), q_mine, q_theirs],
        after=[d_other, send_z],
    )
    z_theirs = swap(z_away)
    blocks = ring_near(gated)
    blocks = (*blocks, *ring_far(blocks[2], blocks[5]))
    like = shape(seq_rows, width)
    (grad_query,) = call(
        query_kernel, [like], [*dy, z_mine, z_theirs], [pltpu.VMEM((width, seq_rows), F32)], staged_out=(0,)
    )
    scale = 1.0 / math.sqrt(seq_rows * ways)
    weight = functools.partial(weight_product, d_out=d_out, d_other=d_other, scale=scale, pack_rows=half + 2 * group)
    pack, away = weight(blocks[:4], RING_FROM[:4])
    theirs_near = swap(away)
    du_away, du_keep = call(
        adjoint_kernel,
        [half_like, half_like],
        [spread(send_z), spectrum, *tables, last_du, theirs_near],
        [pltpu.VMEM(x.shape, x.dtype) for x in (rows_like, spectrum_like, half_like, half_like)]
        + [*table_buffers, pltpu.SemaphoreType.DMA((4,))],
        mib=MOST,
        flops=2 * flops,
        specs=([ANY] * 7, [ANY] * 2),
    )
    du_got = swap(du_away)
    pack, away = weight(blocks[4:], RING_FROM[4:], so_far=(pack,))
    (pack,) = call(
        pack_kernel,
        [shape(*pack.shape)],
        [pack, du_keep, du_got],
        [pltpu.VMEM((ways // 2, 2 * group, columns), BF), pltpu.SemaphoreType.DMA((1,))],
        specs=([ANY, VMEM, VMEM], [ANY]),
        aliases={0: 0},
    )
    groups = [list(range(c, ways, 2)) for c in range(2)]
    parts = lax.all_to_all(pack, "ctx", 0, 0, tiled=True, axis_index_groups=groups)

    (gated_all,) = call(
        assemble_kernel,
        [shape(channels, seq_rows)],
        [*blocks, theirs_near, swap(away)],
        [pltpu.SemaphoreType.DMA((16,))],
        specs=([ANY] * 10, [ANY]),
    )
    layer_out = lax.dot_general(
        gated_all, w_out, (((0,), (0,)), ((), ())), preferred_element_type=F32
    ).astype(BF)

    grad_weight, grad_key, grad_value = call(
        final_kernel,
        [shape(channels // ways, columns, dtype=F32), like, like],
        [parts, key_in, value_in],
        mib=MOST,
        after=[layer_out, grad_query],
        staged_in=(0, 1, 2),
        staged_out=(0, 1, 2),
    )
    return (layer_out, grad_query, grad_key, grad_value, grad_weight)


def solution(mesh):
    both = P("ctx", "fsdp")
    return jax.shard_map(
        on_device,
        mesh=mesh,
        in_specs=(both, both, both, both, P(None, "fsdp"), both),
        out_specs=(both, both, both, both, both),
        check_vma=False,
    )
```

```python
import functools
import math
import typing

import jax
import jax.numpy as jnp
import numpy as np
from jax import lax
from jax.experimental import pallas as pl
from jax.experimental.pallas import tpu as pltpu
from jax.sharding import PartitionSpec as P

ROW = 1024
FAC = 256
QF = 128
HALF = QF // 2 + 1
LANE_TILES = ROW // FAC
BF = jnp.bfloat16
F32 = jnp.float32
MIB = 1 << 20
MOST = 56


def angles(rows, cols, modulus):
    product = (rows[:, None].astype(np.int64) * cols[None, :]) % modulus
    return (product.astype(np.float32) * np.float32(2.0 * math.pi / modulus)).astype(np.float64)


def host_tables(ways, group):
    k2, t1 = np.arange(HALF), np.arange(FAC)
    t2 = (np.arange(LANE_TILES)[:, None] + LANE_TILES * np.arange(ways)[None, :]).reshape(-1)
    eye = np.eye(group)
    a = angles(k2, t2, QF)
    steps = np.stack([np.cos(a), -np.sin(a)])
    first = np.einsum("rkt,cd->rkctd", steps, eye).reshape(2 * HALF * group, t2.size * group)
    weight = np.where((k2 == 0) | (k2 == QF // 2), 1.0, 2.0) / (QF * FAC)
    b = angles(t2, k2, QF)
    back = np.concatenate([np.cos(b) * weight, (-np.sin(b) * weight)[:, 1:-1]], axis=1)
    last = np.einsum("tk,cd->tckd", back, eye).reshape(t2.size * group, -1)
    s = angles(t1, t1, FAC)
    square = np.concatenate([np.cos(s), np.sin(s)])
    w = angles(k2, t1, QF * FAC)
    twiddle = np.concatenate([np.repeat(f(w), group, axis=0) for f in (np.cos, np.sin)]).astype(np.float32)
    as_bf = lambda v: np.asarray(v, np.float32).astype(BF)
    return as_bf(first), as_bf(square), twiddle, as_bf(last)


def params(mib):
    return pltpu.CompilerParams(vmem_limit_bytes=mib * MIB)


VMEM = pl.BlockSpec(memory_space=pltpu.VMEM)
ANY = pl.BlockSpec(memory_space=pl.ANY)
DY_MOVES = ((0, 0), (0, 2), (1, 0), (1, 2), (0, 1), (1, 1), (0, -1), (1, -1))
SLOT = {move: i for i, (flip, step) in enumerate(DY_MOVES) for move in ((flip, step % 4),)}


def place(index, move):
    flip, step = move
    return ((index ^ 4) if flip else index) & 4 | ((index + step) & 3)


def dot(a, b):
    return jnp.dot(a, b, preferred_element_type=F32)


def my_core():
    return lax.axis_index("ctx") & 1


def rows_at(i, n):
    return pl.ds(pl.multiple_of(i * n, n), n)


def product_t(order, values):
    return lax.dot_general(order, values, (((1,), (1,)), ((), ())), preferred_element_type=F32)


def copy_all(copies):
    copies = list(copies)
    for copy in copies:
        copy.start()
    for copy in copies:
        copy.wait()


def iota(axis, n):
    return lax.broadcasted_iota(jnp.int32, (n, n), axis)


def order_in(ways, width):
    row, group = iota(0, width), width // ways
    r = group // 2
    channel = (row // r % 2) * (width // 2) + (row // group) * r + row % r
    return (channel == iota(1, width)).astype(F32).astype(BF)


def order_z(ways, width):
    row = lax.broadcasted_iota(jnp.int32, (width, 2 * width), 0)
    column = lax.broadcasted_iota(jnp.int32, (width, 2 * width), 1)
    r = width // ways // 2
    core = (row // (width // 2)) ^ my_core()
    slot = (row % (width // 2) // r) * 4 * r + core * r + row % r
    return (slot == column).astype(F32).astype(BF)


def dy_kernel(step, moves, w_hbm, d_hbm, *refs):
    outs, (w_ref, d_ref, p_ref, w_sem, d_sem, o_sem) = refs[:-6], refs[-6:]
    me = lax.axis_index("fsdp")
    n = outs[0].shape[0] // 2
    gather = [
        pltpu.make_async_copy(w_hbm.at[rows_at(place(me, move), n), :], w_ref.at[pl.ds(i * n, n), :], w_sem.at[i])
        for i, move in enumerate(moves)
    ]
    pieces = [pl.ds(i * step, step) for i in range(d_ref.shape[0] // step)]
    loads = [
        pltpu.make_async_copy(d_hbm.at[rows, :], d_ref.at[rows, :], d_sem.at[i]) for i, rows in enumerate(pieces)
    ]
    for copy in (*gather, loads[0]):
        copy.start()
    for copy in gather:
        copy.wait()
    stores = []
    for i, rows in enumerate(pieces):
        loads[i].wait()
        if i + 1 < len(pieces):
            loads[i + 1].start()
        p_ref[:, rows] = product_t(w_ref[...], d_ref[rows, :]).astype(BF)
        for j, out in enumerate(outs):
            store = pltpu.make_async_copy(
                p_ref.at[pl.ds(2 * n * j, 2 * n), rows], out.at[:, rows], o_sem.at[i * len(outs) + j]
            )
            store.start()
            stores.append(store)
    for store in stores:
        store.wait()


def prep_kernel(k_ref, v_ref, f_ref, send_ref):
    width = k_ref.shape[1]
    ways = send_ref.shape[0] // (2 * 8)
    order = order_in(ways, width)
    mixed = (k_ref[...].astype(F32) * v_ref[...].astype(F32)).astype(BF)
    parts = [product_t(order, x).reshape(ways, 1, -1, ROW) for x in (mixed, f_ref[...])]
    send_ref[...] = jnp.concatenate(parts, axis=1).reshape(send_ref.shape).astype(BF)


def turn_query_kernel(q_ref, mine_ref, away_ref, qt_ref):
    qt_ref[...] = q_ref[...].astype(F32).T
    core, n = my_core(), mine_ref.shape[0]
    mine_ref[...] = qt_ref[rows_at(core, n), :].astype(BF)
    away_ref[...] = qt_ref[rows_at(1 - core, n), :].astype(BF)


def gate_kernel(ways, z_ref, q_mine_ref, q_theirs_ref, gated_ref, z_away_ref):
    z = dot(order_z(ways, gated_ref.shape[0]), z_ref[...])
    n = z.shape[0] // 2
    z_away_ref[...] = z[n:].astype(BF)
    gated_ref[pl.ds(0, n), :] = (z[:n] * q_mine_ref[...].astype(F32)).astype(BF)
    gated_ref[pl.ds(n, n), :] = (z[n:] * q_theirs_ref[...].astype(F32)).astype(BF)


def sum_kernel(own_ref, x_ref, up_ref, down_ref, keep_ref, far_ref, side_ref):
    n = keep_ref.shape[0]
    near, second = pl.ds(0, n), pl.ds(n, n)
    own = own_ref[near, :].astype(F32) + x_ref[near, :].astype(F32)
    keep_ref[...] = own + (up_ref[near, :].astype(F32) + down_ref[near, :].astype(F32))
    far_ref[...] = (own_ref[second, :].astype(F32) + x_ref[second, :].astype(F32)).astype(BF)
    side_ref[...] = (up_ref[second, :].astype(F32) + down_ref[second, :].astype(F32)).astype(BF)


def dz_kernel(ways, keep_ref, far_ref, side_ref, q_ref, z_ref, send_ref):
    dy = keep_ref[...] + (far_ref[...].astype(F32) + side_ref[...].astype(F32))
    dz = (dy * q_ref[...].astype(F32).T).astype(BF)
    pieces = (z_ref[...].astype(F32), dot(order_in(ways, dz.shape[0]), dz))
    both = jnp.concatenate([x.reshape(ways, 1, -1, ROW) for x in pieces], axis=1)
    send_ref[...] = both.reshape(send_ref.shape).astype(BF)


def query_kernel(ways, keep_ref, far_ref, side_ref, z_ref, z_theirs_ref, gq_ref, gq_t_ref):
    gq_t_ref[...] = keep_ref[...] + (far_ref[...].astype(F32) + side_ref[...].astype(F32))
    core, n = my_core(), z_theirs_ref.shape[0]
    z_mine = dot(order_z(ways, gq_t_ref.shape[0])[:n], z_ref[...]).astype(BF)
    for z, half in ((z_mine, core), (z_theirs_ref[...], 1 - core)):
        own = rows_at(half, n)
        gq_t_ref[own, :] *= z.astype(F32)
    gq_ref[...] = gq_t_ref[...].T.astype(BF)


class Tables(typing.NamedTuple):
    first: typing.Any
    square: typing.Any
    twiddle: typing.Any
    last: typing.Any


def times_square(left, right, tables):
    square = tables.square
    return dot(left, square[:FAC]) + dot(right, square[FAC:])


def transform(x, tables):
    x = jnp.concatenate([x[:, u * FAC : (u + 1) * FAC] for u in range(LANE_TILES)], axis=0)
    section = dot(tables.first[...], x)
    n = section.shape[0] // 2
    twiddle = tables.twiddle
    re, im, tc, ts = section[:n], section[n:], twiddle[:n], twiddle[n:]
    b_re, b_im = re * tc + im * ts, im * tc - re * ts
    left = jnp.concatenate([b_re, b_im], axis=0).astype(BF)
    right = jnp.concatenate([b_im, -b_re], axis=0).astype(BF)
    f = times_square(left, right, tables)
    return f[:n], f[n:]


def signal(p_re, p_im, tables):
    n, group = p_re.shape[0], p_re.shape[0] // HALF
    left = jnp.concatenate([p_re, p_im], axis=0).astype(BF)
    right = jnp.concatenate([-p_im, p_re], axis=0).astype(BF)
    c = times_square(left, right, tables)
    twiddle = tables.twiddle
    re, im, tc, ts = c[:n], c[n:], twiddle[:n], twiddle[n:]
    e_re, e_im = re * tc - im * ts, im * tc + re * ts
    e = jnp.concatenate([e_re, e_im[group : n - group]], axis=0).astype(BF)
    x = dot(tables.last[...], e)
    rows = x.shape[0] // LANE_TILES
    return jnp.concatenate([x[u * rows : (u + 1) * rows] for u in range(LANE_TILES)], axis=1)


def conv_kernel(r_ref, first_ref, square_ref, twiddle_ref, last_ref, z_ref, h_ref):
    tables = Tables(first_ref, square_ref, twiddle_ref, last_ref)
    rows = z_ref.shape[0]
    group = h_ref.shape[0] // (2 * HALF)
    r = r_ref[...].astype(F32).reshape(-1, 2, group, ROW)
    u, h = (transform(r[:, s].reshape(rows, ROW).astype(BF), tables) for s in range(2))
    h_ref[...] = jnp.concatenate(h, axis=0).astype(BF)
    p_re, p_im = u[0] * h[0] - u[1] * h[1], u[0] * h[1] + u[1] * h[0]
    z_ref[...] = signal(p_re, p_im, tables).astype(BF)


def adjoint_kernel(r_ref, h_ref, first_ref, square_ref, twiddle_ref, last_ref, du_ref):
    tables = Tables(first_ref, square_ref, twiddle_ref, last_ref)
    rows = du_ref.shape[0]
    group = h_ref.shape[0] // (2 * HALF)
    r = r_ref[...].astype(F32).reshape(-1, 2, group, ROW)[:, 1]
    g_re, g_im = transform(r.reshape(rows, ROW).astype(BF), tables)
    h = h_ref[...].astype(F32)
    n = h.shape[0] // 2
    h_re, h_im = h[:n], h[n:]
    q_re, q_im = h_re * g_re + h_im * g_im, h_re * g_im - h_im * g_re
    du_ref[...] = signal(q_re, q_im, tables).astype(BF)


def weight_rows(scale, moves, blocks, d_ref, d_other_ref, away_ref, part_ref, loaded=()):
    me, ctx = lax.axis_index("fsdp"), lax.axis_index("ctx")
    n = blocks[0].shape[0] // 2
    mine = jnp.concatenate([block[:n] for block in blocks], axis=0)
    away = jnp.concatenate([block[n:] for block in blocks], axis=0)
    away_ref[...] = away
    p = dot(mine, d_ref[...]) + dot(away, d_other_ref[...])
    p = (p * scale).astype(BF)
    for load in loaded:
        load.wait()
    for i, move in enumerate(moves):
        to = place(me, move)
        flip, step = (to ^ (ctx // 2)) & 1, (to // 2 - ctx // 4) & 3
        slot = jnp.int32(0)
        for (f, d), at in SLOT.items():
            slot = jnp.where((flip == f) & (step == d), at, slot)
        part_ref[rows_at(slot, n), :] = p[i * n : (i + 1) * n]


def near_kernel(scale, moves, *refs):
    count = len(moves)
    blocks, (d_ref, d_other_ref, part_ref, away_ref) = refs[:count], refs[count:]
    weight_rows(scale, moves, blocks, d_ref, d_other_ref, away_ref, part_ref)


def far_kernel(scale, moves, *refs):
    count = len(moves)
    blocks, (d_ref, d_other_ref, near_hbm), refs = refs[:count], refs[count : count + 3], refs[count + 3 :]
    outs, away_ref, (part_ref, sem) = refs[:4], refs[4], refs[5:]
    near = pltpu.make_async_copy(near_hbm, part_ref, sem.at[4])
    near.start()
    weight_rows(scale, moves, blocks, d_ref, d_other_ref, away_ref, part_ref, [near])
    n = outs[0].shape[0]
    copy_all(pltpu.make_async_copy(part_ref.at[pl.ds(i * n, n), :], out, sem.at[i]) for i, out in enumerate(outs))


def assemble_kernel(*refs):
    blocks, theirs, (all_hbm, sem) = refs[:8], refs[8:10], refs[10:]
    me, core = lax.axis_index("fsdp"), my_core()
    n = blocks[0].shape[0] // 2
    copies = []
    for i, (block, move) in enumerate(zip(blocks, RING_FROM)):
        start = 2 * place(me, move)
        other = theirs[i // 4].at[pl.ds(i % 4 * n, n), :]
        for j, (x, half) in enumerate(((block.at[pl.ds(0, n), :], core), (other, 1 - core))):
            copies.append(pltpu.make_async_copy(x, all_hbm.at[rows_at(start + half, n), :], sem.at[2 * i + j]))
    copy_all(copies)


def key_value_kernel(ways, du_ref, k_ref, v_ref, gk_ref, gv_ref):
    du = dot(du_ref[...].astype(F32).T.astype(BF), order_in(ways, du_ref.shape[0]))
    gk_ref[...] = (du * v_ref[...].astype(F32)).astype(BF)
    gv_ref[...] = (du * k_ref[...].astype(F32)).astype(BF)


def final_kernel(keep_ref, far_ref, side_ref, gw_ref):
    gw_ref[...] = keep_ref[...] + (far_ref[...].astype(F32) + side_ref[...].astype(F32))


def staged(kernel, n_in, n_out, n_after, staged_in, staged_out):
    def run(*refs):
        ins, refs = list(refs[:n_in]), refs[n_in + n_after :]
        outs, refs = list(refs[:n_out]), refs[n_out:]
        extra = len(staged_in) + len(staged_out) + 2
        own, extra = refs[: len(refs) - extra], refs[len(refs) - extra :]
        buffers, (in_sem, out_sem) = extra[:-2], extra[-2:]
        loads, stores = [], []
        for j, i in enumerate(staged_in):
            loads.append(pltpu.make_async_copy(ins[i], buffers[j], in_sem.at[j]))
            ins[i] = buffers[j]
        for j, i in enumerate(staged_out):
            buffer = buffers[len(staged_in) + j]
            stores.append(pltpu.make_async_copy(buffer, outs[i], out_sem.at[j]))
            outs[i] = buffer
        copy_all(loads)
        kernel(*ins, *outs, *own)
        copy_all(stores)

    return run


def call(kernel, outs, ins, scratch=(), mib=16, flops=0, specs=None, after=(), staged_in=(), staged_out=(), aliases=None):
    total = sum(math.prod(o.shape) * o.dtype.itemsize for o in (*outs, *ins))
    if after or staged_in or staged_out:
        kernel = staged(kernel, len(ins), len(outs), len(after), staged_in, staged_out)
        buffers = [pltpu.VMEM(ins[i].shape, ins[i].dtype) for i in staged_in]
        buffers += [pltpu.VMEM(outs[i].shape, outs[i].dtype) for i in staged_out]
        sems = [pltpu.SemaphoreType.DMA((max(len(x), 1),)) for x in (staged_in, staged_out)]
        scratch = [*scratch, *buffers, *sems]
    in_specs, out_specs = specs or ([VMEM] * len(ins), [VMEM] * len(outs))
    in_specs = [ANY if i in staged_in else s for i, s in enumerate(in_specs)]
    out_specs = [ANY if i in staged_out else s for i, s in enumerate(out_specs)]
    return pl.pallas_call(
        kernel,
        out_shape=outs,
        in_specs=[*in_specs, *([ANY] * len(after))],
        out_specs=out_specs,
        scratch_shapes=scratch,
        input_output_aliases=aliases or {},
        compiler_params=params(mib),
        cost_estimate=pl.CostEstimate(flops=0, bytes_accessed=0, transcendentals=0),
    )(*ins, *after)


def shape(*dims, dtype=BF):
    return jax.ShapeDtypeStruct(dims, dtype)


def spread(values):
    return lax.all_to_all(values, "ctx", 0, 0, tiled=True)


def move_over(values, move):
    return lax.ppermute(values, "fsdp", [(i, place(i, move)) for i in range(8)])


RING_FROM = ((0, 0), (1, 0), (0, -1), (0, 1), (1, -1), (1, 1), (0, 2), (1, 2))


def ring_first(gated):
    return move_over(gated, (1, 0)), move_over(gated, (0, 1)), move_over(gated, (0, -1))


def ring_rest(gated, other, own_up, own_down):
    other_up, other_down = move_over(other, (0, 1)), move_over(other, (0, -1))
    own_far, other_far = move_over(own_up, (0, 1)), move_over(other_down, (0, -1))
    return gated, other, own_up, own_down, other_up, other_down, own_far, other_far


def dy_product(w_out, d_out, moves, mib=MOST, after=()):
    channels, depth = w_out.shape
    rows = d_out.shape[0]
    step = 512
    pieces = rows // step
    count = len(moves)
    n = channels // 8
    return call(
        functools.partial(dy_kernel, step, moves),
        [shape(2 * n, rows)] * (count // 2),
        [w_out, d_out],
        [
            pltpu.VMEM((count * n, depth), BF),
            pltpu.VMEM((rows, depth), BF),
            pltpu.VMEM((count * n, rows), BF),
            pltpu.SemaphoreType.DMA((count,)),
            pltpu.SemaphoreType.DMA((pieces,)),
            pltpu.SemaphoreType.DMA((count // 2 * pieces,)),
        ],
        mib=mib,
        flops=2 * count * n * depth * rows,
        specs=([ANY] * 2, [ANY] * (count // 2)),
        after=after,
    )


def weight_product(blocks, moves, d_out, d_other, scale, after, near=()):
    rows, columns = d_out.shape
    n = blocks[0].shape[0] // 2
    count = len(moves)
    all_rows = 8 * n
    outs = [shape(all_rows // 4, columns)] * 4 if near else [shape(all_rows, columns)]
    ins = [*blocks, d_out, d_other]
    return call(
        functools.partial(far_kernel if near else near_kernel, scale, moves),
        [*outs, shape(count * n, rows)],
        [*ins, *near],
        [pltpu.VMEM((all_rows, columns), BF), pltpu.SemaphoreType.DMA((5,))] if near else [],
        flops=4 * count * n * rows * columns,
        specs=([VMEM] * len(ins) + [ANY] * len(near), [ANY if near else VMEM] * len(outs) + [VMEM]),
        after=after,
    )


def on_device(query_in, key_in, value_in, filt, w_out, d_out):
    seq_rows, width = query_in.shape
    channels, columns = w_out.shape
    ways = lax.axis_size("ctx")
    group, half = width // ways, width // 2
    n = HALF * group
    *tables, last = host_tables(ways, group)
    slots = np.arange(ways * group).reshape(ways // 2, 2, 2, group // 2)
    pick = lambda rows: last.reshape(LANE_TILES, ways * group, -1)[:, rows.reshape(-1)].reshape(last.shape)
    last_z = pick(slots.transpose(0, 2, 1, 3))

    swap = lambda v: lax.ppermute(v, "ctx", [(i, i ^ 1) for i in range(ways)])
    rows_like, half_like = shape(width, seq_rows), shape(half, seq_rows)

    x_y, up_y, down_y = dy_product(w_out, d_out, DY_MOVES[2:])
    (own_y,) = dy_product(w_out, d_out, DY_MOVES[:2], mib=16, after=[x_y])
    keep_y, far_y, side_y = call(
        sum_kernel,
        [shape(width, seq_rows, dtype=F32), rows_like, rows_like],
        [own_y, move_over(x_y, (1, 0)), move_over(up_y, (0, 1)), move_over(down_y, (0, -1))],
    )
    (send,) = call(
        prep_kernel,
        [shape(ways * 2 * group, seq_rows)],
        [key_in, value_in, filt],
        mib=MOST,
        after=[x_y],
        staged_in=(0, 1, 2),
        staged_out=(0,),
    )
    arrived = spread(send)

    flops = 2 * 2 * n * (tables[0].shape[1] + 2 * FAC) * FAC
    conv, spectrum = call(
        conv_kernel,
        [rows_like, shape(2 * n, FAC)],
        [arrived, *tables, last_z],
        mib=20,
        flops=3 * flops,
        after=[far_y],
        staged_out=(0,),
    )
    dy = (keep_y, move_over(far_y, (0, 2)), move_over(side_y, (1, 0)))
    (send,) = call(
        functools.partial(dz_kernel, ways), [shape(2 * width, seq_rows)], [*dy, query_in, conv], staged_out=(0,)
    )
    q_mine, q_away = call(
        turn_query_kernel,
        [half_like, half_like],
        [query_in],
        [pltpu.VMEM((width, seq_rows), F32)],
        after=[send],
    )
    q_theirs = swap(q_away)
    send, d_late = lax.optimization_barrier((send, d_out))
    d_other = swap(d_late)
    arrived = spread(send)
    gated, z_away = call(
        functools.partial(gate_kernel, ways),
        [rows_like, half_like],
        [arrived, q_mine, q_theirs],
        after=[d_other],
    )
    z_theirs = swap(z_away)
    other, own_up, own_down = ring_first(gated)
    like = shape(seq_rows, width)
    (grad_query,) = call(
        functools.partial(query_kernel, ways),
        [like],
        [*dy, arrived, z_theirs],
        [pltpu.VMEM((width, seq_rows), F32)],
        staged_out=(0,),
    )
    (adjoint,) = call(
        adjoint_kernel, [rows_like], [arrived, spectrum, *tables, last], mib=20, flops=2 * flops, staged_out=(0,)
    )
    other, adjoint = lax.optimization_barrier((other, adjoint))
    blocks = ring_rest(gated, other, own_up, own_down)
    grad_u = spread(adjoint)
    grad_key, grad_value = call(
        functools.partial(key_value_kernel, ways),
        [like, like],
        [grad_u, key_in, value_in],
        mib=MOST,
        staged_in=(0, 1, 2),
        staged_out=(0, 1),
    )

    weight = functools.partial(weight_product, d_out=d_out, d_other=d_other, scale=1.0 / math.sqrt(seq_rows * ways))
    near, away = weight(blocks[:4], RING_FROM[:4], after=[])
    theirs_near = swap(away)
    own_w, x_w, up_w, down_w, away = weight(blocks[4:], RING_FROM[4:], after=[grad_u], near=(near,))
    over_x = lambda v: lax.ppermute(v, "ctx", [(i, i ^ 2) for i in range(ways)])
    along_y = lambda v, step: lax.ppermute(v, "ctx", [(i, (i + 4 * step) % ways) for i in range(ways)])
    part_rows = shape(channels // ways, columns)
    keep_w, far_w, side_w = call(
        sum_kernel,
        [shape(channels // ways, columns, dtype=F32), part_rows, part_rows],
        [own_w, over_x(x_w), along_y(up_w, 1), along_y(down_w, -1)],
    )
    far_w, side_w = along_y(far_w, 2), over_x(side_w)

    (gated_all,) = call(
        assemble_kernel,
        [shape(channels, seq_rows)],
        [*blocks, theirs_near, swap(away)],
        [pltpu.SemaphoreType.DMA((16,))],
        specs=([ANY] * 10, [ANY]),
    )
    layer_out = lax.dot_general(
        gated_all, w_out, (((0,), (0,)), ((), ())), preferred_element_type=F32
    ).astype(BF)

    (grad_weight,) = call(
        final_kernel,
        [shape(channels // ways, columns, dtype=F32)],
        [keep_w, far_w, side_w],
        after=[layer_out, grad_query, grad_key],
    )
    return (layer_out, grad_query, grad_key, grad_value, grad_weight)


def solution(mesh):
    both = P("ctx", "fsdp")
    return jax.shard_map(
        on_device,
        mesh=mesh,
        in_specs=(both, both, both, both, P(None, "fsdp"), both),
        out_specs=(both, both, both, both, both),
        check_vma=False,
    )
```

```python
import functools
import math
import typing

import jax
import jax.numpy as jnp
import numpy as np
from jax import lax
from jax.experimental import pallas as pl
from jax.experimental.pallas import tpu as pltpu
from jax.sharding import PartitionSpec as P

ROW = 1024
FAC = 256
QF = 128
HALF = QF // 2 + 1
LANE_TILES = ROW // FAC
BF = jnp.bfloat16
F32 = jnp.float32
MIB = 1 << 20
MOST = 56


def angles(rows, cols, modulus):
    product = (rows[:, None].astype(np.int64) * cols[None, :]) % modulus
    return (product.astype(np.float32) * np.float32(2.0 * math.pi / modulus)).astype(np.float64)


def host_tables(ways, group):
    k2, t1 = np.arange(HALF), np.arange(FAC)
    t2 = (np.arange(LANE_TILES)[:, None] + LANE_TILES * np.arange(ways)[None, :]).reshape(-1)
    eye = np.eye(group)
    a = angles(k2, t2, QF)
    steps = np.stack([np.cos(a), -np.sin(a)])
    first = np.einsum("rkt,cd->rkctd", steps, eye).reshape(2 * HALF * group, t2.size * group)
    weight = np.where((k2 == 0) | (k2 == QF // 2), 1.0, 2.0) / (QF * FAC)
    b = angles(t2, k2, QF)
    back = np.concatenate([np.cos(b) * weight, (-np.sin(b) * weight)[:, 1:-1]], axis=1)
    last = np.einsum("tk,cd->tckd", back, eye).reshape(t2.size * group, -1)
    s = angles(t1, t1, FAC)
    square = np.concatenate([np.cos(s), np.sin(s)])
    w = angles(k2, t1, QF * FAC)
    twiddle = np.concatenate([np.repeat(f(w), group, axis=0) for f in (np.cos, np.sin)]).astype(np.float32)
    as_bf = lambda v: np.asarray(v, np.float32).astype(BF)
    return as_bf(first), as_bf(square), twiddle, as_bf(last)


def params(mib):
    return pltpu.CompilerParams(vmem_limit_bytes=mib * MIB)


VMEM = pl.BlockSpec(memory_space=pltpu.VMEM)
ANY = pl.BlockSpec(memory_space=pl.ANY)
DY_MOVES = ((0, 0), (0, 2), (1, 0), (1, 2), (0, 1), (1, 1), (0, -1), (1, -1))
DU_FROM = ((0, 0), (1, 0), (0, -1), (0, 1), (0, 2), (1, 2), (1, -1), (1, 1))
SLOT = {move: i for i, (flip, step) in enumerate(DY_MOVES) for move in ((flip, step % 4),)}


def place(index, move):
    flip, step = move
    return ((index ^ 4) if flip else index) & 4 | ((index + step) & 3)


def dot(a, b):
    return jnp.dot(a, b, preferred_element_type=F32)


def my_core():
    return lax.axis_index("ctx") & 1


def rows_at(i, n):
    return pl.ds(pl.multiple_of(i * n, n), n)


def product_t(order, values):
    return lax.dot_general(order, values, (((1,), (1,)), ((), ())), preferred_element_type=F32)


def copy_all(copies):
    copies = list(copies)
    for copy in copies:
        copy.start()
    for copy in copies:
        copy.wait()


def iota(axis, n):
    return lax.broadcasted_iota(jnp.int32, (n, n), axis)


def order_in(ways, width):
    row, group = iota(0, width), width // ways
    r = group // 2
    channel = (row // r % 2) * (width // 2) + (row // group) * r + row % r
    return (channel == iota(1, width)).astype(F32).astype(BF)


def order_z(ways, width):
    row = lax.broadcasted_iota(jnp.int32, (width, 2 * width), 0)
    column = lax.broadcasted_iota(jnp.int32, (width, 2 * width), 1)
    r = width // ways // 2
    core = (row // (width // 2)) ^ my_core()
    slot = (row % (width // 2) // r) * 4 * r + core * r + row % r
    return (slot == column).astype(F32).astype(BF)


def dy_kernel(step, moves, w_hbm, d_hbm, *refs):
    outs, (w_ref, d_ref, p_ref, w_sem, d_sem, o_sem) = refs[:-6], refs[-6:]
    me = lax.axis_index("fsdp")
    n = outs[0].shape[0] // 2
    gather = [
        pltpu.make_async_copy(w_hbm.at[rows_at(place(me, move), n), :], w_ref.at[pl.ds(i * n, n), :], w_sem.at[i])
        for i, move in enumerate(moves)
    ]
    pieces = [pl.ds(i * step, step) for i in range(d_ref.shape[0] // step)]
    loads = [
        pltpu.make_async_copy(d_hbm.at[rows, :], d_ref.at[rows, :], d_sem.at[i]) for i, rows in enumerate(pieces)
    ]
    for copy in (*gather, loads[0]):
        copy.start()
    for copy in gather:
        copy.wait()
    stores = []
    for i, rows in enumerate(pieces):
        loads[i].wait()
        if i + 1 < len(pieces):
            loads[i + 1].start()
        p_ref[:, rows] = product_t(w_ref[...], d_ref[rows, :]).astype(BF)
        for j, out in enumerate(outs):
            store = pltpu.make_async_copy(
                p_ref.at[pl.ds(2 * n * j, 2 * n), rows], out.at[:, rows], o_sem.at[i * len(outs) + j]
            )
            store.start()
            stores.append(store)
    for store in stores:
        store.wait()


def prep_kernel(k_ref, v_ref, f_ref, send_ref):
    width = k_ref.shape[1]
    ways = send_ref.shape[0] // (2 * 8)
    order = order_in(ways, width)
    mixed = (k_ref[...].astype(F32) * v_ref[...].astype(F32)).astype(BF)
    parts = [product_t(order, x).reshape(ways, 1, -1, ROW) for x in (mixed, f_ref[...])]
    send_ref[...] = jnp.concatenate(parts, axis=1).reshape(send_ref.shape).astype(BF)


def turn_query_kernel(q_ref, mine_ref, away_ref, qt_ref):
    qt_ref[...] = q_ref[...].astype(F32).T
    core, n = my_core(), mine_ref.shape[0]
    mine_ref[...] = qt_ref[rows_at(core, n), :].astype(BF)
    away_ref[...] = qt_ref[rows_at(1 - core, n), :].astype(BF)


def gate_kernel(ways, z_ref, q_mine_ref, q_theirs_ref, gated_ref, z_away_ref):
    z = dot(order_z(ways, gated_ref.shape[0]), z_ref[...])
    n = z.shape[0] // 2
    z_away_ref[...] = z[n:].astype(BF)
    gated_ref[pl.ds(0, n), :] = (z[:n] * q_mine_ref[...].astype(F32)).astype(BF)
    gated_ref[pl.ds(n, n), :] = (z[n:] * q_theirs_ref[...].astype(F32)).astype(BF)


def sum_kernel(own_ref, x_ref, up_ref, down_ref, keep_ref, far_ref, side_ref):
    n = keep_ref.shape[0]
    near, second = pl.ds(0, n), pl.ds(n, n)
    own = own_ref[near, :].astype(F32) + x_ref[near, :].astype(F32)
    keep_ref[...] = own + (up_ref[near, :].astype(F32) + down_ref[near, :].astype(F32))
    far_ref[...] = (own_ref[second, :].astype(F32) + x_ref[second, :].astype(F32)).astype(BF)
    side_ref[...] = (up_ref[second, :].astype(F32) + down_ref[second, :].astype(F32)).astype(BF)


def dz_kernel(ways, keep_ref, far_ref, side_ref, q_ref, z_ref, send_ref):
    dy = keep_ref[...] + (far_ref[...].astype(F32) + side_ref[...].astype(F32))
    dz = (dy * q_ref[...].astype(F32).T).astype(BF)
    pieces = (z_ref[...].astype(F32), dot(order_in(ways, dz.shape[0]), dz))
    both = jnp.concatenate([x.reshape(ways, 1, -1, ROW) for x in pieces], axis=1)
    send_ref[...] = both.reshape(send_ref.shape).astype(BF)


def query_kernel(ways, keep_ref, far_ref, side_ref, z_ref, z_theirs_ref, gq_ref, gq_t_ref):
    gq_t_ref[...] = keep_ref[...] + (far_ref[...].astype(F32) + side_ref[...].astype(F32))
    core, n = my_core(), z_theirs_ref.shape[0]
    z_mine = dot(order_z(ways, gq_t_ref.shape[0])[:n], z_ref[...]).astype(BF)
    for z, half in ((z_mine, core), (z_theirs_ref[...], 1 - core)):
        own = rows_at(half, n)
        gq_t_ref[own, :] *= z.astype(F32)
    gq_ref[...] = gq_t_ref[...].T.astype(BF)


class Tables(typing.NamedTuple):
    first: typing.Any
    square: typing.Any
    twiddle: typing.Any
    last: typing.Any


def times_square(left, right, tables):
    square = tables.square
    return dot(left, square[:FAC]) + dot(right, square[FAC:])


def transform(x, tables):
    x = jnp.concatenate([x[:, u * FAC : (u + 1) * FAC] for u in range(LANE_TILES)], axis=0)
    section = dot(tables.first[...], x)
    n = section.shape[0] // 2
    twiddle = tables.twiddle
    re, im, tc, ts = section[:n], section[n:], twiddle[:n], twiddle[n:]
    b_re, b_im = re * tc + im * ts, im * tc - re * ts
    left = jnp.concatenate([b_re, b_im], axis=0).astype(BF)
    right = jnp.concatenate([b_im, -b_re], axis=0).astype(BF)
    f = times_square(left, right, tables)
    return f[:n], f[n:]


def signal(p_re, p_im, tables):
    n, group = p_re.shape[0], p_re.shape[0] // HALF
    left = jnp.concatenate([p_re, p_im], axis=0).astype(BF)
    right = jnp.concatenate([-p_im, p_re], axis=0).astype(BF)
    c = times_square(left, right, tables)
    twiddle = tables.twiddle
    re, im, tc, ts = c[:n], c[n:], twiddle[:n], twiddle[n:]
    e_re, e_im = re * tc - im * ts, im * tc + re * ts
    e = jnp.concatenate([e_re, e_im[group : n - group]], axis=0).astype(BF)
    x = dot(tables.last[...], e)
    rows = x.shape[0] // LANE_TILES
    return jnp.concatenate([x[u * rows : (u + 1) * rows] for u in range(LANE_TILES)], axis=1)


def conv_kernel(r_ref, first_ref, square_ref, twiddle_ref, last_ref, z_ref, h_ref):
    tables = Tables(first_ref, square_ref, twiddle_ref, last_ref)
    rows = z_ref.shape[0]
    group = h_ref.shape[0] // (2 * HALF)
    r = r_ref[...].astype(F32).reshape(-1, 2, group, ROW)
    u, h = (transform(r[:, s].reshape(rows, ROW).astype(BF), tables) for s in range(2))
    h_ref[...] = jnp.concatenate(h, axis=0).astype(BF)
    p_re, p_im = u[0] * h[0] - u[1] * h[1], u[0] * h[1] + u[1] * h[0]
    z_ref[...] = signal(p_re, p_im, tables).astype(BF)


def adjoint_kernel(r_ref, h_ref, first_ref, square_ref, twiddle_ref, last_ref, away_ref, keep_ref):
    tables = Tables(first_ref, square_ref, twiddle_ref, last_ref)
    rows = 2 * keep_ref.shape[0]
    group = h_ref.shape[0] // (2 * HALF)
    r = r_ref[...].astype(F32).reshape(-1, 2, group, ROW)[:, 1]
    g_re, g_im = transform(r.reshape(rows, ROW).astype(BF), tables)
    h = h_ref[...].astype(F32)
    n = h.shape[0] // 2
    h_re, h_im = h[:n], h[n:]
    q_re, q_im = h_re * g_re + h_im * g_im, h_re * g_im - h_im * g_re
    du = signal(q_re, q_im, tables).reshape(-1, 2, group, ROW)
    low, high, first_core = du[:, 0], du[:, 1], my_core() == 0
    keep_ref[...] = jnp.where(first_core, low, high).reshape(keep_ref.shape).astype(BF)
    away_ref[...] = jnp.where(first_core, high, low).reshape(keep_ref.shape).astype(BF)


def slot_of(to):
    ctx = lax.axis_index("ctx")
    flip, step = (to ^ (ctx // 2)) & 1, (to // 2 - ctx // 4) & 3
    slot = jnp.int32(0)
    for (f, d), at in SLOT.items():
        slot = jnp.where((flip == f) & (step == d), at, slot)
    return slot


def weight_rows(scale, moves, blocks, d_ref, d_other_ref, away_ref, part_ref, loaded=()):
    me = lax.axis_index("fsdp")
    n = blocks[0].shape[0] // 2
    slot_rows = part_ref.shape[0] // 8
    mine = jnp.concatenate([block[:n] for block in blocks], axis=0)
    away = jnp.concatenate([block[n:] for block in blocks], axis=0)
    away_ref[...] = away
    p = dot(mine, d_ref[...]) + dot(away, d_other_ref[...])
    p = (p * scale).astype(BF)
    for load in loaded:
        load.wait()
    for i, move in enumerate(moves):
        start = pl.multiple_of(slot_of(place(me, move)) * slot_rows, 16)
        part_ref[pl.ds(start, n), :] = p[i * n : (i + 1) * n]


def near_kernel(scale, moves, *refs):
    count = len(moves)
    blocks, (d_ref, d_other_ref, part_ref, away_ref) = refs[:count], refs[count:]
    weight_rows(scale, moves, blocks, d_ref, d_other_ref, away_ref, part_ref)


def far_kernel(scale, moves, *refs):
    count = len(moves)
    blocks, (d_ref, d_other_ref, keep_ref, got_ref, near_hbm), refs = refs[:count], refs[count : count + 5], refs[count + 5 :]
    outs, away_ref, (part_ref, sem) = refs[:4], refs[4], refs[5:]
    near = pltpu.make_async_copy(near_hbm, part_ref, sem.at[4])
    near.start()
    weight_rows(scale, moves, blocks, d_ref, d_other_ref, away_ref, part_ref, [near])
    slot_rows = part_ref.shape[0] // 8
    group = keep_ref.shape[0] // 8
    keep, got = keep_ref[...].astype(F32), got_ref[...].astype(F32)
    for j in range(8):
        rows = slice(j * group, (j + 1) * group)
        start = pl.multiple_of((slot_of(jnp.int32(j)) + 1) * slot_rows - 2 * group, 16)
        part_ref[pl.ds(start, 2 * group), :] = jnp.concatenate([keep[rows], got[rows]], axis=0).astype(BF)
    n = outs[0].shape[0]
    copy_all(pltpu.make_async_copy(part_ref.at[pl.ds(i * n, n), :], out, sem.at[i]) for i, out in enumerate(outs))


def part_sum_kernel(own_ref, x_ref, up_ref, down_ref, keep_ref, far_ref, side_ref, du_ref):
    n = keep_ref.shape[0]
    own, x, up, down = (ref[...].astype(F32) for ref in (own_ref, x_ref, up_ref, down_ref))
    m = own.shape[0] // 2
    keep_ref[...] = own[:n] + x[:n] + (up[:n] + down[:n])
    for out_ref, a, b in ((far_ref, own, x), (side_ref, up, down)):
        out_ref[...] = jnp.concatenate([a[m : m + n] + b[m : m + n], a[m + n :], b[m + n :]], axis=0).astype(BF)
    du_ref[...] = jnp.concatenate([v[n:m] for v in (own, x, up, down)], axis=0).astype(BF)


def assemble_kernel(*refs):
    blocks, theirs, (all_hbm, sem) = refs[:8], refs[8:10], refs[10:]
    me, core = lax.axis_index("fsdp"), my_core()
    n = blocks[0].shape[0] // 2
    copies = []
    for i, (block, move) in enumerate(zip(blocks, RING_FROM)):
        start = 2 * place(me, move)
        other = theirs[i // 4].at[pl.ds(i % 4 * n, n), :]
        for j, (x, half) in enumerate(((block.at[pl.ds(0, n), :], core), (other, 1 - core))):
            copies.append(pltpu.make_async_copy(x, all_hbm.at[rows_at(start + half, n), :], sem.at[2 * i + j]))
    copy_all(copies)


def final_kernel(keep_ref, far_ref, side_ref, du_ref, k_ref, v_ref, gw_ref, gk_ref, gv_ref, du_t_ref):
    n = gw_ref.shape[0]
    far, side, du = far_ref[...].astype(F32), side_ref[...].astype(F32), du_ref[...].astype(F32)
    gw_ref[...] = keep_ref[...] + (far[:n] + side[:n])
    ctx, core = lax.axis_index("ctx"), my_core()
    width = du_t_ref.shape[0]
    group = width // 16
    pieces = [du[i * 2 * group : (i + 1) * 2 * group] for i in range(4)]
    pieces += [v[n + i * 2 * group : n + (i + 1) * 2 * group] for v in (far, side) for i in range(2)]
    for piece, (flip, step) in zip(pieces, DU_FROM):
        chip = ((ctx // 4 + step) & 3) * 2 + ((ctx // 2) & 1 ^ flip)
        for rows, side_core in ((piece[:group], core), (piece[group:], 1 - core)):
            du_t_ref[rows_at(2 * chip + side_core, group), :] = rows
    du = dot(du_t_ref[...].T.astype(BF), order_in(16, width))
    gk_ref[...] = (du * v_ref[...].astype(F32)).astype(BF)
    gv_ref[...] = (du * k_ref[...].astype(F32)).astype(BF)


def staged(kernel, n_in, n_out, n_after, staged_in, staged_out):
    def run(*refs):
        ins, refs = list(refs[:n_in]), refs[n_in + n_after :]
        outs, refs = list(refs[:n_out]), refs[n_out:]
        extra = len(staged_in) + len(staged_out) + 2
        own, extra = refs[: len(refs) - extra], refs[len(refs) - extra :]
        buffers, (in_sem, out_sem) = extra[:-2], extra[-2:]
        loads, stores = [], []
        for j, i in enumerate(staged_in):
            loads.append(pltpu.make_async_copy(ins[i], buffers[j], in_sem.at[j]))
            ins[i] = buffers[j]
        for j, i in enumerate(staged_out):
            buffer = buffers[len(staged_in) + j]
            stores.append(pltpu.make_async_copy(buffer, outs[i], out_sem.at[j]))
            outs[i] = buffer
        copy_all(loads)
        kernel(*ins, *outs, *own)
        copy_all(stores)

    return run


def call(kernel, outs, ins, scratch=(), mib=16, flops=0, specs=None, after=(), staged_in=(), staged_out=(), aliases=None):
    total = sum(math.prod(o.shape) * o.dtype.itemsize for o in (*outs, *ins))
    if after or staged_in or staged_out:
        kernel = staged(kernel, len(ins), len(outs), len(after), staged_in, staged_out)
        buffers = [pltpu.VMEM(ins[i].shape, ins[i].dtype) for i in staged_in]
        buffers += [pltpu.VMEM(outs[i].shape, outs[i].dtype) for i in staged_out]
        sems = [pltpu.SemaphoreType.DMA((max(len(x), 1),)) for x in (staged_in, staged_out)]
        scratch = [*scratch, *buffers, *sems]
    in_specs, out_specs = specs or ([VMEM] * len(ins), [VMEM] * len(outs))
    in_specs = [ANY if i in staged_in else s for i, s in enumerate(in_specs)]
    out_specs = [ANY if i in staged_out else s for i, s in enumerate(out_specs)]
    return pl.pallas_call(
        kernel,
        out_shape=outs,
        in_specs=[*in_specs, *([ANY] * len(after))],
        out_specs=out_specs,
        scratch_shapes=scratch,
        input_output_aliases=aliases or {},
        compiler_params=params(mib),
        cost_estimate=pl.CostEstimate(flops=0, bytes_accessed=0, transcendentals=0),
    )(*ins, *after)


def shape(*dims, dtype=BF):
    return jax.ShapeDtypeStruct(dims, dtype)


def spread(values):
    return lax.all_to_all(values, "ctx", 0, 0, tiled=True)


def move_over(values, move):
    return lax.ppermute(values, "fsdp", [(i, place(i, move)) for i in range(8)])


RING_FROM = ((0, 0), (1, 0), (0, -1), (0, 1), (1, -1), (1, 1), (0, 2), (1, 2))


def dy_product(w_out, d_out, moves, mib=MOST, after=()):
    channels, depth = w_out.shape
    rows = d_out.shape[0]
    step = 512
    pieces = rows // step
    count = len(moves)
    n = channels // 8
    return call(
        functools.partial(dy_kernel, step, moves),
        [shape(2 * n, rows)] * (count // 2),
        [w_out, d_out],
        [
            pltpu.VMEM((count * n, depth), BF),
            pltpu.VMEM((rows, depth), BF),
            pltpu.VMEM((count * n, rows), BF),
            pltpu.SemaphoreType.DMA((count,)),
            pltpu.SemaphoreType.DMA((pieces,)),
            pltpu.SemaphoreType.DMA((count // 2 * pieces,)),
        ],
        mib=mib,
        flops=2 * count * n * depth * rows,
        specs=([ANY] * 2, [ANY] * (count // 2)),
        after=after,
    )


def weight_product(blocks, moves, d_out, d_other, scale, slot_rows, after=(), du=(), near=()):
    rows, columns = d_out.shape
    n = blocks[0].shape[0] // 2
    count = len(moves)
    all_rows = 8 * slot_rows
    outs = [shape(all_rows // 4, columns)] * 4 if near else [shape(all_rows, columns)]
    ins = [*blocks, d_out, d_other, *du]
    return call(
        functools.partial(far_kernel if near else near_kernel, scale, moves),
        [*outs, shape(count * n, rows)],
        [*ins, *near],
        [pltpu.VMEM((all_rows, columns), BF), pltpu.SemaphoreType.DMA((5,))] if near else [],
        flops=4 * count * n * rows * columns,
        specs=([VMEM] * len(ins) + [ANY] * len(near), [ANY if near else VMEM] * len(outs) + [VMEM]),
        after=after,
    )


def on_device(query_in, key_in, value_in, filt, w_out, d_out):
    seq_rows, width = query_in.shape
    channels, columns = w_out.shape
    ways = lax.axis_size("ctx")
    group, half = width // ways, width // 2
    n = HALF * group
    *tables, last = host_tables(ways, group)
    slots = np.arange(ways * group).reshape(ways // 2, 2, 2, group // 2)
    pick = lambda rows: last.reshape(LANE_TILES, ways * group, -1)[:, rows.reshape(-1)].reshape(last.shape)
    last_z = pick(slots.transpose(0, 2, 1, 3))

    swap = lambda v: lax.ppermute(v, "ctx", [(i, i ^ 1) for i in range(ways)])
    rows_like, half_like = shape(width, seq_rows), shape(half, seq_rows)

    x_y, up_y, down_y = dy_product(w_out, d_out, DY_MOVES[2:])
    (own_y,) = dy_product(w_out, d_out, DY_MOVES[:2], mib=16, after=[x_y])
    keep_y, far_y, side_y = call(
        sum_kernel,
        [shape(width, seq_rows, dtype=F32), rows_like, rows_like],
        [own_y, move_over(x_y, (1, 0)), move_over(up_y, (0, 1)), move_over(down_y, (0, -1))],
    )
    (send,) = call(
        prep_kernel,
        [shape(ways * 2 * group, seq_rows)],
        [key_in, value_in, filt],
        mib=MOST,
        after=[x_y],
        staged_in=(0, 1, 2),
        staged_out=(0,),
    )
    arrived = spread(send)

    flops = 2 * 2 * n * (tables[0].shape[1] + 2 * FAC) * FAC
    conv, spectrum = call(
        conv_kernel,
        [rows_like, shape(2 * n, FAC)],
        [arrived, *tables, last_z],
        mib=20,
        flops=3 * flops,
        after=[far_y],
        staged_out=(0,),
    )
    dy = (keep_y, move_over(far_y, (0, 2)), move_over(side_y, (1, 0)))
    (send,) = call(
        functools.partial(dz_kernel, ways), [shape(2 * width, seq_rows)], [*dy, query_in, conv], staged_out=(0,)
    )
    q_mine, q_away = call(
        turn_query_kernel,
        [half_like, half_like],
        [query_in],
        [pltpu.VMEM((width, seq_rows), F32)],
        after=[send],
    )
    q_theirs = swap(q_away)
    send, d_late = lax.optimization_barrier((send, d_out))
    d_other = swap(d_late)
    arrived = spread(send)
    gated, z_away = call(
        functools.partial(gate_kernel, ways),
        [rows_like, half_like],
        [arrived, q_mine, q_theirs],
        after=[d_other],
    )
    z_theirs = swap(z_away)
    own_far, other = move_over(gated, (0, 2)), move_over(gated, (1, 0))
    own_up, own_down = move_over(gated, (0, 1)), move_over(gated, (0, -1))
    like = shape(seq_rows, width)
    (grad_query,) = call(
        functools.partial(query_kernel, ways),
        [like],
        [*dy, arrived, z_theirs],
        [pltpu.VMEM((width, seq_rows), F32)],
        staged_out=(0,),
    )
    du_away, du_keep = call(
        adjoint_kernel, [half_like, half_like], [arrived, spectrum, *tables, last], mib=20, flops=2 * flops
    )
    other, own_up, own_down, du_away = lax.optimization_barrier((other, own_up, own_down, du_away))
    du_got = swap(du_away)
    other_up, other_down = move_over(other, (0, 1)), move_over(other, (0, -1))
    other_far = move_over(own_far, (1, 0))
    blocks = gated, other, own_up, own_down, other_up, other_down, own_far, other_far

    slot_rows = half + 2 * group
    scale = 1.0 / math.sqrt(seq_rows * ways)
    weight = functools.partial(weight_product, d_out=d_out, d_other=d_other, scale=scale, slot_rows=slot_rows)
    near, away = weight(blocks[:4], RING_FROM[:4])
    theirs_near = swap(away)
    own_w, x_w, up_w, down_w, away = weight(blocks[4:], RING_FROM[4:], du=(du_keep, du_got), near=(near,))
    over_x = lambda v: lax.ppermute(v, "ctx", [(i, i ^ 2) for i in range(ways)])
    along_y = lambda v, step: lax.ppermute(v, "ctx", [(i, (i + 4 * step) % ways) for i in range(ways)])
    part_like = shape(channels // ways, columns, dtype=F32)
    onward = shape(half + 4 * group, columns)
    keep_w, far_w, side_w, du_near = call(
        part_sum_kernel,
        [part_like, onward, onward, half_like],
        [own_w, over_x(x_w), along_y(up_w, 1), along_y(down_w, -1)],
    )
    far_w, side_w = along_y(far_w, 2), over_x(side_w)

    (gated_all,) = call(
        assemble_kernel,
        [shape(channels, seq_rows)],
        [*blocks, theirs_near, swap(away)],
        [pltpu.SemaphoreType.DMA((16,))],
        specs=([ANY] * 10, [ANY]),
    )
    layer_out = lax.dot_general(
        gated_all, w_out, (((0,), (0,)), ((), ())), preferred_element_type=F32
    ).astype(BF)

    grad_weight, grad_key, grad_value = call(
        final_kernel,
        [part_like, like, like],
        [keep_w, far_w, side_w, du_near, key_in, value_in],
        [pltpu.VMEM((width, columns), F32)],
        after=[layer_out, grad_query],
        staged_out=(0, 1, 2),
    )
    return (layer_out, grad_query, grad_key, grad_value, grad_weight)


def solution(mesh):
    both = P("ctx", "fsdp")
    return jax.shard_map(
        on_device,
        mesh=mesh,
        in_specs=(both, both, both, both, P(None, "fsdp"), both),
        out_specs=(both, both, both, both, both),
        check_vma=False,
    )
```

```python
import functools
import math

import jax
import jax.numpy as jnp
import numpy as np
from jax import lax
from jax.experimental import pallas as pl
from jax.experimental.pallas import tpu as pltpu
from jax.sharding import PartitionSpec as P

ROW = 1024
FAC = 256
QF = 128
HALF = QF // 2 + 1
LANE_TILES = ROW // FAC
BF = jnp.bfloat16
F32 = jnp.float32
MIB = 1 << 20
MOST = 56


def angles(rows, cols, modulus):
    product = (rows[:, None].astype(np.int64) * cols[None, :]) % modulus
    return (product.astype(np.float32) * np.float32(2.0 * math.pi / modulus)).astype(np.float64)


def host_tables(ways, group):
    k2, t1 = np.arange(HALF), np.arange(FAC)
    t2 = (np.arange(LANE_TILES)[:, None] + LANE_TILES * np.arange(ways)[None, :]).reshape(-1)
    a = angles(k2, t2, QF)
    steps = np.stack([np.cos(a), -np.sin(a)])
    first = np.einsum("rkt,cd->rkctd", steps, np.eye(group)).reshape(2 * HALF * group, t2.size * group)
    s = angles(t1, t1, FAC)
    square = np.concatenate([np.cos(s), np.sin(s)])
    w = angles(k2, t1, QF * FAC)
    twiddle = np.concatenate([np.cos(w), np.sin(w)]).astype(np.float32)
    as_bf = lambda v: np.asarray(v, np.float32).astype(BF)
    return as_bf(first), as_bf(square), twiddle


def params(mib):
    return pltpu.CompilerParams(vmem_limit_bytes=mib * MIB)


VMEM = pl.BlockSpec(memory_space=pltpu.VMEM)
ANY = pl.BlockSpec(memory_space=pl.ANY)
DY_MOVES = ((0, 0), (0, 2), (1, 0), (1, 2), (0, 1), (1, 1), (0, -1), (1, -1))
DU_FROM = ((0, 0), (1, 0), (0, -1), (0, 1), (0, 2), (1, 2), (1, -1), (1, 1))
SLOT = {move: i for i, (flip, step) in enumerate(DY_MOVES) for move in ((flip, step % 4),)}


def place(index, move):
    flip, step = move
    return ((index ^ 4) if flip else index) & 4 | ((index + step) & 3)


def dot(a, b):
    return jnp.dot(a, b, preferred_element_type=F32)


def my_core():
    return lax.axis_index("ctx") & 1


def rows_at(i, n):
    return pl.ds(pl.multiple_of(i * n, n), n)


def product_t(order, values):
    return lax.dot_general(order, values, (((1,), (1,)), ((), ())), preferred_element_type=F32)


def copy_all(copies):
    copies = list(copies)
    for copy in copies:
        copy.start()
    for copy in copies:
        copy.wait()


def iota(axis, n):
    return lax.broadcasted_iota(jnp.int32, (n, n), axis)


def order_in(ways, width):
    row, group = iota(0, width), width // ways
    r = group // 2
    channel = (row // r % 2) * (width // 2) + (row // group) * r + row % r
    return (channel == iota(1, width)).astype(F32).astype(BF)


def order_z(ways, width):
    row = lax.broadcasted_iota(jnp.int32, (width, 2 * width), 0)
    column = lax.broadcasted_iota(jnp.int32, (width, 2 * width), 1)
    r = width // ways // 2
    core = (row // (width // 2)) ^ my_core()
    slot = (row % (width // 2) // r) * 4 * r + core * r + row % r
    return (slot == column).astype(F32).astype(BF)


def dy_kernel(step, moves, between, w_hbm, d_hbm, *refs):
    outs, (w_ref, d_ref, p_ref, w_sem, d_sem, o_sem) = refs[:-6], refs[-6:]
    me = lax.axis_index("fsdp")
    n = outs[0].shape[0] // 2
    gather = [
        pltpu.make_async_copy(w_hbm.at[rows_at(place(me, move), n), :], w_ref.at[pl.ds(i * n, n), :], w_sem.at[i])
        for i, move in enumerate(moves)
    ]
    pieces = [pl.ds(i * step, step) for i in range(d_ref.shape[0] // step)]
    loads = [
        pltpu.make_async_copy(d_hbm.at[rows, :], d_ref.at[rows, :], d_sem.at[i]) for i, rows in enumerate(pieces)
    ]
    other_loads, other_work, other_stores = between or ((), None, ())
    for copy in (*gather, loads[0], *other_loads):
        copy.start()
    for copy in gather:
        copy.wait()
    stores = []
    for i, rows in enumerate(pieces):
        loads[i].wait()
        if i + 1 < len(pieces):
            loads[i + 1].start()
        p_ref[:, rows] = product_t(w_ref[...], d_ref[rows, :]).astype(BF)
        for j, out in enumerate(outs):
            store = pltpu.make_async_copy(
                p_ref.at[pl.ds(2 * n * j, 2 * n), rows], out.at[:, rows], o_sem.at[i * len(outs) + j]
            )
            store.start()
            stores.append(store)
        if i == 0 and other_work:
            for copy in other_loads:
                copy.wait()
            other_work()
            for copy in other_stores:
                copy.start()
                stores.append(copy)
    for store in stores:
        store.wait()


def open_kernel(step, moves, w_hbm, d_hbm, k_hbm, v_hbm, f_hbm, *refs):
    count = len(moves) // 2
    outs, send_hbm, (k_ref, v_ref, f_ref, send_ref, sem), refs = refs[:count], refs[count], refs[-5:], refs[count + 1 : -5]
    froms = zip((k_hbm, v_hbm, f_hbm), (k_ref, v_ref, f_ref))
    loads = [pltpu.make_async_copy(x, to, sem.at[i]) for i, (x, to) in enumerate(froms)]

    def mix():
        width = k_ref.shape[1]
        ways = send_ref.shape[0] // (2 * 8)
        order = order_in(ways, width)
        mixed = (k_ref[...].astype(F32) * v_ref[...].astype(F32)).astype(BF)
        parts = [product_t(order, x).reshape(ways, 1, -1, ROW) for x in (mixed, f_ref[...])]
        send_ref[...] = jnp.concatenate(parts, axis=1).reshape(send_ref.shape).astype(BF)

    between = (loads, mix, [pltpu.make_async_copy(send_ref, send_hbm, sem.at[3])])
    dy_kernel(step, moves, between, w_hbm, d_hbm, *outs, *refs)


def turn_query_kernel(q_ref, mine_ref, away_ref, qt_ref):
    qt_ref[...] = q_ref[...].astype(F32).T
    core, n = my_core(), mine_ref.shape[0]
    mine_ref[...] = qt_ref[rows_at(core, n), :].astype(BF)
    away_ref[...] = qt_ref[rows_at(1 - core, n), :].astype(BF)


def gate_kernel(ways, z_ref, q_mine_ref, q_theirs_ref, gated_ref, z_away_ref):
    z = dot(order_z(ways, gated_ref.shape[0]), z_ref[...])
    n = z.shape[0] // 2
    z_away_ref[...] = z[n:].astype(BF)
    gated_ref[pl.ds(0, n), :] = (z[:n] * q_mine_ref[...].astype(F32)).astype(BF)
    gated_ref[pl.ds(n, n), :] = (z[n:] * q_theirs_ref[...].astype(F32)).astype(BF)


def sum_kernel(own_ref, x_ref, up_ref, down_ref, keep_ref, far_ref, side_ref):
    n = keep_ref.shape[0]
    near, second = pl.ds(0, n), pl.ds(n, n)
    own = own_ref[near, :].astype(F32) + x_ref[near, :].astype(F32)
    keep_ref[...] = own + (up_ref[near, :].astype(F32) + down_ref[near, :].astype(F32))
    far_ref[...] = (own_ref[second, :].astype(F32) + x_ref[second, :].astype(F32)).astype(BF)
    side_ref[...] = (up_ref[second, :].astype(F32) + down_ref[second, :].astype(F32)).astype(BF)


def dz_kernel(ways, keep_ref, far_ref, side_ref, q_ref, z_ref, send_ref):
    dy = keep_ref[...] + (far_ref[...].astype(F32) + side_ref[...].astype(F32))
    dz = (dy * q_ref[...].astype(F32).T).astype(BF)
    pieces = (z_ref[...].astype(F32), dot(order_in(ways, dz.shape[0]), dz))
    both = jnp.concatenate([x.reshape(ways, 1, -1, ROW) for x in pieces], axis=1)
    send_ref[...] = both.reshape(send_ref.shape).astype(BF)


def query_kernel(ways, keep_ref, far_ref, side_ref, z_ref, z_theirs_ref, gq_ref, gq_t_ref):
    gq_t_ref[...] = keep_ref[...] + (far_ref[...].astype(F32) + side_ref[...].astype(F32))
    core, n = my_core(), z_theirs_ref.shape[0]
    z_mine = dot(order_z(ways, gq_t_ref.shape[0])[:n], z_ref[...]).astype(BF)
    for z, half in ((z_mine, core), (z_theirs_ref[...], 1 - core)):
        own = rows_at(half, n)
        gq_t_ref[own, :] *= z.astype(F32)
    gq_ref[...] = gq_t_ref[...].T.astype(BF)


class Tables:
    def __init__(self, first, square, twiddle):
        self.first, self.square = first, square
        self.group = first.shape[0] // twiddle.shape[0]
        rows = [jnp.broadcast_to(twiddle[i : i + 1, :], (self.group, FAC)) for i in range(twiddle.shape[0])]
        self.twiddle = jnp.concatenate(rows, axis=0)


def times_square(left, right, tables):
    square = tables.square
    return dot(left, square[:FAC]) + dot(right, square[FAC:])


def transform(x, tables):
    x = jnp.concatenate([x[:, u * FAC : (u + 1) * FAC] for u in range(LANE_TILES)], axis=0)
    section = dot(tables.first[...], x)
    n = section.shape[0] // 2
    twiddle = tables.twiddle
    re, im, tc, ts = section[:n], section[n:], twiddle[:n], twiddle[n:]
    b_re, b_im = re * tc + im * ts, im * tc - re * ts
    left = jnp.concatenate([b_re, b_im], axis=0).astype(BF)
    right = jnp.concatenate([b_im, -b_re], axis=0).astype(BF)
    f = times_square(left, right, tables)
    return f[:n], f[n:]


def signal(p_re, p_im, tables):
    n, group = p_re.shape[0], tables.group
    left = jnp.concatenate([p_re, p_im], axis=0).astype(BF)
    right = jnp.concatenate([-p_im, p_re], axis=0).astype(BF)
    c = times_square(left, right, tables)
    re, im, tc, ts = c[:n], c[n:], tables.twiddle[:n], tables.twiddle[n:]
    row = lax.broadcasted_iota(jnp.int32, re.shape, 0)
    weight = jnp.where((row < group) | (row >= n - group), 1.0 / (QF * FAC), 2.0 / (QF * FAC))
    e = jnp.concatenate([(re * tc - im * ts) * weight, (im * tc + re * ts) * weight], axis=0).astype(BF)
    x = lax.dot_general(tables.first[...], e, (((0,), (0,)), ((), ())), preferred_element_type=F32)
    rows = x.shape[0] // LANE_TILES
    return jnp.concatenate([x[u * rows : (u + 1) * rows] for u in range(LANE_TILES)], axis=1)


def conv_kernel(r_ref, first_ref, square_ref, twiddle_ref, z_ref, h_ref):
    tables = Tables(first_ref, square_ref, twiddle_ref)
    rows = z_ref.shape[0]
    group = h_ref.shape[0] // (2 * HALF)
    r = r_ref[...].astype(F32).reshape(-1, 2, group, ROW)
    u, h = (transform(r[:, s].reshape(rows, ROW).astype(BF), tables) for s in range(2))
    h_ref[...] = jnp.concatenate(h, axis=0).astype(BF)
    p_re, p_im = u[0] * h[0] - u[1] * h[1], u[0] * h[1] + u[1] * h[0]
    z = signal(p_re, p_im, tables).astype(BF)
    row, r = iota(0, rows), group // 2
    source = row // (4 * r) * 4 * r + row // r % 2 * 2 * r + row // (2 * r) % 2 * r + row % r
    z_ref[...] = dot((source == iota(1, rows)).astype(F32).astype(BF), z).astype(BF)


def adjoint_kernel(r_ref, h_ref, first_ref, square_ref, twiddle_ref, away_ref, keep_ref):
    tables = Tables(first_ref, square_ref, twiddle_ref)
    rows = 2 * keep_ref.shape[0]
    group = h_ref.shape[0] // (2 * HALF)
    r = r_ref[...].astype(F32).reshape(-1, 2, group, ROW)[:, 1]
    g_re, g_im = transform(r.reshape(rows, ROW).astype(BF), tables)
    h = h_ref[...].astype(F32)
    n = h.shape[0] // 2
    h_re, h_im = h[:n], h[n:]
    q_re, q_im = h_re * g_re + h_im * g_im, h_re * g_im - h_im * g_re
    du = signal(q_re, q_im, tables).reshape(-1, 2, group, ROW)
    low, high, first_core = du[:, 0], du[:, 1], my_core() == 0
    keep_ref[...] = jnp.where(first_core, low, high).reshape(keep_ref.shape).astype(BF)
    away_ref[...] = jnp.where(first_core, high, low).reshape(keep_ref.shape).astype(BF)


def slot_of(to):
    ctx = lax.axis_index("ctx")
    flip, step = (to ^ (ctx // 2)) & 1, (to // 2 - ctx // 4) & 3
    slot = jnp.int32(0)
    for (f, d), at in SLOT.items():
        slot = jnp.where((flip == f) & (step == d), at, slot)
    return slot


def weight_rows(scale, moves, blocks, d_ref, d_other_ref, away_ref, part_ref, loaded=()):
    me = lax.axis_index("fsdp")
    n = blocks[0].shape[0] // 2
    slot_rows = part_ref.shape[0] // 8
    mine = jnp.concatenate([block[:n] for block in blocks], axis=0)
    away = jnp.concatenate([block[n:] for block in blocks], axis=0)
    away_ref[...] = away
    p = dot(mine, d_ref[...]) + dot(away, d_other_ref[...])
    p = (p * scale).astype(BF)
    for load in loaded:
        load.wait()
    for i, move in enumerate(moves):
        start = pl.multiple_of(slot_of(place(me, move)) * slot_rows, 16)
        part_ref[pl.ds(start, n), :] = p[i * n : (i + 1) * n]


def near_kernel(scale, moves, *refs):
    count = len(moves)
    blocks, (d_ref, d_other_ref, part_ref, away_ref) = refs[:count], refs[count:]
    weight_rows(scale, moves, blocks, d_ref, d_other_ref, away_ref, part_ref)


def far_kernel(scale, moves, *refs):
    count = len(moves)
    blocks, (d_ref, d_other_ref, keep_ref, got_ref, near_hbm), refs = refs[:count], refs[count : count + 5], refs[count + 5 :]
    outs, away_ref, (part_ref, sem) = refs[:4], refs[4], refs[5:]
    near = pltpu.make_async_copy(near_hbm, part_ref, sem.at[4])
    near.start()
    weight_rows(scale, moves, blocks, d_ref, d_other_ref, away_ref, part_ref, [near])
    slot_rows = part_ref.shape[0] // 8
    group = keep_ref.shape[0] // 8
    keep, got = keep_ref[...].astype(F32), got_ref[...].astype(F32)
    for j in range(8):
        rows = slice(j * group, (j + 1) * group)
        start = pl.multiple_of((slot_of(jnp.int32(j)) + 1) * slot_rows - 2 * group, 16)
        part_ref[pl.ds(start, 2 * group), :] = jnp.concatenate([keep[rows], got[rows]], axis=0).astype(BF)
    n = outs[0].shape[0]
    copy_all(pltpu.make_async_copy(part_ref.at[pl.ds(i * n, n), :], out, sem.at[i]) for i, out in enumerate(outs))


def part_sum_kernel(own_ref, x_ref, up_ref, down_ref, keep_ref, far_ref, side_ref, du_ref):
    n = keep_ref.shape[0]
    own, x, up, down = (ref[...].astype(F32) for ref in (own_ref, x_ref, up_ref, down_ref))
    m = own.shape[0] // 2
    keep_ref[...] = own[:n] + x[:n] + (up[:n] + down[:n])
    for out_ref, a, b in ((far_ref, own, x), (side_ref, up, down)):
        out_ref[...] = jnp.concatenate([a[m : m + n] + b[m : m + n], a[m + n :], b[m + n :]], axis=0).astype(BF)
    du_ref[...] = jnp.concatenate([v[n:m] for v in (own, x, up, down)], axis=0).astype(BF)


def assemble_kernel(*refs):
    blocks, theirs, (all_hbm, sem) = refs[:8], refs[8:10], refs[10:]
    me, core = lax.axis_index("fsdp"), my_core()
    n = blocks[0].shape[0] // 2
    copies = []
    for i, (block, move) in enumerate(zip(blocks, RING_FROM)):
        start = 2 * place(me, move)
        other = theirs[i // 4].at[pl.ds(i % 4 * n, n), :]
        for j, (x, half) in enumerate(((block.at[pl.ds(0, n), :], core), (other, 1 - core))):
            copies.append(pltpu.make_async_copy(x, all_hbm.at[rows_at(start + half, n), :], sem.at[2 * i + j]))
    copy_all(copies)


def final_kernel(keep_ref, far_ref, side_ref, du_ref, k_ref, v_ref, gw_ref, gk_ref, gv_ref, du_t_ref):
    n = gw_ref.shape[0]
    far, side, du = far_ref[...].astype(F32), side_ref[...].astype(F32), du_ref[...].astype(F32)
    gw_ref[...] = keep_ref[...] + (far[:n] + side[:n])
    ctx, core = lax.axis_index("ctx"), my_core()
    width = du_t_ref.shape[0]
    group = width // 16
    pieces = [du[i * 2 * group : (i + 1) * 2 * group] for i in range(4)]
    pieces += [v[n + i * 2 * group : n + (i + 1) * 2 * group] for v in (far, side) for i in range(2)]
    for piece, (flip, step) in zip(pieces, DU_FROM):
        chip = ((ctx // 4 + step) & 3) * 2 + ((ctx // 2) & 1 ^ flip)
        for rows, side_core in ((piece[:group], core), (piece[group:], 1 - core)):
            du_t_ref[rows_at(2 * chip + side_core, group), :] = rows
    du = dot(du_t_ref[...].T.astype(BF), order_in(16, width))
    gk_ref[...] = (du * v_ref[...].astype(F32)).astype(BF)
    gv_ref[...] = (du * k_ref[...].astype(F32)).astype(BF)


def staged(kernel, n_in, n_out, n_after, staged_in, staged_out):
    def run(*refs):
        ins, refs = list(refs[:n_in]), refs[n_in + n_after :]
        outs, refs = list(refs[:n_out]), refs[n_out:]
        extra = len(staged_in) + len(staged_out) + 2
        own, extra = refs[: len(refs) - extra], refs[len(refs) - extra :]
        buffers, (in_sem, out_sem) = extra[:-2], extra[-2:]
        loads, stores = [], []
        for j, i in enumerate(staged_in):
            loads.append(pltpu.make_async_copy(ins[i], buffers[j], in_sem.at[j]))
            ins[i] = buffers[j]
        for j, i in enumerate(staged_out):
            buffer = buffers[len(staged_in) + j]
            stores.append(pltpu.make_async_copy(buffer, outs[i], out_sem.at[j]))
            outs[i] = buffer
        copy_all(loads)
        kernel(*ins, *outs, *own)
        copy_all(stores)

    return run


def call(kernel, outs, ins, scratch=(), mib=16, flops=0, specs=None, after=(), staged_in=(), staged_out=(), aliases=None):
    total = sum(math.prod(o.shape) * o.dtype.itemsize for o in (*outs, *ins))
    if after or staged_in or staged_out:
        kernel = staged(kernel, len(ins), len(outs), len(after), staged_in, staged_out)
        buffers = [pltpu.VMEM(ins[i].shape, ins[i].dtype) for i in staged_in]
        buffers += [pltpu.VMEM(outs[i].shape, outs[i].dtype) for i in staged_out]
        sems = [pltpu.SemaphoreType.DMA((max(len(x), 1),)) for x in (staged_in, staged_out)]
        scratch = [*scratch, *buffers, *sems]
    in_specs, out_specs = specs or ([VMEM] * len(ins), [VMEM] * len(outs))
    in_specs = [ANY if i in staged_in else s for i, s in enumerate(in_specs)]
    out_specs = [ANY if i in staged_out else s for i, s in enumerate(out_specs)]
    return pl.pallas_call(
        kernel,
        out_shape=outs,
        in_specs=[*in_specs, *([ANY] * len(after))],
        out_specs=out_specs,
        scratch_shapes=scratch,
        input_output_aliases=aliases or {},
        compiler_params=params(mib),
        cost_estimate=pl.CostEstimate(flops=0, bytes_accessed=0, transcendentals=0),
    )(*ins, *after)


def shape(*dims, dtype=BF):
    return jax.ShapeDtypeStruct(dims, dtype)


def spread(values):
    return lax.all_to_all(values, "ctx", 0, 0, tiled=True)


def move_over(values, move):
    return lax.ppermute(values, "fsdp", [(i, place(i, move)) for i in range(8)])


RING_FROM = ((0, 0), (1, 0), (0, -1), (0, 1), (1, -1), (1, 1), (0, 2), (1, 2))


def dy_product(w_out, d_out, moves, signals=(), mib=MOST, after=()):
    channels, depth = w_out.shape
    rows = d_out.shape[0]
    step = 512
    pieces = rows // step
    count = len(moves)
    n = channels // 8
    outs = [shape(2 * n, rows)] * (count // 2)
    scratch = [
        pltpu.VMEM((count * n, depth), BF),
        pltpu.VMEM((rows, depth), BF),
        pltpu.VMEM((count * n, rows), BF),
        pltpu.SemaphoreType.DMA((count,)),
        pltpu.SemaphoreType.DMA((pieces,)),
        pltpu.SemaphoreType.DMA((count // 2 * pieces,)),
    ]
    kernel = functools.partial(dy_kernel, step, moves, None)
    if signals:
        kernel = functools.partial(open_kernel, step, moves)
        outs.append(shape(2 * signals[0].shape[1], rows))
        scratch += [pltpu.VMEM(x.shape, x.dtype) for x in (*signals, outs[-1])] + [pltpu.SemaphoreType.DMA((4,))]
    return call(
        kernel,
        outs,
        [w_out, d_out, *signals],
        scratch,
        mib=mib,
        flops=2 * count * n * depth * rows,
        specs=([ANY] * (2 + len(signals)), [ANY] * len(outs)),
        after=after,
    )


def weight_product(blocks, moves, d_out, d_other, scale, slot_rows, after=(), du=(), near=()):
    rows, columns = d_out.shape
    n = blocks[0].shape[0] // 2
    count = len(moves)
    all_rows = 8 * slot_rows
    outs = [shape(all_rows // 4, columns)] * 4 if near else [shape(all_rows, columns)]
    ins = [*blocks, d_out, d_other, *du]
    return call(
        functools.partial(far_kernel if near else near_kernel, scale, moves),
        [*outs, shape(count * n, rows)],
        [*ins, *near],
        [pltpu.VMEM((all_rows, columns), BF), pltpu.SemaphoreType.DMA((5,))] if near else [],
        flops=4 * count * n * rows * columns,
        specs=([VMEM] * len(ins) + [ANY] * len(near), [ANY if near else VMEM] * len(outs) + [VMEM]),
        after=after,
    )


def on_device(query_in, key_in, value_in, filt, w_out, d_out):
    seq_rows, width = query_in.shape
    channels, columns = w_out.shape
    ways = lax.axis_size("ctx")
    group, half = width // ways, width // 2
    n = HALF * group
    tables = host_tables(ways, group)

    swap = lambda v: lax.ppermute(v, "ctx", [(i, i ^ 1) for i in range(ways)])
    rows_like, half_like = shape(width, seq_rows), shape(half, seq_rows)

    x_y, up_y, down_y, send = dy_product(w_out, d_out, DY_MOVES[2:], (key_in, value_in, filt))
    (own_y,) = dy_product(w_out, d_out, DY_MOVES[:2], mib=16, after=[x_y])
    keep_y, far_y, side_y = call(
        sum_kernel,
        [shape(width, seq_rows, dtype=F32), rows_like, rows_like],
        [own_y, move_over(x_y, (1, 0)), move_over(up_y, (0, 1)), move_over(down_y, (0, -1))],
    )
    arrived = spread(send)

    flops = 2 * 2 * n * (4 * FAC) * FAC
    conv, spectrum = call(
        conv_kernel,
        [rows_like, shape(2 * n, FAC)],
        [arrived, *tables],
        mib=20,
        flops=3 * flops,
        after=[far_y],
        staged_out=(0,),
    )
    dy = (keep_y, move_over(far_y, (0, 2)), move_over(side_y, (1, 0)))
    (send,) = call(
        functools.partial(dz_kernel, ways), [shape(2 * width, seq_rows)], [*dy, query_in, conv], staged_out=(0,)
    )
    q_mine, q_away = call(
        turn_query_kernel,
        [half_like, half_like],
        [query_in],
        [pltpu.VMEM((width, seq_rows), F32)],
        after=[send],
    )
    q_theirs = swap(q_away)
    send, d_late = lax.optimization_barrier((send, d_out))
    d_other = swap(d_late)
    arrived = spread(send)
    gated, z_away = call(
        functools.partial(gate_kernel, ways),
        [rows_like, half_like],
        [arrived, q_mine, q_theirs],
        after=[d_other],
    )
    z_theirs = swap(z_away)
    own_far, other = move_over(gated, (0, 2)), move_over(gated, (1, 0))
    own_up, own_down = move_over(gated, (0, 1)), move_over(gated, (0, -1))
    like = shape(seq_rows, width)
    (grad_query,) = call(
        functools.partial(query_kernel, ways),
        [like],
        [*dy, arrived, z_theirs],
        [pltpu.VMEM((width, seq_rows), F32)],
        staged_out=(0,),
    )
    du_away, du_keep = call(
        adjoint_kernel, [half_like, half_like], [arrived, spectrum, *tables], mib=20, flops=2 * flops
    )
    other, own_far, du_away = lax.optimization_barrier((other, own_far, du_away))
    du_got = swap(du_away)
    other_far = move_over(own_far, (1, 0))
    other_up, other_down = move_over(other, (0, 1)), move_over(other, (0, -1))
    blocks = gated, other, own_up, own_down, other_up, other_down, own_far, other_far

    slot_rows = half + 2 * group
    scale = 1.0 / math.sqrt(seq_rows * ways)
    weight = functools.partial(weight_product, d_out=d_out, d_other=d_other, scale=scale, slot_rows=slot_rows)
    near, away = weight(blocks[:4], RING_FROM[:4])
    theirs_near = swap(away)
    own_w, x_w, up_w, down_w, away = weight(blocks[4:], RING_FROM[4:], du=(du_keep, du_got), near=(near,))
    over_x = lambda v: lax.ppermute(v, "ctx", [(i, i ^ 2) for i in range(ways)])
    along_y = lambda v, step: lax.ppermute(v, "ctx", [(i, (i + 4 * step) % ways) for i in range(ways)])
    part_like = shape(channels // ways, columns, dtype=F32)
    onward = shape(half + 4 * group, columns)
    keep_w, far_w, side_w, du_near = call(
        part_sum_kernel,
        [part_like, onward, onward, half_like],
        [own_w, over_x(x_w), along_y(up_w, 1), along_y(down_w, -1)],
    )
    far_w, side_w = along_y(far_w, 2), over_x(side_w)

    (gated_all,) = call(
        assemble_kernel,
        [shape(channels, seq_rows)],
        [*blocks, theirs_near, swap(away)],
        [pltpu.SemaphoreType.DMA((16,))],
        specs=([ANY] * 10, [ANY]),
    )
    layer_out = lax.dot_general(
        gated_all, w_out, (((0,), (0,)), ((), ())), preferred_element_type=F32
    ).astype(BF)

    grad_weight, grad_key, grad_value = call(
        final_kernel,
        [part_like, like, like],
        [keep_w, far_w, side_w, du_near, key_in, value_in],
        [pltpu.VMEM((width, columns), F32)],
        after=[layer_out, grad_query],
        staged_out=(0, 1, 2),
    )
    return (layer_out, grad_query, grad_key, grad_value, grad_weight)


def solution(mesh):
    both = P("ctx", "fsdp")
    return jax.shard_map(
        on_device,
        mesh=mesh,
        in_specs=(both, both, both, both, P(None, "fsdp"), both),
        out_specs=(both, both, both, both, both),
        check_vma=False,
    )
```

```python
import functools
import math

import jax
import jax.numpy as jnp
import numpy as np
from jax import lax
from jax.experimental import pallas as pl
from jax.experimental.pallas import tpu as pltpu
from jax.sharding import PartitionSpec as P

ROW = 1024
FAC = 256
QF = 128
HALF = QF // 2 + 1
LANE_TILES = ROW // FAC
BF = jnp.bfloat16
F32 = jnp.float32
MIB = 1 << 20
MOST = 56


def angles(rows, cols, modulus):
    product = (rows[:, None].astype(np.int64) * cols[None, :]) % modulus
    return (product.astype(np.float32) * np.float32(2.0 * math.pi / modulus)).astype(np.float64)


def host_tables(ways, group):
    k2, t1 = np.arange(HALF), np.arange(FAC)
    t2 = (np.arange(LANE_TILES)[:, None] + LANE_TILES * np.arange(ways)[None, :]).reshape(-1)
    a = angles(k2, t2, QF)
    steps = np.stack([np.cos(a), -np.sin(a)])
    first = np.einsum("rkt,cd->rkctd", steps, np.eye(group)).reshape(2 * HALF * group, t2.size * group)
    s = angles(t1, t1, FAC)
    square = np.concatenate([np.cos(s), np.sin(s)])
    w = angles(k2, t1, QF * FAC)
    twiddle = np.concatenate([np.cos(w), np.sin(w)]).astype(np.float32)
    as_bf = lambda v: np.asarray(v, np.float32).astype(BF)
    return as_bf(first), as_bf(square), twiddle


def params(mib):
    return pltpu.CompilerParams(vmem_limit_bytes=mib * MIB)


VMEM = pl.BlockSpec(memory_space=pltpu.VMEM)
ANY = pl.BlockSpec(memory_space=pl.ANY)
DY_MOVES = ((0, 0), (0, 2), (1, 0), (1, 2), (0, 1), (1, 1), (0, -1), (1, -1))
DU_FROM = ((0, 0), (1, 0), (0, -1), (0, 1), (0, 2), (1, 2), (1, -1), (1, 1))
SLOT = {move: i for i, (flip, step) in enumerate(DY_MOVES) for move in ((flip, step % 4),)}


def place(index, move):
    flip, step = move
    return ((index ^ 4) if flip else index) & 4 | ((index + step) & 3)


def dot(a, b):
    return jnp.dot(a, b, preferred_element_type=F32)


def my_core():
    return lax.axis_index("ctx") & 1


def rows_at(i, n):
    return pl.ds(pl.multiple_of(i * n, n), n)


def product_t(order, values):
    return lax.dot_general(order, values, (((1,), (1,)), ((), ())), preferred_element_type=F32)


def copy_all(copies):
    copies = list(copies)
    for copy in copies:
        copy.start()
    for copy in copies:
        copy.wait()


def iota(axis, n):
    return lax.broadcasted_iota(jnp.int32, (n, n), axis)


def order_in(ways, width):
    row, group = iota(0, width), width // ways
    r = group // 2
    channel = (row // r % 2) * (width // 2) + (row // group) * r + row % r
    return (channel == iota(1, width)).astype(F32).astype(BF)


def order_z(ways, width):
    row = lax.broadcasted_iota(jnp.int32, (width, 2 * width), 0)
    column = lax.broadcasted_iota(jnp.int32, (width, 2 * width), 1)
    r = width // ways // 2
    core = (row // (width // 2)) ^ my_core()
    slot = (row % (width // 2) // r) * 4 * r + core * r + row % r
    return (slot == column).astype(F32).astype(BF)


def dy_kernel(step, moves, between, w_hbm, d_hbm, *refs):
    outs, (w_ref, d_ref, p_ref, w_sem, d_sem, o_sem) = refs[:-6], refs[-6:]
    me = lax.axis_index("fsdp")
    n = outs[0].shape[0] // 2
    gather = [
        pltpu.make_async_copy(w_hbm.at[rows_at(place(me, move), n), :], w_ref.at[pl.ds(i * n, n), :], w_sem.at[i])
        for i, move in enumerate(moves)
    ]
    pieces = [pl.ds(i * step, step) for i in range(d_ref.shape[0] // step)]
    loads = [
        pltpu.make_async_copy(d_hbm.at[rows, :], d_ref.at[rows, :], d_sem.at[i]) for i, rows in enumerate(pieces)
    ]
    other_loads, other_work, other_stores = between or ((), None, ())
    for copy in (*gather, loads[0], *other_loads):
        copy.start()
    for copy in gather:
        copy.wait()
    stores = []
    for i, rows in enumerate(pieces):
        loads[i].wait()
        if i + 1 < len(pieces):
            loads[i + 1].start()
        p_ref[:, rows] = product_t(w_ref[...], d_ref[rows, :]).astype(BF)
        for j, out in enumerate(outs):
            store = pltpu.make_async_copy(
                p_ref.at[pl.ds(2 * n * j, 2 * n), rows], out.at[:, rows], o_sem.at[i * len(outs) + j]
            )
            store.start()
            stores.append(store)
        if i == 0 and other_work:
            for copy in other_loads:
                copy.wait()
            other_work()
            for copy in other_stores:
                copy.start()
                stores.append(copy)
    for store in stores:
        store.wait()


def open_kernel(step, moves, w_hbm, d_hbm, k_hbm, v_hbm, f_hbm, *refs):
    count = len(moves) // 2
    outs, send_hbm, (k_ref, v_ref, f_ref, send_ref, sem), refs = refs[:count], refs[count], refs[-5:], refs[count + 1 : -5]
    froms = zip((k_hbm, v_hbm, f_hbm), (k_ref, v_ref, f_ref))
    loads = [pltpu.make_async_copy(x, to, sem.at[i]) for i, (x, to) in enumerate(froms)]

    def mix():
        width = k_ref.shape[1]
        ways = send_ref.shape[0] // (2 * 8)
        order = order_in(ways, width)
        mixed = (k_ref[...].astype(F32) * v_ref[...].astype(F32)).astype(BF)
        parts = [product_t(order, x).reshape(ways, 1, -1, ROW) for x in (mixed, f_ref[...])]
        send_ref[...] = jnp.concatenate(parts, axis=1).reshape(send_ref.shape).astype(BF)

    between = (loads, mix, [pltpu.make_async_copy(send_ref, send_hbm, sem.at[3])])
    dy_kernel(step, moves, between, w_hbm, d_hbm, *outs, *refs)


def turn_query_kernel(q_ref, mine_ref, away_ref, qt_ref):
    qt_ref[...] = q_ref[...].astype(F32).T
    core, n = my_core(), mine_ref.shape[0]
    mine_ref[...] = qt_ref[rows_at(core, n), :].astype(BF)
    away_ref[...] = qt_ref[rows_at(1 - core, n), :].astype(BF)


def gate_kernel(ways, z_ref, q_mine_ref, q_theirs_ref, gated_ref, z_away_ref):
    z = dot(order_z(ways, gated_ref.shape[0]), z_ref[...])
    n = z.shape[0] // 2
    z_away_ref[...] = z[n:].astype(BF)
    gated_ref[pl.ds(0, n), :] = (z[:n] * q_mine_ref[...].astype(F32)).astype(BF)
    gated_ref[pl.ds(n, n), :] = (z[n:] * q_theirs_ref[...].astype(F32)).astype(BF)


def sum_kernel(own_ref, up_ref, x_ref, down_ref, keep_ref, far_ref, side_ref):
    n = keep_ref.shape[0]
    near, second = pl.ds(0, n), pl.ds(n, n)
    own = own_ref[near, :].astype(F32) + x_ref[near, :].astype(F32)
    keep_ref[...] = own + (up_ref[near, :].astype(F32) + down_ref[near, :].astype(F32))
    far_ref[...] = (own_ref[second, :].astype(F32) + x_ref[second, :].astype(F32)).astype(BF)
    side_ref[...] = (up_ref[second, :].astype(F32) + down_ref[second, :].astype(F32)).astype(BF)


def dz_kernel(ways, keep_ref, far_ref, side_ref, q_ref, z_ref, send_ref):
    dy = keep_ref[...] + (far_ref[...].astype(F32) + side_ref[...].astype(F32))
    dz = (dy * q_ref[...].astype(F32).T).astype(BF)
    pieces = (z_ref[...].astype(F32), dot(order_in(ways, dz.shape[0]), dz))
    both = jnp.concatenate([x.reshape(ways, 1, -1, ROW) for x in pieces], axis=1)
    send_ref[...] = both.reshape(send_ref.shape).astype(BF)


def query_kernel(ways, keep_ref, far_ref, side_ref, z_ref, z_theirs_ref, gq_ref, gq_t_ref):
    gq_t_ref[...] = keep_ref[...] + (far_ref[...].astype(F32) + side_ref[...].astype(F32))
    core, n = my_core(), z_theirs_ref.shape[0]
    z_mine = dot(order_z(ways, gq_t_ref.shape[0])[:n], z_ref[...]).astype(BF)
    for z, half in ((z_mine, core), (z_theirs_ref[...], 1 - core)):
        own = rows_at(half, n)
        gq_t_ref[own, :] *= z.astype(F32)
    gq_ref[...] = gq_t_ref[...].T.astype(BF)


class Tables:
    def __init__(self, first, square, twiddle):
        self.first, self.square = first, square
        self.group = first.shape[0] // twiddle.shape[0]
        rows = [jnp.broadcast_to(twiddle[i : i + 1, :], (self.group, FAC)) for i in range(twiddle.shape[0])]
        self.twiddle = jnp.concatenate(rows, axis=0)


def times_square(left, right, tables):
    square = tables.square
    return dot(left, square[:FAC]) + dot(right, square[FAC:])


def transform(x, tables):
    x = jnp.concatenate([x[:, u * FAC : (u + 1) * FAC] for u in range(LANE_TILES)], axis=0)
    section = dot(tables.first[...], x)
    n = section.shape[0] // 2
    twiddle = tables.twiddle
    re, im, tc, ts = section[:n], section[n:], twiddle[:n], twiddle[n:]
    b_re, b_im = re * tc + im * ts, im * tc - re * ts
    left = jnp.concatenate([b_re, b_im], axis=0).astype(BF)
    right = jnp.concatenate([b_im, -b_re], axis=0).astype(BF)
    f = times_square(left, right, tables)
    return f[:n], f[n:]


def signal(p_re, p_im, tables):
    n, group = p_re.shape[0], tables.group
    left = jnp.concatenate([p_re, p_im], axis=0).astype(BF)
    right = jnp.concatenate([-p_im, p_re], axis=0).astype(BF)
    c = times_square(left, right, tables)
    re, im, tc, ts = c[:n], c[n:], tables.twiddle[:n], tables.twiddle[n:]
    row = lax.broadcasted_iota(jnp.int32, re.shape, 0)
    weight = jnp.where((row < group) | (row >= n - group), 1.0 / (QF * FAC), 2.0 / (QF * FAC))
    e = jnp.concatenate([(re * tc - im * ts) * weight, (im * tc + re * ts) * weight], axis=0).astype(BF)
    x = lax.dot_general(tables.first[...], e, (((0,), (0,)), ((), ())), preferred_element_type=F32)
    rows = x.shape[0] // LANE_TILES
    return jnp.concatenate([x[u * rows : (u + 1) * rows] for u in range(LANE_TILES)], axis=1)


def conv_kernel(r_ref, first_ref, square_ref, twiddle_ref, z_ref, h_ref):
    tables = Tables(first_ref, square_ref, twiddle_ref)
    rows = z_ref.shape[0]
    group = h_ref.shape[0] // (2 * HALF)
    r = r_ref[...].astype(F32).reshape(-1, 2, group, ROW)
    u, h = (transform(r[:, s].reshape(rows, ROW).astype(BF), tables) for s in range(2))
    h_ref[...] = jnp.concatenate(h, axis=0).astype(BF)
    p_re, p_im = u[0] * h[0] - u[1] * h[1], u[0] * h[1] + u[1] * h[0]
    z = signal(p_re, p_im, tables).astype(BF)
    row, r = iota(0, rows), group // 2
    source = row // (4 * r) * 4 * r + row // r % 2 * 2 * r + row // (2 * r) % 2 * r + row % r
    z_ref[...] = dot((source == iota(1, rows)).astype(F32).astype(BF), z).astype(BF)


def adjoint_kernel(r_ref, h_ref, first_ref, square_ref, twiddle_ref, away_ref, keep_ref):
    tables = Tables(first_ref, square_ref, twiddle_ref)
    rows = 2 * keep_ref.shape[0]
    group = h_ref.shape[0] // (2 * HALF)
    r = r_ref[...].astype(F32).reshape(-1, 2, group, ROW)[:, 1]
    g_re, g_im = transform(r.reshape(rows, ROW).astype(BF), tables)
    h = h_ref[...].astype(F32)
    n = h.shape[0] // 2
    h_re, h_im = h[:n], h[n:]
    q_re, q_im = h_re * g_re + h_im * g_im, h_re * g_im - h_im * g_re
    du = signal(q_re, q_im, tables).reshape(-1, 2, group, ROW)
    low, high, first_core = du[:, 0], du[:, 1], my_core() == 0
    keep_ref[...] = jnp.where(first_core, low, high).reshape(keep_ref.shape).astype(BF)
    away_ref[...] = jnp.where(first_core, high, low).reshape(keep_ref.shape).astype(BF)


def slot_of(to):
    ctx = lax.axis_index("ctx")
    flip, step = (to ^ (ctx // 2)) & 1, (to // 2 - ctx // 4) & 3
    slot = jnp.int32(0)
    for (f, d), at in SLOT.items():
        slot = jnp.where((flip == f) & (step == d), at, slot)
    return slot


def weight_rows(scale, moves, blocks, d_ref, d_other_ref, away_ref, part_ref, loaded=()):
    me = lax.axis_index("fsdp")
    n = blocks[0].shape[0] // 2
    slot_rows = part_ref.shape[0] // 8
    mine = jnp.concatenate([block[:n] for block in blocks], axis=0)
    away = jnp.concatenate([block[n:] for block in blocks], axis=0)
    away_ref[...] = away
    p = dot(mine, d_ref[...]) + dot(away, d_other_ref[...])
    p = (p * scale).astype(BF)
    for load in loaded:
        load.wait()
    for i, move in enumerate(moves):
        start = pl.multiple_of(slot_of(place(me, move)) * slot_rows, 16)
        part_ref[pl.ds(start, n), :] = p[i * n : (i + 1) * n]


def near_kernel(scale, moves, *refs):
    count = len(moves)
    blocks, (d_ref, d_other_ref, part_ref, away_ref) = refs[:count], refs[count:]
    weight_rows(scale, moves, blocks, d_ref, d_other_ref, away_ref, part_ref)


def far_kernel(scale, moves, *refs):
    count = len(moves)
    blocks, (d_ref, d_other_ref, keep_ref, got_ref, near_hbm), refs = refs[:count], refs[count : count + 5], refs[count + 5 :]
    outs, away_ref, (part_ref, sem) = refs[:4], refs[4], refs[5:]
    near = pltpu.make_async_copy(near_hbm, part_ref, sem.at[4])
    near.start()
    weight_rows(scale, moves, blocks, d_ref, d_other_ref, away_ref, part_ref, [near])
    slot_rows = part_ref.shape[0] // 8
    group = keep_ref.shape[0] // 8
    keep, got = keep_ref[...].astype(F32), got_ref[...].astype(F32)
    for j in range(8):
        rows = slice(j * group, (j + 1) * group)
        start = pl.multiple_of((slot_of(jnp.int32(j)) + 1) * slot_rows - 2 * group, 16)
        part_ref[pl.ds(start, 2 * group), :] = jnp.concatenate([keep[rows], got[rows]], axis=0).astype(BF)
    n = outs[0].shape[0]
    copy_all(pltpu.make_async_copy(part_ref.at[pl.ds(i * n, n), :], out, sem.at[i]) for i, out in enumerate(outs))


def part_sum_kernel(own_ref, x_ref, up_ref, down_ref, keep_ref, far_ref, side_ref, du_ref):
    n = keep_ref.shape[0]
    own, x, up, down = (ref[...].astype(F32) for ref in (own_ref, x_ref, up_ref, down_ref))
    m = own.shape[0] // 2
    keep_ref[...] = own[:n] + x[:n] + (up[:n] + down[:n])
    for out_ref, a, b in ((far_ref, own, x), (side_ref, up, down)):
        out_ref[...] = jnp.concatenate([a[m : m + n] + b[m : m + n], a[m + n :], b[m + n :]], axis=0).astype(BF)
    du_ref[...] = jnp.concatenate([v[n:m] for v in (own, x, up, down)], axis=0).astype(BF)


def assemble_kernel(*refs):
    blocks, theirs, (all_hbm, sem) = refs[:8], refs[8:10], refs[10:]
    me, core = lax.axis_index("fsdp"), my_core()
    n = blocks[0].shape[0] // 2
    copies = []
    for i, (block, move) in enumerate(zip(blocks, RING_FROM)):
        start = 2 * place(me, move)
        other = theirs[i // 4].at[pl.ds(i % 4 * n, n), :]
        for j, (x, half) in enumerate(((block.at[pl.ds(0, n), :], core), (other, 1 - core))):
            copies.append(pltpu.make_async_copy(x, all_hbm.at[rows_at(start + half, n), :], sem.at[2 * i + j]))
    copy_all(copies)


def final_kernel(keep_ref, far_ref, side_ref, du_ref, k_ref, v_ref, gw_ref, gk_ref, gv_ref, du_t_ref):
    n = gw_ref.shape[0]
    far, side, du = far_ref[...].astype(F32), side_ref[...].astype(F32), du_ref[...].astype(F32)
    gw_ref[...] = keep_ref[...] + (far[:n] + side[:n])
    ctx, core = lax.axis_index("ctx"), my_core()
    width = du_t_ref.shape[0]
    group = width // 16
    pieces = [du[i * 2 * group : (i + 1) * 2 * group] for i in range(4)]
    pieces += [v[n + i * 2 * group : n + (i + 1) * 2 * group] for v in (far, side) for i in range(2)]
    for piece, (flip, step) in zip(pieces, DU_FROM):
        chip = ((ctx // 4 + step) & 3) * 2 + ((ctx // 2) & 1 ^ flip)
        for rows, side_core in ((piece[:group], core), (piece[group:], 1 - core)):
            du_t_ref[rows_at(2 * chip + side_core, group), :] = rows
    du = dot(du_t_ref[...].T.astype(BF), order_in(16, width))
    gk_ref[...] = (du * v_ref[...].astype(F32)).astype(BF)
    gv_ref[...] = (du * k_ref[...].astype(F32)).astype(BF)


def staged(kernel, n_in, n_out, n_after, staged_in, staged_out):
    def run(*refs):
        ins, refs = list(refs[:n_in]), refs[n_in + n_after :]
        outs, refs = list(refs[:n_out]), refs[n_out:]
        extra = len(staged_in) + len(staged_out) + 2
        own, extra = refs[: len(refs) - extra], refs[len(refs) - extra :]
        buffers, (in_sem, out_sem) = extra[:-2], extra[-2:]
        loads, stores = [], []
        for j, i in enumerate(staged_in):
            loads.append(pltpu.make_async_copy(ins[i], buffers[j], in_sem.at[j]))
            ins[i] = buffers[j]
        for j, i in enumerate(staged_out):
            buffer = buffers[len(staged_in) + j]
            stores.append(pltpu.make_async_copy(buffer, outs[i], out_sem.at[j]))
            outs[i] = buffer
        copy_all(loads)
        kernel(*ins, *outs, *own)
        copy_all(stores)

    return run


def call(kernel, outs, ins, scratch=(), mib=16, flops=0, specs=None, after=(), staged_in=(), staged_out=(), aliases=None):
    total = sum(math.prod(o.shape) * o.dtype.itemsize for o in (*outs, *ins))
    if after or staged_in or staged_out:
        kernel = staged(kernel, len(ins), len(outs), len(after), staged_in, staged_out)
        buffers = [pltpu.VMEM(ins[i].shape, ins[i].dtype) for i in staged_in]
        buffers += [pltpu.VMEM(outs[i].shape, outs[i].dtype) for i in staged_out]
        sems = [pltpu.SemaphoreType.DMA((max(len(x), 1),)) for x in (staged_in, staged_out)]
        scratch = [*scratch, *buffers, *sems]
    in_specs, out_specs = specs or ([VMEM] * len(ins), [VMEM] * len(outs))
    in_specs = [ANY if i in staged_in else s for i, s in enumerate(in_specs)]
    out_specs = [ANY if i in staged_out else s for i, s in enumerate(out_specs)]
    return pl.pallas_call(
        kernel,
        out_shape=outs,
        in_specs=[*in_specs, *([ANY] * len(after))],
        out_specs=out_specs,
        scratch_shapes=scratch,
        input_output_aliases=aliases or {},
        compiler_params=params(mib),
        cost_estimate=pl.CostEstimate(flops=0, bytes_accessed=0, transcendentals=0),
    )(*ins, *after)


def shape(*dims, dtype=BF):
    return jax.ShapeDtypeStruct(dims, dtype)


def spread(values):
    return lax.all_to_all(values, "ctx", 0, 0, tiled=True)


def move_over(values, move):
    return lax.ppermute(values, "fsdp", [(i, place(i, move)) for i in range(8)])


RING_FROM = ((0, 0), (1, 0), (0, -1), (0, 1), (1, -1), (1, 1), (0, 2), (1, 2))


def dy_product(w_out, d_out, moves, signals=(), mib=MOST, after=()):
    channels, depth = w_out.shape
    rows = d_out.shape[0]
    step = 512
    pieces = rows // step
    count = len(moves)
    n = channels // 8
    outs = [shape(2 * n, rows)] * (count // 2)
    scratch = [
        pltpu.VMEM((count * n, depth), BF),
        pltpu.VMEM((rows, depth), BF),
        pltpu.VMEM((count * n, rows), BF),
        pltpu.SemaphoreType.DMA((count,)),
        pltpu.SemaphoreType.DMA((pieces,)),
        pltpu.SemaphoreType.DMA((count // 2 * pieces,)),
    ]
    kernel = functools.partial(dy_kernel, step, moves, None)
    if signals:
        kernel = functools.partial(open_kernel, step, moves)
        outs.append(shape(2 * signals[0].shape[1], rows))
        scratch += [pltpu.VMEM(x.shape, x.dtype) for x in (*signals, outs[-1])] + [pltpu.SemaphoreType.DMA((4,))]
    return call(
        kernel,
        outs,
        [w_out, d_out, *signals],
        scratch,
        mib=mib,
        flops=2 * count * n * depth * rows,
        specs=([ANY] * (2 + len(signals)), [ANY] * len(outs)),
        after=after,
    )


def weight_product(blocks, moves, d_out, d_other, scale, slot_rows, after=(), du=(), near=()):
    rows, columns = d_out.shape
    n = blocks[0].shape[0] // 2
    count = len(moves)
    all_rows = 8 * slot_rows
    outs = [shape(all_rows // 4, columns)] * 4 if near else [shape(all_rows, columns)]
    ins = [*blocks, d_out, d_other, *du]
    return call(
        functools.partial(far_kernel if near else near_kernel, scale, moves),
        [*outs, shape(count * n, rows)],
        [*ins, *near],
        [pltpu.VMEM((all_rows, columns), BF), pltpu.SemaphoreType.DMA((5,))] if near else [],
        flops=4 * count * n * rows * columns,
        specs=([VMEM] * len(ins) + [ANY] * len(near), [ANY if near else VMEM] * len(outs) + [VMEM]),
        after=after,
    )


def on_device(query_in, key_in, value_in, filt, w_out, d_out):
    seq_rows, width = query_in.shape
    channels, columns = w_out.shape
    ways = lax.axis_size("ctx")
    group, half = width // ways, width // 2
    n = HALF * group
    tables = host_tables(ways, group)

    swap = lambda v: lax.ppermute(v, "ctx", [(i, i ^ 1) for i in range(ways)])
    rows_like, half_like = shape(width, seq_rows), shape(half, seq_rows)

    x_y, up_y, down_y, send = dy_product(w_out, d_out, DY_MOVES[2:], (key_in, value_in, filt))
    (own_y,) = dy_product(w_out, d_out, DY_MOVES[:2], mib=16, after=[x_y])
    keep_y, far_y, side_y = call(
        sum_kernel,
        [shape(width, seq_rows, dtype=F32), rows_like, rows_like],
        [own_y, move_over(up_y, (0, 1)), move_over(x_y, (1, 0)), move_over(down_y, (0, -1))],
    )
    arrived = spread(send)

    flops = 2 * 2 * n * (4 * FAC) * FAC
    conv, spectrum = call(
        conv_kernel,
        [rows_like, shape(2 * n, FAC)],
        [arrived, *tables],
        mib=20,
        flops=3 * flops,
        after=[far_y],
    )
    dy = (keep_y, move_over(far_y, (0, 2)), move_over(side_y, (1, 0)))
    (send,) = call(
        functools.partial(dz_kernel, ways), [shape(2 * width, seq_rows)], [*dy, query_in, conv], staged_out=(0,)
    )
    q_mine, q_away = call(
        turn_query_kernel,
        [half_like, half_like],
        [query_in],
        [pltpu.VMEM((width, seq_rows), F32)],
        after=[send],
    )
    q_theirs = swap(q_away)
    send, d_late = lax.optimization_barrier((send, d_out))
    d_other = swap(d_late)
    arrived = spread(send)
    gated, z_away = call(
        functools.partial(gate_kernel, ways),
        [rows_like, half_like],
        [arrived, q_mine, q_theirs],
        after=[d_other],
    )
    z_theirs = swap(z_away)
    own_far, other = move_over(gated, (0, 2)), move_over(gated, (1, 0))
    own_up, own_down = move_over(gated, (0, 1)), move_over(gated, (0, -1))
    like = shape(seq_rows, width)
    du_away, du_keep = call(
        adjoint_kernel, [half_like, half_like], [arrived, spectrum, *tables], mib=20, flops=2 * flops
    )
    other, own_far, du_away = lax.optimization_barrier((other, own_far, du_away))
    du_got = swap(du_away)
    other_far = move_over(own_far, (1, 0))
    other_up, other_down = move_over(other, (0, 1)), move_over(other, (0, -1))
    blocks = gated, other, own_up, own_down, other_up, other_down, own_far, other_far

    slot_rows = half + 2 * group
    scale = 1.0 / math.sqrt(seq_rows * ways)
    weight = functools.partial(weight_product, d_out=d_out, d_other=d_other, scale=scale, slot_rows=slot_rows)
    near, away = weight(blocks[:4], RING_FROM[:4], after=[z_theirs])
    theirs_near = swap(away)
    own_w, x_w, up_w, down_w, away = weight(blocks[4:], RING_FROM[4:], du=(du_keep, du_got), near=(near,))
    (gated_all,) = call(
        assemble_kernel,
        [shape(channels, seq_rows)],
        [*blocks, theirs_near, swap(away)],
        [pltpu.SemaphoreType.DMA((16,))],
        specs=([ANY] * 10, [ANY]),
    )
    layer_out = lax.dot_general(
        gated_all, w_out, (((0,), (0,)), ((), ())), preferred_element_type=F32
    ).astype(BF)

    over_x = lambda v: lax.ppermute(v, "ctx", [(i, i ^ 2) for i in range(ways)])
    along_y = lambda v, step: lax.ppermute(v, "ctx", [(i, (i + 4 * step) % ways) for i in range(ways)])
    part_like = shape(channels // ways, columns, dtype=F32)
    onward = shape(half + 4 * group, columns)
    keep_w, far_w, side_w, du_near = call(
        part_sum_kernel,
        [part_like, onward, onward, half_like],
        [own_w, over_x(x_w), along_y(up_w, 1), along_y(down_w, -1)],
        after=[layer_out],
    )
    onward_w = far_w
    far_w, side_w = along_y(far_w, 2), over_x(side_w)
    (grad_query,) = call(
        functools.partial(query_kernel, ways),
        [like],
        [*dy, arrived, z_theirs],
        [pltpu.VMEM((width, seq_rows), F32)],
        staged_out=(0,),
        after=[onward_w],
    )

    grad_weight, grad_key, grad_value = call(
        final_kernel,
        [part_like, like, like],
        [keep_w, far_w, side_w, du_near, key_in, value_in],
        [pltpu.VMEM((width, columns), F32)],
        staged_out=(0, 1, 2),
    )
    return (layer_out, grad_query, grad_key, grad_value, grad_weight)


def solution(mesh):
    both = P("ctx", "fsdp")
    return jax.shard_map(
        on_device,
        mesh=mesh,
        in_specs=(both, both, both, both, P(None, "fsdp"), both),
        out_specs=(both, both, both, both, both),
        check_vma=False,
    )
```

```python
import functools
import math

import jax
import jax.numpy as jnp
import numpy as np
from jax import lax
from jax.experimental import pallas as pl
from jax.experimental.pallas import tpu as pltpu
from jax.sharding import PartitionSpec as P

ROW = 1024
FAC = 256
QF = 128
HALF = QF // 2 + 1
LANE_TILES = ROW // FAC
BF = jnp.bfloat16
F32 = jnp.float32
MIB = 1 << 20
MOST = 56


def angles(rows, cols, modulus):
    product = (rows[:, None].astype(np.int64) * cols[None, :]) % modulus
    return (product.astype(np.float32) * np.float32(2.0 * math.pi / modulus)).astype(np.float64)


def host_tables(ways, group):
    k2, t1 = np.arange(HALF), np.arange(FAC)
    t2 = (np.arange(LANE_TILES)[:, None] + LANE_TILES * np.arange(ways)[None, :]).reshape(-1)
    a = angles(k2, t2, QF)
    steps = np.stack([np.cos(a), -np.sin(a)])
    first = np.einsum("rkt,cd->rkctd", steps, np.eye(group)).reshape(2 * HALF * group, t2.size * group)
    s = angles(t1, t1, FAC)
    square = np.concatenate([np.cos(s), np.sin(s)])
    w = angles(k2, t1, QF * FAC)
    twiddle = np.concatenate([np.cos(w), np.sin(w)]).astype(np.float32)
    as_bf = lambda v: np.asarray(v, np.float32).astype(BF)
    return as_bf(first), as_bf(square), twiddle


def params(mib):
    return pltpu.CompilerParams(vmem_limit_bytes=mib * MIB)


VMEM = pl.BlockSpec(memory_space=pltpu.VMEM)
ANY = pl.BlockSpec(memory_space=pl.ANY)
DY_MOVES = ((0, 0), (0, 2), (1, 0), (1, 2), (0, 1), (1, 1), (0, -1), (1, -1))
DU_FROM = ((0, 0), (1, 0), (0, -1), (0, 1), (0, 2), (1, 2), (1, -1), (1, 1))
SLOT = {move: i for i, (flip, step) in enumerate(DY_MOVES) for move in ((flip, step % 4),)}


def place(index, move):
    flip, step = move
    return ((index ^ 4) if flip else index) & 4 | ((index + step) & 3)


def dot(a, b):
    return jnp.dot(a, b, preferred_element_type=F32)


def my_core():
    return lax.axis_index("ctx") & 1


def rows_at(i, n):
    return pl.ds(pl.multiple_of(i * n, n), n)


def product_t(order, values):
    return lax.dot_general(order, values, (((1,), (1,)), ((), ())), preferred_element_type=F32)


def copy_all(copies):
    copies = list(copies)
    for copy in copies:
        copy.start()
    for copy in copies:
        copy.wait()


def iota(axis, n):
    return lax.broadcasted_iota(jnp.int32, (n, n), axis)


def order_in(ways, width):
    row, group = iota(0, width), width // ways
    r = group // 2
    channel = (row // r % 2) * (width // 2) + (row // group) * r + row % r
    return (channel == iota(1, width)).astype(F32).astype(BF)


def order_z(ways, width):
    row = lax.broadcasted_iota(jnp.int32, (width, 2 * width), 0)
    column = lax.broadcasted_iota(jnp.int32, (width, 2 * width), 1)
    r = width // ways // 2
    core = (row // (width // 2)) ^ my_core()
    slot = (row % (width // 2) // r) * 4 * r + core * r + row % r
    return (slot == column).astype(F32).astype(BF)


def dy_kernel(step, moves, between, w_hbm, d_hbm, *refs):
    outs, (w_ref, d_ref, p_ref, w_sem, d_sem, o_sem) = refs[:-6], refs[-6:]
    me = lax.axis_index("fsdp")
    n = outs[0].shape[0] // 2
    gather = [
        pltpu.make_async_copy(w_hbm.at[rows_at(place(me, move), n), :], w_ref.at[pl.ds(i * n, n), :], w_sem.at[i])
        for i, move in enumerate(moves)
    ]
    pieces = [pl.ds(i * step, step) for i in range(d_ref.shape[0] // step)]
    loads = [
        pltpu.make_async_copy(d_hbm.at[rows, :], d_ref.at[rows, :], d_sem.at[i]) for i, rows in enumerate(pieces)
    ]
    other_loads, other_work, other_stores = between or ((), None, ())
    for copy in (*gather, loads[0], *other_loads):
        copy.start()
    for copy in gather:
        copy.wait()
    stores = []
    for i, rows in enumerate(pieces):
        loads[i].wait()
        if i + 1 < len(pieces):
            loads[i + 1].start()
        p_ref[:, rows] = product_t(w_ref[...], d_ref[rows, :]).astype(BF)
        for j, out in enumerate(outs):
            store = pltpu.make_async_copy(
                p_ref.at[pl.ds(2 * n * j, 2 * n), rows], out.at[:, rows], o_sem.at[i * len(outs) + j]
            )
            store.start()
            stores.append(store)
        if i == 0 and other_work:
            for copy in other_loads:
                copy.wait()
            other_work()
            for copy in other_stores:
                copy.start()
                stores.append(copy)
    for store in stores:
        store.wait()


def open_kernel(step, moves, w_hbm, d_hbm, k_hbm, v_hbm, f_hbm, *refs):
    count = len(moves) // 2
    outs, send_hbm, (k_ref, v_ref, f_ref, send_ref, sem), refs = refs[:count], refs[count], refs[-5:], refs[count + 1 : -5]
    froms = zip((k_hbm, v_hbm, f_hbm), (k_ref, v_ref, f_ref))
    loads = [pltpu.make_async_copy(x, to, sem.at[i]) for i, (x, to) in enumerate(froms)]

    def mix():
        width = k_ref.shape[1]
        ways = send_ref.shape[0] // (2 * 8)
        order = order_in(ways, width)
        mixed = (k_ref[...].astype(F32) * v_ref[...].astype(F32)).astype(BF)
        parts = [product_t(order, x).reshape(ways, 1, -1, ROW) for x in (mixed, f_ref[...])]
        send_ref[...] = jnp.concatenate(parts, axis=1).reshape(send_ref.shape).astype(BF)

    between = (loads, mix, [pltpu.make_async_copy(send_ref, send_hbm, sem.at[3])])
    dy_kernel(step, moves, between, w_hbm, d_hbm, *outs, *refs)


def turn_query_kernel(q_ref, mine_ref, away_ref, qt_ref):
    qt_ref[...] = q_ref[...].astype(F32).T
    core, n = my_core(), mine_ref.shape[0]
    mine_ref[...] = qt_ref[rows_at(core, n), :].astype(BF)
    away_ref[...] = qt_ref[rows_at(1 - core, n), :].astype(BF)


def gate_kernel(ways, z_ref, q_mine_ref, q_theirs_ref, gated_ref, z_away_ref):
    z = dot(order_z(ways, gated_ref.shape[0]), z_ref[...])
    n = z.shape[0] // 2
    z_away_ref[...] = z[n:].astype(BF)
    gated_ref[pl.ds(0, n), :] = (z[:n] * q_mine_ref[...].astype(F32)).astype(BF)
    gated_ref[pl.ds(n, n), :] = (z[n:] * q_theirs_ref[...].astype(F32)).astype(BF)


def sum_kernel(own_ref, up_ref, x_ref, down_ref, keep_ref, far_ref, side_ref):
    n = keep_ref.shape[0]
    near, second = pl.ds(0, n), pl.ds(n, n)
    own = own_ref[near, :].astype(F32) + x_ref[near, :].astype(F32)
    keep_ref[...] = own + (up_ref[near, :].astype(F32) + down_ref[near, :].astype(F32))
    far_ref[...] = (own_ref[second, :].astype(F32) + x_ref[second, :].astype(F32)).astype(BF)
    side_ref[...] = (up_ref[second, :].astype(F32) + down_ref[second, :].astype(F32)).astype(BF)


def dz_kernel(ways, keep_ref, far_ref, side_ref, q_ref, z_ref, send_ref):
    dy = keep_ref[...] + (far_ref[...].astype(F32) + side_ref[...].astype(F32))
    dz = (dy * q_ref[...].astype(F32).T).astype(BF)
    pieces = (z_ref[...].astype(F32), dot(order_in(ways, dz.shape[0]), dz))
    both = jnp.concatenate([x.reshape(ways, 1, -1, ROW) for x in pieces], axis=1)
    send_ref[...] = both.reshape(send_ref.shape).astype(BF)


def query_kernel(ways, keep_ref, far_ref, side_ref, z_ref, z_theirs_ref, gq_ref, gq_t_ref):
    gq_t_ref[...] = keep_ref[...] + (far_ref[...].astype(F32) + side_ref[...].astype(F32))
    core, n = my_core(), z_theirs_ref.shape[0]
    z_mine = dot(order_z(ways, gq_t_ref.shape[0])[:n], z_ref[...]).astype(BF)
    for z, half in ((z_mine, core), (z_theirs_ref[...], 1 - core)):
        own = rows_at(half, n)
        gq_t_ref[own, :] *= z.astype(F32)
    gq_ref[...] = gq_t_ref[...].T.astype(BF)


class Tables:
    def __init__(self, first, square, twiddle):
        half = first.shape[1] // 2
        self.first, self.square = [first.at[:, pl.ds(i * half, half)] for i in range(2)], square
        self.group = first.shape[0] // twiddle.shape[0]
        rows = [jnp.broadcast_to(twiddle[i : i + 1, :], (self.group, FAC)) for i in range(twiddle.shape[0])]
        self.twiddle = jnp.concatenate(rows, axis=0)


def times_square(left, right, tables):
    square = tables.square
    return dot(left, square[:FAC]) + dot(right, square[FAC:])


def transform(x, tables):
    x = jnp.concatenate([x[:, u * FAC : (u + 1) * FAC] for u in range(LANE_TILES)], axis=0)
    width = tables.first[0].shape[1]
    section = sum(dot(part[...], x[i * width : (i + 1) * width]) for i, part in enumerate(tables.first))
    n = section.shape[0] // 2
    twiddle = tables.twiddle
    re, im, tc, ts = section[:n], section[n:], twiddle[:n], twiddle[n:]
    b_re, b_im = re * tc + im * ts, im * tc - re * ts
    left = jnp.concatenate([b_re, b_im], axis=0).astype(BF)
    right = jnp.concatenate([b_im, -b_re], axis=0).astype(BF)
    f = times_square(left, right, tables)
    return f[:n], f[n:]


def signal(p_re, p_im, tables):
    n, group = p_re.shape[0], tables.group
    left = jnp.concatenate([p_re, p_im], axis=0).astype(BF)
    right = jnp.concatenate([-p_im, p_re], axis=0).astype(BF)
    c = times_square(left, right, tables)
    re, im, tc, ts = c[:n], c[n:], tables.twiddle[:n], tables.twiddle[n:]
    row = lax.broadcasted_iota(jnp.int32, re.shape, 0)
    weight = jnp.where((row < group) | (row >= n - group), 1.0 / (QF * FAC), 2.0 / (QF * FAC))
    e = jnp.concatenate([(re * tc - im * ts) * weight, (im * tc + re * ts) * weight], axis=0).astype(BF)
    turned = lambda part: lax.dot_general(part[...], e, (((0,), (0,)), ((), ())), preferred_element_type=F32)
    x = jnp.concatenate([turned(part) for part in tables.first], axis=0)
    rows = x.shape[0] // LANE_TILES
    return jnp.concatenate([x[u * rows : (u + 1) * rows] for u in range(LANE_TILES)], axis=1)


def conv_kernel(r_ref, first_ref, square_ref, twiddle_ref, z_ref, h_ref):
    tables = Tables(first_ref, square_ref, twiddle_ref)
    rows = z_ref.shape[0]
    group = h_ref.shape[0] // (2 * HALF)
    r = r_ref[...].astype(F32).reshape(-1, 2, group, ROW)
    u, h = (transform(r[:, s].reshape(rows, ROW).astype(BF), tables) for s in range(2))
    h_ref[...] = jnp.concatenate(h, axis=0).astype(BF)
    p_re, p_im = u[0] * h[0] - u[1] * h[1], u[0] * h[1] + u[1] * h[0]
    z = signal(p_re, p_im, tables).astype(BF)
    row, r = iota(0, rows), group // 2
    source = row // (4 * r) * 4 * r + row // r % 2 * 2 * r + row // (2 * r) % 2 * r + row % r
    z_ref[...] = dot((source == iota(1, rows)).astype(F32).astype(BF), z).astype(BF)


def adjoint_kernel(r_ref, h_ref, first_ref, square_ref, twiddle_ref, away_ref, keep_ref):
    tables = Tables(first_ref, square_ref, twiddle_ref)
    rows = 2 * keep_ref.shape[0]
    group = h_ref.shape[0] // (2 * HALF)
    r = r_ref[...].astype(F32).reshape(-1, 2, group, ROW)[:, 1]
    g_re, g_im = transform(r.reshape(rows, ROW).astype(BF), tables)
    h = h_ref[...].astype(F32)
    n = h.shape[0] // 2
    h_re, h_im = h[:n], h[n:]
    q_re, q_im = h_re * g_re + h_im * g_im, h_re * g_im - h_im * g_re
    du = signal(q_re, q_im, tables).reshape(-1, 2, group, ROW)
    low, high, first_core = du[:, 0], du[:, 1], my_core() == 0
    keep_ref[...] = jnp.where(first_core, low, high).reshape(keep_ref.shape).astype(BF)
    away_ref[...] = jnp.where(first_core, high, low).reshape(keep_ref.shape).astype(BF)


def slot_of(to):
    ctx = lax.axis_index("ctx")
    flip, step = (to ^ (ctx // 2)) & 1, (to // 2 - ctx // 4) & 3
    slot = jnp.int32(0)
    for (f, d), at in SLOT.items():
        slot = jnp.where((flip == f) & (step == d), at, slot)
    return slot


def weight_rows(scale, moves, blocks, d_ref, d_other_ref, away_ref, part_ref, loaded=()):
    me = lax.axis_index("fsdp")
    n = blocks[0].shape[0] // 2
    slot_rows = part_ref.shape[0] // 8
    mine = jnp.concatenate([block[:n] for block in blocks], axis=0)
    away = jnp.concatenate([block[n:] for block in blocks], axis=0)
    away_ref[...] = away
    p = dot(mine, d_ref[...]) + dot(away, d_other_ref[...])
    p = (p * scale).astype(BF)
    for load in loaded:
        load.wait()
    for i, move in enumerate(moves):
        start = pl.multiple_of(slot_of(place(me, move)) * slot_rows, 16)
        part_ref[pl.ds(start, n), :] = p[i * n : (i + 1) * n]


def near_kernel(scale, moves, *refs):
    count = len(moves)
    blocks, (d_ref, d_other_ref, part_ref, away_ref) = refs[:count], refs[count:]
    weight_rows(scale, moves, blocks, d_ref, d_other_ref, away_ref, part_ref)


def far_kernel(scale, moves, *refs):
    count = len(moves)
    blocks, (d_ref, d_other_ref, keep_ref, got_ref, near_hbm), refs = refs[:count], refs[count : count + 5], refs[count + 5 :]
    outs, away_ref, (part_ref, sem) = refs[:4], refs[4], refs[5:]
    near = pltpu.make_async_copy(near_hbm, part_ref, sem.at[4])
    near.start()
    weight_rows(scale, moves, blocks, d_ref, d_other_ref, away_ref, part_ref, [near])
    slot_rows = part_ref.shape[0] // 8
    group = keep_ref.shape[0] // 8
    keep, got = keep_ref[...].astype(F32), got_ref[...].astype(F32)
    for j in range(8):
        rows = slice(j * group, (j + 1) * group)
        start = pl.multiple_of((slot_of(jnp.int32(j)) + 1) * slot_rows - 2 * group, 16)
        part_ref[pl.ds(start, 2 * group), :] = jnp.concatenate([keep[rows], got[rows]], axis=0).astype(BF)
    n = outs[0].shape[0]
    copy_all(pltpu.make_async_copy(part_ref.at[pl.ds(i * n, n), :], out, sem.at[i]) for i, out in enumerate(outs))


def part_sum_kernel(own_ref, x_ref, up_ref, down_ref, keep_ref, far_ref, side_ref, du_ref):
    n = keep_ref.shape[0]
    own, x, up, down = (ref[...].astype(F32) for ref in (own_ref, x_ref, up_ref, down_ref))
    m = own.shape[0] // 2
    keep_ref[...] = own[:n] + x[:n] + (up[:n] + down[:n])
    for out_ref, a, b in ((far_ref, own, x), (side_ref, up, down)):
        out_ref[...] = jnp.concatenate([a[m : m + n] + b[m : m + n], a[m + n :], b[m + n :]], axis=0).astype(BF)
    du_ref[...] = jnp.concatenate([v[n:m] for v in (own, x, up, down)], axis=0).astype(BF)


def assemble_kernel(*refs):
    blocks, theirs, (all_hbm, sem) = refs[:8], refs[8:10], refs[10:]
    me, core = lax.axis_index("fsdp"), my_core()
    n = blocks[0].shape[0] // 2
    copies = []
    for i, (block, move) in enumerate(zip(blocks, RING_FROM)):
        start = 2 * place(me, move)
        other = theirs[i // 4].at[pl.ds(i % 4 * n, n), :]
        for j, (x, half) in enumerate(((block.at[pl.ds(0, n), :], core), (other, 1 - core))):
            copies.append(pltpu.make_async_copy(x, all_hbm.at[rows_at(start + half, n), :], sem.at[2 * i + j]))
    copy_all(copies)


def final_kernel(keep_ref, far_ref, side_ref, du_ref, k_ref, v_ref, gw_ref, gk_ref, gv_ref, du_t_ref):
    n = gw_ref.shape[0]
    far, side, du = far_ref[...].astype(F32), side_ref[...].astype(F32), du_ref[...].astype(F32)
    gw_ref[...] = keep_ref[...] + (far[:n] + side[:n])
    ctx, core = lax.axis_index("ctx"), my_core()
    width = du_t_ref.shape[0]
    group = width // 16
    pieces = [du[i * 2 * group : (i + 1) * 2 * group] for i in range(4)]
    pieces += [v[n + i * 2 * group : n + (i + 1) * 2 * group] for v in (far, side) for i in range(2)]
    for piece, (flip, step) in zip(pieces, DU_FROM):
        chip = ((ctx // 4 + step) & 3) * 2 + ((ctx // 2) & 1 ^ flip)
        for rows, side_core in ((piece[:group], core), (piece[group:], 1 - core)):
            du_t_ref[rows_at(2 * chip + side_core, group), :] = rows
    du = dot(du_t_ref[...].T.astype(BF), order_in(16, width))
    gk_ref[...] = (du * v_ref[...].astype(F32)).astype(BF)
    gv_ref[...] = (du * k_ref[...].astype(F32)).astype(BF)


def staged(kernel, n_in, n_out, n_after, staged_in, staged_out):
    def run(*refs):
        ins, refs = list(refs[:n_in]), refs[n_in + n_after :]
        outs, refs = list(refs[:n_out]), refs[n_out:]
        extra = len(staged_in) + len(staged_out) + 2
        own, extra = refs[: len(refs) - extra], refs[len(refs) - extra :]
        buffers, (in_sem, out_sem) = extra[:-2], extra[-2:]
        loads, stores = [], []
        for j, i in enumerate(staged_in):
            loads.append(pltpu.make_async_copy(ins[i], buffers[j], in_sem.at[j]))
            ins[i] = buffers[j]
        for j, i in enumerate(staged_out):
            buffer = buffers[len(staged_in) + j]
            stores.append(pltpu.make_async_copy(buffer, outs[i], out_sem.at[j]))
            outs[i] = buffer
        copy_all(loads)
        kernel(*ins, *outs, *own)
        copy_all(stores)

    return run


def call(kernel, outs, ins, scratch=(), mib=16, flops=0, specs=None, after=(), staged_in=(), staged_out=(), aliases=None):
    total = sum(math.prod(o.shape) * o.dtype.itemsize for o in (*outs, *ins))
    if after or staged_in or staged_out:
        kernel = staged(kernel, len(ins), len(outs), len(after), staged_in, staged_out)
        buffers = [pltpu.VMEM(ins[i].shape, ins[i].dtype) for i in staged_in]
        buffers += [pltpu.VMEM(outs[i].shape, outs[i].dtype) for i in staged_out]
        sems = [pltpu.SemaphoreType.DMA((max(len(x), 1),)) for x in (staged_in, staged_out)]
        scratch = [*scratch, *buffers, *sems]
    in_specs, out_specs = specs or ([VMEM] * len(ins), [VMEM] * len(outs))
    in_specs = [ANY if i in staged_in else s for i, s in enumerate(in_specs)]
    out_specs = [ANY if i in staged_out else s for i, s in enumerate(out_specs)]
    return pl.pallas_call(
        kernel,
        out_shape=outs,
        in_specs=[*in_specs, *([ANY] * len(after))],
        out_specs=out_specs,
        scratch_shapes=scratch,
        input_output_aliases=aliases or {},
        compiler_params=params(mib),
        cost_estimate=pl.CostEstimate(flops=0, bytes_accessed=0, transcendentals=0),
    )(*ins, *after)


def shape(*dims, dtype=BF):
    return jax.ShapeDtypeStruct(dims, dtype)


def spread(values):
    return lax.all_to_all(values, "ctx", 0, 0, tiled=True)


def move_over(values, move):
    return lax.ppermute(values, "fsdp", [(i, place(i, move)) for i in range(8)])


RING_FROM = ((0, 0), (1, 0), (0, -1), (0, 1), (1, -1), (1, 1), (0, 2), (1, 2))


def dy_product(w_out, d_out, moves, signals=(), mib=MOST, after=()):
    channels, depth = w_out.shape
    rows = d_out.shape[0]
    step = 512
    pieces = rows // step
    count = len(moves)
    n = channels // 8
    outs = [shape(2 * n, rows)] * (count // 2)
    scratch = [
        pltpu.VMEM((count * n, depth), BF),
        pltpu.VMEM((rows, depth), BF),
        pltpu.VMEM((count * n, rows), BF),
        pltpu.SemaphoreType.DMA((count,)),
        pltpu.SemaphoreType.DMA((pieces,)),
        pltpu.SemaphoreType.DMA((count // 2 * pieces,)),
    ]
    kernel = functools.partial(dy_kernel, step, moves, None)
    if signals:
        kernel = functools.partial(open_kernel, step, moves)
        outs.append(shape(2 * signals[0].shape[1], rows))
        scratch += [pltpu.VMEM(x.shape, x.dtype) for x in (*signals, outs[-1])] + [pltpu.SemaphoreType.DMA((4,))]
    return call(
        kernel,
        outs,
        [w_out, d_out, *signals],
        scratch,
        mib=mib,
        flops=2 * count * n * depth * rows,
        specs=([ANY] * (2 + len(signals)), [ANY] * len(outs)),
        after=after,
    )


def weight_product(blocks, moves, d_out, d_other, scale, slot_rows, after=(), du=(), near=()):
    rows, columns = d_out.shape
    n = blocks[0].shape[0] // 2
    count = len(moves)
    all_rows = 8 * slot_rows
    outs = [shape(all_rows // 4, columns)] * 4 if near else [shape(all_rows, columns)]
    ins = [*blocks, d_out, d_other, *du]
    return call(
        functools.partial(far_kernel if near else near_kernel, scale, moves),
        [*outs, shape(count * n, rows)],
        [*ins, *near],
        [pltpu.VMEM((all_rows, columns), BF), pltpu.SemaphoreType.DMA((5,))] if near else [],
        flops=4 * count * n * rows * columns,
        specs=([VMEM] * len(ins) + [ANY] * len(near), [ANY if near else VMEM] * len(outs) + [VMEM]),
        after=after,
    )


def on_device(query_in, key_in, value_in, filt, w_out, d_out):
    seq_rows, width = query_in.shape
    channels, columns = w_out.shape
    ways = lax.axis_size("ctx")
    group, half = width // ways, width // 2
    n = HALF * group
    tables = host_tables(ways, group)

    swap = lambda v: lax.ppermute(v, "ctx", [(i, i ^ 1) for i in range(ways)])
    rows_like, half_like = shape(width, seq_rows), shape(half, seq_rows)

    x_y, up_y, down_y, send = dy_product(w_out, d_out, DY_MOVES[2:], (key_in, value_in, filt))
    (own_y,) = dy_product(w_out, d_out, DY_MOVES[:2], mib=16, after=[x_y])
    keep_y, far_y, side_y = call(
        sum_kernel,
        [shape(width, seq_rows, dtype=F32), rows_like, rows_like],
        [own_y, move_over(up_y, (0, 1)), move_over(x_y, (1, 0)), move_over(down_y, (0, -1))],
    )
    arrived = spread(send)

    flops = 2 * 2 * n * (4 * FAC) * FAC
    conv, spectrum = call(
        conv_kernel,
        [rows_like, shape(2 * n, FAC)],
        [arrived, *tables],
        mib=20,
        flops=3 * flops,
        after=[far_y],
    )
    dy = (keep_y, move_over(far_y, (0, 2)), move_over(side_y, (1, 0)))
    (send,) = call(
        functools.partial(dz_kernel, ways), [shape(2 * width, seq_rows)], [*dy, query_in, conv], staged_out=(0,)
    )
    q_mine, q_away = call(
        turn_query_kernel,
        [half_like, half_like],
        [query_in],
        [pltpu.VMEM((width, seq_rows), F32)],
        after=[send],
    )
    q_theirs = swap(q_away)
    send, d_late = lax.optimization_barrier((send, d_out))
    d_other = swap(d_late)
    arrived = spread(send)
    gated, z_away = call(
        functools.partial(gate_kernel, ways),
        [rows_like, half_like],
        [arrived, q_mine, q_theirs],
        after=[d_other],
    )
    z_theirs = swap(z_away)
    own_far, other = move_over(gated, (0, 2)), move_over(gated, (1, 0))
    own_up, own_down = move_over(gated, (0, 1)), move_over(gated, (0, -1))
    like = shape(seq_rows, width)
    du_away, du_keep = call(
        adjoint_kernel, [half_like, half_like], [arrived, spectrum, *tables], mib=20, flops=2 * flops
    )
    own_far, other, du_away = lax.optimization_barrier((own_far, other, du_away))
    du_got = swap(du_away)
    other_far = move_over(own_far, (1, 0))
    other_up, other_down = move_over(other, (0, 1)), move_over(other, (0, -1))
    blocks = gated, other, own_up, own_down, other_up, other_down, own_far, other_far

    slot_rows = half + 2 * group
    scale = 1.0 / math.sqrt(seq_rows * ways)
    weight = functools.partial(weight_product, d_out=d_out, d_other=d_other, scale=scale, slot_rows=slot_rows)
    near, away = weight(blocks[:4], RING_FROM[:4], after=[z_theirs])
    theirs_near = swap(away)
    own_w, x_w, up_w, down_w, away = weight(blocks[4:], RING_FROM[4:], du=(du_keep, du_got), near=(near,))
    (gated_all,) = call(
        assemble_kernel,
        [shape(channels, seq_rows)],
        [*blocks, theirs_near, swap(away)],
        [pltpu.SemaphoreType.DMA((16,))],
        specs=([ANY] * 10, [ANY]),
    )
    layer_out = lax.dot_general(
        gated_all, w_out, (((0,), (0,)), ((), ())), preferred_element_type=F32
    ).astype(BF)

    over_x = lambda v: lax.ppermute(v, "ctx", [(i, i ^ 2) for i in range(ways)])
    along_y = lambda v, step: lax.ppermute(v, "ctx", [(i, (i + 4 * step) % ways) for i in range(ways)])
    part_like = shape(channels // ways, columns, dtype=F32)
    onward = shape(half + 4 * group, columns)
    keep_w, far_w, side_w, du_near = call(
        part_sum_kernel,
        [part_like, onward, onward, half_like],
        [own_w, over_x(x_w), along_y(up_w, 1), along_y(down_w, -1)],
        after=[layer_out],
    )
    onward_w = far_w
    far_w, side_w = along_y(far_w, 2), over_x(side_w)
    (grad_query,) = call(
        functools.partial(query_kernel, ways),
        [like],
        [*dy, arrived, z_theirs],
        [pltpu.VMEM((width, seq_rows), F32)],
        staged_out=(0,),
        after=[onward_w],
    )

    grad_weight, grad_key, grad_value = call(
        final_kernel,
        [part_like, like, like],
        [keep_w, far_w, side_w, du_near, key_in, value_in],
        [pltpu.VMEM((width, columns), F32)],
        staged_out=(0, 1, 2),
    )
    return (layer_out, grad_query, grad_key, grad_value, grad_weight)


def solution(mesh):
    both = P("ctx", "fsdp")
    return jax.shard_map(
        on_device,
        mesh=mesh,
        in_specs=(both, both, both, both, P(None, "fsdp"), both),
        out_specs=(both, both, both, both, both),
        check_vma=False,
    )
```

```python
import functools
import math

import jax
import jax.numpy as jnp
import numpy as np
from jax import lax
from jax.experimental import pallas as pl
from jax.experimental.pallas import tpu as pltpu
from jax.sharding import PartitionSpec as P

ROW = 1024
FAC = 256
QF = 128
HALF = QF // 2 + 1
LANE_TILES = ROW // FAC
BF = jnp.bfloat16
F32 = jnp.float32
MIB = 1 << 20
MOST = 56


def angles(rows, cols, modulus):
    product = (rows[:, None].astype(np.int64) * cols[None, :]) % modulus
    return (product.astype(np.float32) * np.float32(2.0 * math.pi / modulus)).astype(np.float64)


def host_tables(ways, group):
    k2, t1 = np.arange(HALF), np.arange(FAC)
    t2 = (np.arange(LANE_TILES)[:, None] + LANE_TILES * np.arange(ways)[None, :]).reshape(-1)
    a = angles(k2, t2, QF)
    steps = np.stack([np.cos(a), -np.sin(a)])
    first = np.einsum("rkt,cd->rkctd", steps, np.eye(group)).reshape(2 * HALF * group, t2.size * group)
    s = angles(t1, t1, FAC)
    square = np.concatenate([np.cos(s), np.sin(s)])
    w = angles(k2, t1, QF * FAC)
    twiddle = np.concatenate([np.cos(w), np.sin(w)]).astype(np.float32)
    as_bf = lambda v: np.asarray(v, np.float32).astype(BF)
    return as_bf(first), as_bf(square), twiddle


def params(mib):
    return pltpu.CompilerParams(vmem_limit_bytes=mib * MIB)


VMEM = pl.BlockSpec(memory_space=pltpu.VMEM)
ANY = pl.BlockSpec(memory_space=pl.ANY)
DY_MOVES = ((0, 0), (0, 2), (1, 0), (1, 2), (0, 1), (1, 1), (0, -1), (1, -1))
DU_FROM = ((0, 0), (1, 0), (0, -1), (0, 1), (0, 2), (1, 2), (1, -1), (1, 1))
SLOT = {move: i for i, (flip, step) in enumerate(DY_MOVES) for move in ((flip, step % 4),)}


def place(index, move):
    flip, step = move
    return ((index ^ 4) if flip else index) & 4 | ((index + step) & 3)


def dot(a, b):
    return jnp.dot(a, b, preferred_element_type=F32)


def my_core():
    return lax.axis_index("ctx") & 1


def rows_at(i, n):
    return pl.ds(pl.multiple_of(i * n, n), n)


def product_t(order, values):
    return lax.dot_general(order, values, (((1,), (1,)), ((), ())), preferred_element_type=F32)


def copy_all(copies):
    copies = list(copies)
    for copy in copies:
        copy.start()
    for copy in copies:
        copy.wait()


def iota(axis, n):
    return lax.broadcasted_iota(jnp.int32, (n, n), axis)


def order_in(ways, width):
    row, group = iota(0, width), width // ways
    r = group // 2
    channel = (row // r % 2) * (width // 2) + (row // group) * r + row % r
    return (channel == iota(1, width)).astype(F32).astype(BF)


def order_z(ways, width):
    row = lax.broadcasted_iota(jnp.int32, (width, 2 * width), 0)
    column = lax.broadcasted_iota(jnp.int32, (width, 2 * width), 1)
    r = width // ways // 2
    core = (row // (width // 2)) ^ my_core()
    slot = (row % (width // 2) // r) * 4 * r + core * r + row % r
    return (slot == column).astype(F32).astype(BF)


def dy_kernel(step, moves, between, w_hbm, d_hbm, *refs):
    outs, (w_ref, d_ref, p_ref, w_sem, d_sem, o_sem) = refs[:-6], refs[-6:]
    me = lax.axis_index("fsdp")
    n = outs[0].shape[0] // 2
    gather = [
        pltpu.make_async_copy(w_hbm.at[rows_at(place(me, move), n), :], w_ref.at[pl.ds(i * n, n), :], w_sem.at[i])
        for i, move in enumerate(moves)
    ]
    pieces = [pl.ds(i * step, step) for i in range(d_ref.shape[0] // step)]
    loads = [
        pltpu.make_async_copy(d_hbm.at[rows, :], d_ref.at[rows, :], d_sem.at[i]) for i, rows in enumerate(pieces)
    ]
    other_loads, other_work, other_stores = between or ((), None, ())
    for copy in (*gather, loads[0], *other_loads):
        copy.start()
    for copy in gather:
        copy.wait()
    stores = []
    for i, rows in enumerate(pieces):
        loads[i].wait()
        if i + 1 < len(pieces):
            loads[i + 1].start()
        p_ref[:, rows] = product_t(w_ref[...], d_ref[rows, :]).astype(BF)
        for j, out in enumerate(outs):
            store = pltpu.make_async_copy(
                p_ref.at[pl.ds(2 * n * j, 2 * n), rows], out.at[:, rows], o_sem.at[i * len(outs) + j]
            )
            store.start()
            stores.append(store)
        if i == 0 and other_work:
            for copy in other_loads:
                copy.wait()
            other_work()
            for copy in other_stores:
                copy.start()
                stores.append(copy)
    for store in stores:
        store.wait()


def open_kernel(step, moves, w_hbm, d_hbm, k_hbm, v_hbm, f_hbm, *refs):
    count = len(moves) // 2
    outs, send_hbm, (k_ref, v_ref, f_ref, send_ref, sem), refs = refs[:count], refs[count], refs[-5:], refs[count + 1 : -5]
    froms = zip((k_hbm, v_hbm, f_hbm), (k_ref, v_ref, f_ref))
    loads = [pltpu.make_async_copy(x, to, sem.at[i]) for i, (x, to) in enumerate(froms)]

    def mix():
        width = k_ref.shape[1]
        ways = send_ref.shape[0] // (2 * 8)
        order = order_in(ways, width)
        mixed = (k_ref[...].astype(F32) * v_ref[...].astype(F32)).astype(BF)
        parts = [product_t(order, x).reshape(ways, 1, -1, ROW) for x in (mixed, f_ref[...])]
        send_ref[...] = jnp.concatenate(parts, axis=1).reshape(send_ref.shape).astype(BF)

    between = (loads, mix, [pltpu.make_async_copy(send_ref, send_hbm, sem.at[3])])
    dy_kernel(step, moves, between, w_hbm, d_hbm, *outs, *refs)


def turn_query_kernel(q_ref, mine_ref, away_ref, qt_ref):
    qt_ref[...] = q_ref[...].astype(F32).T
    core, n = my_core(), mine_ref.shape[0]
    mine_ref[...] = qt_ref[rows_at(core, n), :].astype(BF)
    away_ref[...] = qt_ref[rows_at(1 - core, n), :].astype(BF)


def gate_kernel(ways, z_ref, q_mine_ref, q_theirs_ref, gated_ref, z_away_ref):
    z = dot(order_z(ways, gated_ref.shape[0]), z_ref[...])
    n = z.shape[0] // 2
    z_away_ref[...] = z[n:].astype(BF)
    gated_ref[pl.ds(0, n), :] = (z[:n] * q_mine_ref[...].astype(F32)).astype(BF)
    gated_ref[pl.ds(n, n), :] = (z[n:] * q_theirs_ref[...].astype(F32)).astype(BF)


def sum_kernel(own_ref, up_ref, x_ref, down_ref, keep_ref, far_ref, side_ref):
    n = keep_ref.shape[0]
    near, second = pl.ds(0, n), pl.ds(n, n)
    own = own_ref[near, :].astype(F32) + x_ref[near, :].astype(F32)
    keep_ref[...] = own + (up_ref[near, :].astype(F32) + down_ref[near, :].astype(F32))
    far_ref[...] = (own_ref[second, :].astype(F32) + x_ref[second, :].astype(F32)).astype(BF)
    side_ref[...] = (up_ref[second, :].astype(F32) + down_ref[second, :].astype(F32)).astype(BF)


def dz_kernel(ways, keep_ref, far_ref, side_ref, q_ref, z_ref, send_ref):
    dy = keep_ref[...] + (far_ref[...].astype(F32) + side_ref[...].astype(F32))
    dz = (dy * q_ref[...].astype(F32).T).astype(BF)
    pieces = (z_ref[...].astype(F32), dot(order_in(ways, dz.shape[0]), dz))
    both = jnp.concatenate([x.reshape(ways, 1, -1, ROW) for x in pieces], axis=1)
    send_ref[...] = both.reshape(send_ref.shape).astype(BF)


def query_kernel(ways, keep_ref, far_ref, side_ref, z_ref, z_theirs_ref, gq_ref, gq_t_ref):
    gq_t_ref[...] = keep_ref[...] + (far_ref[...].astype(F32) + side_ref[...].astype(F32))
    core, n = my_core(), z_theirs_ref.shape[0]
    z_mine = dot(order_z(ways, gq_t_ref.shape[0])[:n], z_ref[...]).astype(BF)
    for z, half in ((z_mine, core), (z_theirs_ref[...], 1 - core)):
        own = rows_at(half, n)
        gq_t_ref[own, :] *= z.astype(F32)
    gq_ref[...] = gq_t_ref[...].T.astype(BF)


class Tables:
    def __init__(self, first, square, twiddle):
        half = first.shape[1] // 2
        self.first, self.square = [first.at[:, pl.ds(i * half, half)] for i in range(2)], square
        self.group = first.shape[0] // twiddle.shape[0]
        rows = [jnp.broadcast_to(twiddle[i : i + 1, :], (self.group, FAC)) for i in range(twiddle.shape[0])]
        self.twiddle = jnp.concatenate(rows, axis=0)


def times_square(left, right, tables):
    square = tables.square
    return dot(left, square[:FAC]) + dot(right, square[FAC:])


def transform(x, tables):
    x = jnp.concatenate([x[:, u * FAC : (u + 1) * FAC] for u in range(LANE_TILES)], axis=0)
    width = tables.first[0].shape[1]
    section = sum(dot(part[...], x[i * width : (i + 1) * width]) for i, part in enumerate(tables.first))
    n = section.shape[0] // 2
    twiddle = tables.twiddle
    re, im, tc, ts = section[:n], section[n:], twiddle[:n], twiddle[n:]
    b_re, b_im = re * tc + im * ts, im * tc - re * ts
    left = jnp.concatenate([b_re, b_im], axis=0).astype(BF)
    right = jnp.concatenate([b_im, -b_re], axis=0).astype(BF)
    f = times_square(left, right, tables)
    return f[:n], f[n:]


def signal(p_re, p_im, tables):
    n, group = p_re.shape[0], tables.group
    left = jnp.concatenate([p_re, p_im], axis=0).astype(BF)
    right = jnp.concatenate([-p_im, p_re], axis=0).astype(BF)
    c = times_square(left, right, tables)
    re, im, tc, ts = c[:n], c[n:], tables.twiddle[:n], tables.twiddle[n:]
    row = lax.broadcasted_iota(jnp.int32, re.shape, 0)
    weight = jnp.where((row < group) | (row >= n - group), 1.0 / (QF * FAC), 2.0 / (QF * FAC))
    e = jnp.concatenate([(re * tc - im * ts) * weight, (im * tc + re * ts) * weight], axis=0).astype(BF)
    turned = lambda part: lax.dot_general(part[...], e, (((0,), (0,)), ((), ())), preferred_element_type=F32)
    x = jnp.concatenate([turned(part) for part in tables.first], axis=0)
    rows = x.shape[0] // LANE_TILES
    return jnp.concatenate([x[u * rows : (u + 1) * rows] for u in range(LANE_TILES)], axis=1)


def conv_kernel(r_ref, first_ref, square_ref, twiddle_ref, _, z_ref, h_hbm, h_ref, sem):
    tables = Tables(first_ref, square_ref, twiddle_ref)
    rows = z_ref.shape[0]
    group = h_ref.shape[0] // (2 * HALF)
    r = r_ref[...].astype(F32).reshape(-1, 2, group, ROW)
    u, h = (transform(r[:, s].reshape(rows, ROW).astype(BF), tables) for s in range(2))
    h_ref[...] = jnp.concatenate(h, axis=0).astype(BF)
    store = pltpu.make_async_copy(h_ref, h_hbm, sem.at[0])
    store.start()
    p_re, p_im = u[0] * h[0] - u[1] * h[1], u[0] * h[1] + u[1] * h[0]
    z = signal(p_re, p_im, tables).astype(BF)
    row, r = iota(0, rows), group // 2
    source = row // (4 * r) * 4 * r + row // r % 2 * 2 * r + row // (2 * r) % 2 * r + row % r
    z_ref[...] = dot((source == iota(1, rows)).astype(F32).astype(BF), z).astype(BF)
    store.wait()


def adjoint_kernel(r_ref, h_ref, first_ref, square_ref, twiddle_ref, away_ref, keep_ref):
    tables = Tables(first_ref, square_ref, twiddle_ref)
    rows = 2 * keep_ref.shape[0]
    group = h_ref.shape[0] // (2 * HALF)
    r = r_ref[...].astype(F32).reshape(-1, 2, group, ROW)[:, 1]
    g_re, g_im = transform(r.reshape(rows, ROW).astype(BF), tables)
    h = h_ref[...].astype(F32)
    n = h.shape[0] // 2
    h_re, h_im = h[:n], h[n:]
    q_re, q_im = h_re * g_re + h_im * g_im, h_re * g_im - h_im * g_re
    du = signal(q_re, q_im, tables).reshape(-1, 2, group, ROW)
    low, high, first_core = du[:, 0], du[:, 1], my_core() == 0
    keep_ref[...] = jnp.where(first_core, low, high).reshape(keep_ref.shape).astype(BF)
    away_ref[...] = jnp.where(first_core, high, low).reshape(keep_ref.shape).astype(BF)


def slot_of(to):
    ctx = lax.axis_index("ctx")
    flip, step = (to ^ (ctx // 2)) & 1, (to // 2 - ctx // 4) & 3
    slot = jnp.int32(0)
    for (f, d), at in SLOT.items():
        slot = jnp.where((flip == f) & (step == d), at, slot)
    return slot


def weight_rows(scale, moves, blocks, d_ref, d_other_ref, away_ref, part_ref, loaded=()):
    me = lax.axis_index("fsdp")
    n = blocks[0].shape[0] // 2
    slot_rows = part_ref.shape[0] // 8
    mine = jnp.concatenate([block[:n] for block in blocks], axis=0)
    away = jnp.concatenate([block[n:] for block in blocks], axis=0)
    away_ref[...] = away
    p = dot(mine, d_ref[...]) + dot(away, d_other_ref[...])
    p = (p * scale).astype(BF)
    for load in loaded:
        load.wait()
    for i, move in enumerate(moves):
        start = pl.multiple_of(slot_of(place(me, move)) * slot_rows, 16)
        part_ref[pl.ds(start, n), :] = p[i * n : (i + 1) * n]


def near_kernel(scale, moves, *refs):
    count = len(moves)
    blocks, (d_ref, d_other_ref, part_ref, away_ref) = refs[:count], refs[count:]
    weight_rows(scale, moves, blocks, d_ref, d_other_ref, away_ref, part_ref)


def far_kernel(scale, moves, *refs):
    count = len(moves)
    blocks, (d_ref, d_other_ref, keep_ref, got_ref, near_hbm), refs = refs[:count], refs[count : count + 5], refs[count + 5 :]
    outs, away_ref, (part_ref, sem) = refs[:4], refs[4], refs[5:]
    near = pltpu.make_async_copy(near_hbm, part_ref, sem.at[4])
    near.start()
    weight_rows(scale, moves, blocks, d_ref, d_other_ref, away_ref, part_ref, [near])
    slot_rows = part_ref.shape[0] // 8
    group = keep_ref.shape[0] // 8
    keep, got = keep_ref[...].astype(F32), got_ref[...].astype(F32)
    for j in range(8):
        rows = slice(j * group, (j + 1) * group)
        start = pl.multiple_of((slot_of(jnp.int32(j)) + 1) * slot_rows - 2 * group, 16)
        part_ref[pl.ds(start, 2 * group), :] = jnp.concatenate([keep[rows], got[rows]], axis=0).astype(BF)
    n = outs[0].shape[0]
    copy_all(pltpu.make_async_copy(part_ref.at[pl.ds(i * n, n), :], out, sem.at[i]) for i, out in enumerate(outs))


def part_sum_kernel(own_ref, x_ref, up_ref, down_ref, keep_ref, far_ref, side_ref, du_ref):
    n = keep_ref.shape[0]
    own, x, up, down = (ref[...].astype(F32) for ref in (own_ref, x_ref, up_ref, down_ref))
    m = own.shape[0] // 2
    keep_ref[...] = own[:n] + x[:n] + (up[:n] + down[:n])
    for out_ref, a, b in ((far_ref, own, x), (side_ref, up, down)):
        out_ref[...] = jnp.concatenate([a[m : m + n] + b[m : m + n], a[m + n :], b[m + n :]], axis=0).astype(BF)
    du_ref[...] = jnp.concatenate([v[n:m] for v in (own, x, up, down)], axis=0).astype(BF)


def assemble_kernel(*refs):
    blocks, theirs, (all_hbm, sem) = refs[:8], refs[8:10], refs[10:]
    me, core = lax.axis_index("fsdp"), my_core()
    n = blocks[0].shape[0] // 2
    copies = []
    for i, (block, move) in enumerate(zip(blocks, RING_FROM)):
        start = 2 * place(me, move)
        other = theirs[i // 4].at[pl.ds(i % 4 * n, n), :]
        for j, (x, half) in enumerate(((block.at[pl.ds(0, n), :], core), (other, 1 - core))):
            copies.append(pltpu.make_async_copy(x, all_hbm.at[rows_at(start + half, n), :], sem.at[2 * i + j]))
    copy_all(copies)


def final_kernel(keep_ref, far_ref, side_ref, du_ref, k_ref, v_ref, gw_ref, gk_ref, gv_ref, du_t_ref):
    n = gw_ref.shape[0]
    far, side, du = far_ref[...].astype(F32), side_ref[...].astype(F32), du_ref[...].astype(F32)
    gw_ref[...] = keep_ref[...] + (far[:n] + side[:n])
    ctx, core = lax.axis_index("ctx"), my_core()
    width = du_t_ref.shape[0]
    group = width // 16
    pieces = [du[i * 2 * group : (i + 1) * 2 * group] for i in range(4)]
    pieces += [v[n + i * 2 * group : n + (i + 1) * 2 * group] for v in (far, side) for i in range(2)]
    for piece, (flip, step) in zip(pieces, DU_FROM):
        chip = ((ctx // 4 + step) & 3) * 2 + ((ctx // 2) & 1 ^ flip)
        for rows, side_core in ((piece[:group], core), (piece[group:], 1 - core)):
            du_t_ref[rows_at(2 * chip + side_core, group), :] = rows
    du = dot(du_t_ref[...].T.astype(BF), order_in(16, width))
    gk_ref[...] = (du * v_ref[...].astype(F32)).astype(BF)
    gv_ref[...] = (du * k_ref[...].astype(F32)).astype(BF)


def staged(kernel, n_in, n_out, n_after, staged_in, staged_out):
    def run(*refs):
        ins, refs = list(refs[:n_in]), refs[n_in + n_after :]
        outs, refs = list(refs[:n_out]), refs[n_out:]
        extra = len(staged_in) + len(staged_out) + 2
        own, extra = refs[: len(refs) - extra], refs[len(refs) - extra :]
        buffers, (in_sem, out_sem) = extra[:-2], extra[-2:]
        loads, stores = [], []
        for j, i in enumerate(staged_in):
            loads.append(pltpu.make_async_copy(ins[i], buffers[j], in_sem.at[j]))
            ins[i] = buffers[j]
        for j, i in enumerate(staged_out):
            buffer = buffers[len(staged_in) + j]
            stores.append(pltpu.make_async_copy(buffer, outs[i], out_sem.at[j]))
            outs[i] = buffer
        copy_all(loads)
        kernel(*ins, *outs, *own)
        copy_all(stores)

    return run


def call(kernel, outs, ins, scratch=(), mib=16, flops=0, specs=None, after=(), staged_in=(), staged_out=(), aliases=None):
    total = sum(math.prod(o.shape) * o.dtype.itemsize for o in (*outs, *ins))
    if after or staged_in or staged_out:
        kernel = staged(kernel, len(ins), len(outs), len(after), staged_in, staged_out)
        buffers = [pltpu.VMEM(ins[i].shape, ins[i].dtype) for i in staged_in]
        buffers += [pltpu.VMEM(outs[i].shape, outs[i].dtype) for i in staged_out]
        sems = [pltpu.SemaphoreType.DMA((max(len(x), 1),)) for x in (staged_in, staged_out)]
        scratch = [*scratch, *buffers, *sems]
    in_specs, out_specs = specs or ([VMEM] * len(ins), [VMEM] * len(outs))
    in_specs = [ANY if i in staged_in else s for i, s in enumerate(in_specs)]
    out_specs = [ANY if i in staged_out else s for i, s in enumerate(out_specs)]
    return pl.pallas_call(
        kernel,
        out_shape=outs,
        in_specs=[*in_specs, *([ANY] * len(after))],
        out_specs=out_specs,
        scratch_shapes=scratch,
        input_output_aliases=aliases or {},
        compiler_params=params(mib),
        cost_estimate=pl.CostEstimate(flops=0, bytes_accessed=0, transcendentals=0),
    )(*ins, *after)


def shape(*dims, dtype=BF):
    return jax.ShapeDtypeStruct(dims, dtype)


def spread(values):
    return lax.all_to_all(values, "ctx", 0, 0, tiled=True)


def move_over(values, move):
    return lax.ppermute(values, "fsdp", [(i, place(i, move)) for i in range(8)])


RING_FROM = ((0, 0), (1, 0), (0, -1), (0, 1), (1, -1), (1, 1), (0, 2), (1, 2))


def dy_product(w_out, d_out, moves, signals=(), mib=MOST, after=()):
    channels, depth = w_out.shape
    rows = d_out.shape[0]
    step = 512
    pieces = rows // step
    count = len(moves)
    n = channels // 8
    outs = [shape(2 * n, rows)] * (count // 2)
    scratch = [
        pltpu.VMEM((count * n, depth), BF),
        pltpu.VMEM((rows, depth), BF),
        pltpu.VMEM((count * n, rows), BF),
        pltpu.SemaphoreType.DMA((count,)),
        pltpu.SemaphoreType.DMA((pieces,)),
        pltpu.SemaphoreType.DMA((count // 2 * pieces,)),
    ]
    kernel = functools.partial(dy_kernel, step, moves, None)
    if signals:
        kernel = functools.partial(open_kernel, step, moves)
        outs.append(shape(2 * signals[0].shape[1], rows))
        scratch += [pltpu.VMEM(x.shape, x.dtype) for x in (*signals, outs[-1])] + [pltpu.SemaphoreType.DMA((4,))]
    return call(
        kernel,
        outs,
        [w_out, d_out, *signals],
        scratch,
        mib=mib,
        flops=2 * count * n * depth * rows,
        specs=([ANY] * (2 + len(signals)), [ANY] * len(outs)),
        after=after,
    )


def weight_product(blocks, moves, d_out, d_other, scale, slot_rows, after=(), du=(), near=()):
    rows, columns = d_out.shape
    n = blocks[0].shape[0] // 2
    count = len(moves)
    all_rows = 8 * slot_rows
    outs = [shape(all_rows // 4, columns)] * 4 if near else [shape(all_rows, columns)]
    ins = [*blocks, d_out, d_other, *du]
    return call(
        functools.partial(far_kernel if near else near_kernel, scale, moves),
        [*outs, shape(count * n, rows)],
        [*ins, *near],
        [pltpu.VMEM((all_rows, columns), BF), pltpu.SemaphoreType.DMA((5,))] if near else [],
        flops=4 * count * n * rows * columns,
        specs=([VMEM] * len(ins) + [ANY] * len(near), [ANY if near else VMEM] * len(outs) + [VMEM]),
        after=after,
    )


def on_device(query_in, key_in, value_in, filt, w_out, d_out):
    seq_rows, width = query_in.shape
    channels, columns = w_out.shape
    ways = lax.axis_size("ctx")
    group, half = width // ways, width // 2
    n = HALF * group
    tables = host_tables(ways, group)

    swap = lambda v: lax.ppermute(v, "ctx", [(i, i ^ 1) for i in range(ways)])
    rows_like, half_like = shape(width, seq_rows), shape(half, seq_rows)

    x_y, up_y, down_y, send = dy_product(w_out, d_out, DY_MOVES[2:], (key_in, value_in, filt))
    (own_y,) = dy_product(w_out, d_out, DY_MOVES[:2], mib=16, after=[x_y])
    keep_y, far_y, side_y = call(
        sum_kernel,
        [shape(width, seq_rows, dtype=F32), rows_like, rows_like],
        [own_y, move_over(up_y, (0, 1)), move_over(x_y, (1, 0)), move_over(down_y, (0, -1))],
    )
    arrived = spread(send)

    flops = 2 * 2 * n * (4 * FAC) * FAC
    conv, spectrum = call(
        conv_kernel,
        [rows_like, shape(2 * n, FAC)],
        [arrived, *tables, far_y],
        [pltpu.VMEM((2 * n, FAC), BF), pltpu.SemaphoreType.DMA((1,))],
        mib=20,
        flops=3 * flops,
        specs=([VMEM] * 4 + [ANY], [VMEM, ANY]),
    )
    dy = (keep_y, move_over(far_y, (0, 2)), move_over(side_y, (1, 0)))
    (send,) = call(
        functools.partial(dz_kernel, ways), [shape(2 * width, seq_rows)], [*dy, query_in, conv], staged_out=(0,)
    )
    q_mine, q_away = call(
        turn_query_kernel,
        [half_like, half_like],
        [query_in],
        [pltpu.VMEM((width, seq_rows), F32)],
        after=[send],
    )
    q_theirs = swap(q_away)
    send, d_late = lax.optimization_barrier((send, d_out))
    d_other = swap(d_late)
    arrived = spread(send)
    gated, z_away = call(
        functools.partial(gate_kernel, ways),
        [rows_like, half_like],
        [arrived, q_mine, q_theirs],
        after=[d_other],
    )
    z_theirs = swap(z_away)
    own_far, other = move_over(gated, (0, 2)), move_over(gated, (1, 0))
    own_up, own_down = move_over(gated, (0, 1)), move_over(gated, (0, -1))
    like = shape(seq_rows, width)
    du_away, du_keep = call(
        adjoint_kernel, [half_like, half_like], [arrived, spectrum, *tables], mib=20, flops=2 * flops
    )
    own_far, other, du_away = lax.optimization_barrier((own_far, other, du_away))
    du_got = swap(du_away)
    other_far = move_over(own_far, (1, 0))
    other_up, other_down = move_over(other, (0, 1)), move_over(other, (0, -1))
    blocks = gated, other, own_up, own_down, other_up, other_down, own_far, other_far

    slot_rows = half + 2 * group
    scale = 1.0 / math.sqrt(seq_rows * ways)
    weight = functools.partial(weight_product, d_out=d_out, d_other=d_other, scale=scale, slot_rows=slot_rows)
    near, away = weight(blocks[:4], RING_FROM[:4], after=[z_theirs])
    theirs_near = swap(away)
    own_w, x_w, up_w, down_w, away = weight(blocks[4:], RING_FROM[4:], du=(du_keep, du_got), near=(near,))
    (gated_all,) = call(
        assemble_kernel,
        [shape(channels, seq_rows)],
        [*blocks, theirs_near, swap(away)],
        [pltpu.SemaphoreType.DMA((16,))],
        specs=([ANY] * 10, [ANY]),
    )
    layer_out = lax.dot_general(
        gated_all, w_out, (((0,), (0,)), ((), ())), preferred_element_type=F32
    ).astype(BF)

    over_x = lambda v: lax.ppermute(v, "ctx", [(i, i ^ 2) for i in range(ways)])
    along_y = lambda v, step: lax.ppermute(v, "ctx", [(i, (i + 4 * step) % ways) for i in range(ways)])
    part_like = shape(channels // ways, columns, dtype=F32)
    onward = shape(half + 4 * group, columns)
    keep_w, far_w, side_w, du_near = call(
        part_sum_kernel,
        [part_like, onward, onward, half_like],
        [own_w, over_x(x_w), along_y(up_w, 1), along_y(down_w, -1)],
        after=[layer_out],
    )
    onward_w = far_w
    far_w, side_w = along_y(far_w, 2), over_x(side_w)
    (grad_query,) = call(
        functools.partial(query_kernel, ways),
        [like],
        [*dy, arrived, z_theirs],
        [pltpu.VMEM((width, seq_rows), F32)],
        staged_out=(0,),
        after=[onward_w],
    )

    grad_weight, grad_key, grad_value = call(
        final_kernel,
        [part_like, like, like],
        [keep_w, far_w, side_w, du_near, key_in, value_in],
        [pltpu.VMEM((width, columns), F32)],
        staged_out=(0, 1, 2),
    )
    return (layer_out, grad_query, grad_key, grad_value, grad_weight)


def solution(mesh):
    both = P("ctx", "fsdp")
    return jax.shard_map(
        on_device,
        mesh=mesh,
        in_specs=(both, both, both, both, P(None, "fsdp"), both),
        out_specs=(both, both, both, both, both),
        check_vma=False,
    )
```
